32 devices in a mesh: row: 4 (over y, core), col: 8 (over z, x).
Axes of the slice: x: 2, y: 2, z: 4, core: 2. Of those that a mesh axis runs over, the one named last changes fastest.
Arguments:
- features: bfloat16 [8192, 512], P(('row', 'col')), may hold values from -6 to 6
- memory: float32 [8192, 512], P(('col', 'row')), may hold values from -1 to 1
- tile_values: bfloat16 [4, 8, 64, 128, 128], P('row', 'col'), as said below
- tile_rows: int32 [4, 8, 64], P('row', 'col'), may hold values from 0 to 7, as said below
- tile_cols: int32 [4, 8, 64], P('row', 'col'), may hold values from 0 to 15
- tile_count: int32 [4, 8], P('row', 'col'), may hold values from 8 to 64, as said below
- conv_weight: bfloat16 [512, 512], replicated, may hold values from -0.25 to 0.25
- conv_bias: float32 [512], replicated, may hold values from -3 to 3
- input_weight: bfloat16 [512, 1536], replicated, may hold values from -0.25 to 0.25
- input_bias: float32 [1536], replicated, may hold values from -3 to 3
- hidden_weight: bfloat16 [512, 1536], replicated, may hold values from -0.25 to 0.25
- hidden_bias: float32 [1536], replicated, may hold values from -3 to 3
Outputs:
- new_memory: float32 [8192, 512], P(('col', 'row'))
The draws below stay inside these ranges and needn't reach their ends.
Inputs may be any that keep to these rules, and one draw needn't show every extreme that they name: `tile_values`: edge weights are nonnegative. For each device pair (r, c) the 64 pairs (tile_rows, tile_cols) are distinct. `tile_count`: in every draw some device pair has all 64 slots live.
All inputs are finite; a program needn't handle non-finite values.
Results may differ from the reference program's by a relative error of at most 0.017.
Values may be sent and summed in bfloat16 or wider, within the bound.
No kernel may reach another device: no remote copies, remote signals or barrier semaphores. Data moves between devices by JAX's collectives and lax.ppermute only.
A program may use at most 128 MiB of HBM per device.

```python
import math
import jax
import jax.numpy as jnp
from jax import lax

F = 512
TILE = 128
NODES = 8192
DST_GROUP = 1024
SRC_GROUP = 2048
ROW_BLOCKS = 8
COL_BLOCKS = 16
SLOTS = 64
N_ROW = 4
N_COL = 8


def tile_layout(key):
    layout_key = jax.random.fold_in(key, 7)
    device_keys = jax.random.split(layout_key, N_ROW * N_COL)

    def one_device(device_key):
        return jax.random.permutation(device_key, ROW_BLOCKS * COL_BLOCKS)[:SLOTS]
    chosen = jax.vmap(one_device)(device_keys).astype(jnp.int32).reshape(N_ROW, N_COL, SLOTS)
    return (chosen // COL_BLOCKS, chosen % COL_BLOCKS)


def draw_tile_rows(key, part):
    return tile_layout(key)[0]


def draw_tile_cols(key, part):
    return tile_layout(key)[1]


def draw_tile_count(key, part):
    device_total = N_ROW * N_COL
    shifts = jax.random.randint(jax.random.fold_in(key, 21), (device_total,), 0, 3)
    ceiling = jnp.right_shift(jnp.full((device_total,), SLOTS, jnp.int32), shifts.astype(jnp.int32))
    shortfall = jax.random.randint(jax.random.fold_in(key, 22), (device_total,), 0, ceiling // 2 + 1)
    counts = ceiling - shortfall
    busiest = jax.random.randint(jax.random.fold_in(key, 23), (), 0, device_total)
    lightest = (busiest + 1 + jax.random.randint(jax.random.fold_in(key, 24), (), 0, device_total - 1)) % device_total
    positions = jnp.arange(device_total)
    counts = jnp.where(positions == busiest, SLOTS, counts)
    counts = jnp.where(positions == lightest, SLOTS // 8, counts)
    return counts.reshape(N_ROW, N_COL).astype(jnp.int32)


def draw_tile_values(key, part):
    row_ids, col_ids = tile_layout(key)
    offsets = jnp.arange(TILE)
    group_col = jnp.arange(N_COL)[None, :, None, None]
    group_row = jnp.arange(N_ROW)[:, None, None, None]
    dst_index = group_col * DST_GROUP + row_ids[..., None] * TILE + offsets
    src_index = group_row * SRC_GROUP + col_ids[..., None] * TILE + offsets
    lowest, highest = (0.2, 5.0)
    dst_scale = jnp.exp(jax.random.uniform(jax.random.fold_in(key, 31), (NODES,), jnp.float32, math.log(lowest), math.log(highest)))
    src_scale = jnp.exp(jax.random.uniform(jax.random.fold_in(key, 32), (NODES,), jnp.float32, math.log(lowest), math.log(highest)))
    growth = 1.0 + 2.0 * jnp.arange(N_COL, dtype=jnp.float32) / (N_COL - 1)
    dst_part = dst_scale[dst_index] * growth[None, :, None, None]
    src_part = src_scale[src_index]
    full_shape = (N_ROW, N_COL, SLOTS, TILE, TILE)
    present = jax.random.bernoulli(jax.random.fold_in(key, 33), 0.3, full_shape)
    jitter = jax.random.uniform(jax.random.fold_in(key, 34), full_shape, jnp.float32, 0.5, 1.5)
    values = jnp.where(present, dst_part[..., :, None] * src_part[..., None, :] * jitter, jnp.float32(0.0))
    return values.astype(jnp.bfloat16)


def shard_levels(stream_key, extent, cuts, smallest, high):
    gain, own = 1.0, jax.random.fold_in(stream_key, 6)
    for dim, shards_of in cuts:
        draws = jnp.exp(jax.random.uniform(jax.random.fold_in(own, dim), (shards_of,), jnp.float32, smallest / len(cuts), high / len(cuts)))
        gain = gain * jnp.repeat(draws, extent[dim] // shards_of).reshape([-1 if axis == dim else 1 for axis in range(len(extent))])
    return gain


def centred(own_key, dims, scale, bound, cuts=(), kind=jnp.bfloat16):
    gain = shard_levels(own_key, dims, cuts, -0.22, 0.18) if cuts else 1.0
    array = jax.random.normal(own_key, dims, jnp.float32) * scale * gain
    return jnp.minimum(jnp.maximum(array, -bound), bound).astype(kind)


def setup_inputs(seed: int = 0) -> dict:
    streams_of = jax.random.split(jax.random.key(seed), 13)
    features = centred(streams_of[0], (NODES, F), 1.0, 6.0, ((0, 32),))
    memory = jnp.clip(jax.random.uniform(streams_of[1], (NODES, F), jnp.float32, -1.0, 1.0) * shard_levels(streams_of[1], (NODES, F), ((0, 32),), -0.4, 0.0), -1.0, 1.0)
    tile_values = draw_tile_values(jax.random.fold_in(streams_of[12], 71), 0)
    tile_rows = draw_tile_rows(jax.random.fold_in(streams_of[12], 71), 0)
    tile_cols = draw_tile_cols(jax.random.fold_in(streams_of[12], 71), 0)
    tile_count = draw_tile_count(jax.random.fold_in(streams_of[12], 71), 0)
    conv_weight = centred(streams_of[6], (F, F), F ** -0.5, 0.25)
    conv_bias = centred(streams_of[7], (F,), 0.5, 3.0, (), jnp.float32)
    input_weight = centred(streams_of[8], (F, 3 * F), F ** -0.5, 0.25)
    input_bias = centred(streams_of[9], (3 * F,), 0.5, 3.0, (), jnp.float32)
    hidden_weight = centred(streams_of[10], (F, 3 * F), F ** -0.5, 0.25)
    hidden_bias = centred(streams_of[11], (3 * F,), 0.5, 3.0, (), jnp.float32)
    return {"features": features, "memory": memory, "tile_values": tile_values, "tile_rows": tile_rows, "tile_cols": tile_cols, "tile_count": tile_count, "conv_weight": conv_weight, "conv_bias": conv_bias, "input_weight": input_weight, "input_bias": input_bias, "hidden_weight": hidden_weight, "hidden_bias": hidden_bias}


norm_epsilon = 1e-06

def gru_update(message, memory, input_weight, input_bias, hidden_weight, hidden_bias):
    width = memory.shape[1]
    from_input = jnp.dot(message, input_weight, preferred_element_type=jnp.float32) + input_bias
    held = memory.astype(jnp.bfloat16)
    from_memory = jnp.dot(held, hidden_weight, preferred_element_type=jnp.float32) + hidden_bias
    reset = jax.nn.sigmoid(from_input[:, :width] + from_memory[:, :width])
    update = jax.nn.sigmoid(from_input[:, width:2 * width] + from_memory[:, width:2 * width])
    candidate = jnp.tanh(from_input[:, 2 * width:] + reset * from_memory[:, 2 * width:])
    return (1.0 - update) * candidate + update * memory

def device_product(tile_data, row_ids, col_ids, live_count, panel):
    live = jnp.arange(tile_data.shape[0]) < live_count
    tiles_wide = jnp.where(live[:, None, None], tile_data.astype(jnp.float32), jnp.float32(0.0))
    picked = panel[col_ids].astype(jnp.float32)
    products = jnp.einsum('tpq,tqf->tpf', tiles_wide, picked)
    return jnp.zeros((ROW_BLOCKS, TILE, F), jnp.float32).at[row_ids].add(products)

def reference(features, memory, tile_values, tile_rows, tile_cols, tile_count, conv_weight, conv_bias, input_weight, input_bias, hidden_weight, hidden_bias):
    live = jnp.arange(SLOTS)[None, None, :] < tile_count[:, :, None]
    column_sums = lax.optimization_barrier(jnp.sum(tile_values, axis=3, dtype=jnp.float32)) * live[..., None]
    group_index = jnp.broadcast_to(jnp.arange(N_ROW)[:, None, None], tile_cols.shape)
    out_degree = 1.0 + jnp.zeros((N_ROW, COL_BLOCKS, TILE), jnp.float32).at[group_index, tile_cols].add(column_sums)
    scaled = (features.reshape(N_ROW, COL_BLOCKS, TILE, F).astype(jnp.float32) * lax.rsqrt(out_degree)[..., None]).astype(jnp.bfloat16)

    def one_group(target):

        def one_source(source):
            return device_product(tile_values[source, target], tile_rows[source, target], tile_cols[source, target], tile_count[source, target], scaled[source])
        pieces = lax.map(one_source, jnp.arange(N_ROW))
        return lax.optimization_barrier(jnp.sum(pieces, axis=0))
    partial_value = lax.map(one_group, jnp.arange(N_COL)).reshape(NODES, F)
    normed = (partial_value / jnp.sqrt(lax.optimization_barrier(jnp.mean(partial_value * partial_value, axis=1, keepdims=True)) + norm_epsilon)).astype(jnp.bfloat16)
    message = jax.nn.relu(jnp.dot(normed, conv_weight, preferred_element_type=jnp.float32) + conv_bias).astype(jnp.bfloat16)
    return gru_update(message, memory, input_weight, input_bias, hidden_weight, hidden_bias)
```

```python
import functools

import jax
import jax.numpy as jnp
from jax import lax
from jax.experimental import pallas as pl
from jax.experimental.pallas import tpu as pltpu
from jax.sharding import PartitionSpec as P

norm_epsilon = 1e-06
MIB = 1 << 20
LANES = 128


def vmem():
    return pl.BlockSpec(memory_space=pltpu.VMEM)


def smem():
    return pl.BlockSpec(memory_space=pltpu.SMEM)


def params(limit_mib):
    return pltpu.CompilerParams(vmem_limit_bytes=limit_mib * MIB)


def cost(flops, bytes_accessed):
    return pl.CostEstimate(flops=flops, bytes_accessed=bytes_accessed, transcendentals=0)


def arrival_place(owner, me, n):
    step = lax.rem(lax.shift_right_logical(me, 1) - lax.shift_right_logical(owner, 1) + n // 2, n // 2)
    return 2 * step + ((owner ^ me) & 1)


def arrival_owner(place, me, n):
    return lax.rem((me ^ (place % 2)) - 2 * (place // 2) + n, n)


def build_kernel(own_rows, n_col, place_ref, count_ref, rows_ref, cols_ref, tiles_ref, dense_ref, degree_ref, acc_ref):
    row_me, col_me = place_ref[0], place_ref[1]
    size = tiles_ref.shape[1]
    per = own_rows // size
    dense_ref[...] = jnp.zeros_like(dense_ref)
    acc_ref[...] = jnp.zeros_like(acc_ref)

    def one(slot, carry):
        a, b = rows_ref[slot], cols_ref[slot]
        row = ((lax.div(a, per) ^ row_me) * per + lax.rem(a, per)) * size
        col = (arrival_place(lax.div(b, per), col_me, n_col) * per + lax.rem(b, per)) * size
        tile = tiles_ref[slot]
        dense_ref[pl.ds(pl.multiple_of(row, size), size), pl.ds(pl.multiple_of(col, size), size)] = tile
        wide = tile.astype(jnp.float32).reshape(size // 8, 8, size)
        acc_ref[b] += jnp.sum(wide, axis=0)
        return carry

    lax.fori_loop(0, count_ref[0], one, 0)
    degree_ref[...] = jnp.sum(acc_ref[...], axis=1)


def scale_kernel(own_rows, n_col, place_ref, degree_ref, scale_ref):
    col_me = place_ref[1]
    size = degree_ref.shape[1]
    per = own_rows // size
    for place in range(n_col):
        owner = arrival_owner(place, col_me, n_col)
        for half in range(per):
            line = lax.rsqrt(1.0 + degree_ref[pl.ds(owner * per + half, 1), :])
            spread = jnp.broadcast_to(line, (size, size)).T
            scale_ref[pl.ds((place * per + half) * size, size), :] = spread


def product_kernel(n_row, *refs):
    dense_ref, scale_ref = refs[0], refs[1]
    panel_ref = refs[-1]
    out_refs = refs[-1 - n_row : -1]
    block_refs = refs[2 : -1 - n_row]
    own_rows, width = block_refs[0].shape
    for place, block in enumerate(block_refs):
        rows = slice(place * own_rows, (place + 1) * own_rows)
        scale = scale_ref[rows, :]
        for left in range(0, width, LANES):
            cut = slice(left, left + LANES)
            panel_ref[rows, cut] = (block[:, cut].astype(jnp.float32) * scale).astype(jnp.bfloat16)
    for part in reversed(range(n_row)):
        rows = slice(part * own_rows, (part + 1) * own_rows)
        value = jnp.dot(dense_ref[rows, :], panel_ref[...], preferred_element_type=jnp.float32)
        out_refs[part][...] = value.astype(out_refs[part].dtype)


def sigmoid(x):
    return 0.5 * jnp.tanh(0.5 * x) + 0.5


def tail_kernel(*refs):
    (conv_ref, conv_bias_ref, input_ref, input_bias_ref, gates_ref, memory_ref), sums = refs[:6], refs[6:-1]
    out_ref = refs[-1]
    width = memory_ref.shape[1]
    owned = sums[0][...].astype(jnp.float32)
    for other in sums[1:]:
        owned = owned + other[...].astype(jnp.float32)
    spread = jnp.mean(owned * owned, axis=1, keepdims=True) + norm_epsilon
    normed = (owned / jnp.sqrt(spread)).astype(jnp.bfloat16)
    message = jnp.maximum(
        jnp.dot(normed, conv_ref[...], preferred_element_type=jnp.float32) + conv_bias_ref[...], 0.0
    ).astype(jnp.bfloat16)

    def gate(index):
        cut = slice(index * width, (index + 1) * width)
        dots = jnp.dot(message, input_ref[:, cut], preferred_element_type=jnp.float32)
        return dots + input_bias_ref[:, cut], gates_ref[:, cut]

    mine, held = gate(0)
    reset = sigmoid(mine + held)
    mine, held = gate(2)
    candidate = jnp.tanh(mine + reset * held)
    mine, held = gate(1)
    update = sigmoid(mine + held)
    out_ref[...] = (1.0 - update) * candidate + update * memory_ref[...]


def on_device(
    features,
    memory,
    tile_values,
    tile_rows,
    tile_cols,
    tile_count,
    conv_weight,
    conv_bias,
    input_weight,
    input_bias,
    hidden_weight,
    hidden_bias,
):
    own_rows, width = features.shape
    n_row, n_col = lax.axis_size("row"), lax.axis_size("col")
    slots, size = tile_values.shape[2], tile_values.shape[3]
    dst_rows, src_rows = own_rows * n_row, own_rows * n_col
    col_blocks = src_rows // size
    place = jnp.stack([lax.axis_index("row"), lax.axis_index("col")]).astype(jnp.int32)

    pair = [(i, i ^ 1) for i in range(n_col)]
    ring = [(i, (i + 2) % n_col) for i in range(n_col)]
    blocks = []
    riding = features
    for step in range(n_col // 2):
        blocks += [riding, lax.ppermute(riding, "col", pair)]
        if step + 1 < n_col // 2:
            riding = lax.ppermute(riding, "col", ring)

    dense, degree = pl.pallas_call(
        functools.partial(build_kernel, own_rows, n_col),
        out_shape=(
            jax.ShapeDtypeStruct((dst_rows, src_rows), jnp.bfloat16),
            jax.ShapeDtypeStruct((col_blocks, size), jnp.float32),
        ),
        in_specs=[smem()] * 4 + [vmem()],
        out_specs=(vmem(), vmem()),
        scratch_shapes=[pltpu.VMEM((col_blocks, 8, size), jnp.float32)],
        compiler_params=params(52),
        cost_estimate=cost(0, 2 * slots * size * size + 2 * dst_rows * src_rows),
        name="build",
    )(place, tile_count.reshape(1), tile_rows.reshape(slots), tile_cols.reshape(slots), tile_values.reshape(slots, size, size))

    bit = 1
    while bit < n_col:
        swap = [(i, i ^ bit) for i in range(n_col)]
        degree = degree + lax.ppermute(degree, "col", swap)
        bit *= 2

    scale = pl.pallas_call(
        functools.partial(scale_kernel, own_rows, n_col),
        out_shape=jax.ShapeDtypeStruct((src_rows, size), jnp.float32),
        in_specs=[smem(), vmem()],
        out_specs=vmem(),
        compiler_params=params(16),
        cost_estimate=cost(0, 4 * src_rows * size),
        name="scale",
    )(place, degree)

    gates = (
        jnp.dot(memory.astype(jnp.bfloat16), hidden_weight, preferred_element_type=jnp.float32) + hidden_bias
    )

    kept = [part == 0 or (part & (part - 1)) == 0 and part > 1 for part in range(n_row)]
    parts = pl.pallas_call(
        functools.partial(product_kernel, n_row),
        out_shape=tuple(
            jax.ShapeDtypeStruct((own_rows, width), jnp.float32 if keep else jnp.bfloat16) for keep in kept
        ),
        in_specs=[vmem()] * (2 + n_col),
        out_specs=tuple([vmem()] * n_row),
        scratch_shapes=[pltpu.VMEM((src_rows, width), jnp.bfloat16)],
        compiler_params=params(56),
        cost_estimate=cost(2 * dst_rows * src_rows * width, 2 * dst_rows * src_rows + 2 * src_rows * width),
        name="product",
    )(dense, scale, *blocks)

    sums = [[part] for part in parts]
    bit = 1
    while bit < n_row:
        swap = [(i, i ^ bit) for i in range(n_row)]
        for part in reversed(range(n_row)):
            if part & bit and part & (bit - 1) == 0:
                total = functools.reduce(
                    lambda x, y: x.astype(jnp.float32) + y.astype(jnp.float32), sums[part]
                ).astype(jnp.bfloat16)
                sums[part ^ bit].append(lax.ppermute(total, "row", swap))
        bit *= 2

    return pl.pallas_call(
        tail_kernel,
        out_shape=jax.ShapeDtypeStruct((own_rows, width), jnp.float32),
        in_specs=[vmem()] * (6 + len(sums[0])),
        out_specs=vmem(),
        compiler_params=params(32),
        cost_estimate=cost(8 * own_rows * width * width, 8 * width * width + 20 * own_rows * width),
        name="tail",
    )(
        conv_weight,
        conv_bias.reshape(1, width),
        input_weight,
        input_bias.reshape(1, 3 * width),
        gates,
        memory,
        *sums[0],
    )


def solution(mesh):
    placed = (
        P(("row", "col"), None),
        P(("col", "row"), None),
        P("row", "col", None, None, None),
        P("row", "col", None),
        P("row", "col", None),
        P("row", "col"),
        P(),
        P(),
        P(),
        P(),
        P(),
        P(),
    )
    return jax.shard_map(
        on_device, mesh=mesh, in_specs=placed, out_specs=P(("col", "row"), None), check_vma=False
    )
```

```python
import functools

import jax
import jax.numpy as jnp
from jax import lax
from jax.experimental import pallas as pl
from jax.experimental.pallas import tpu as pltpu
from jax.sharding import PartitionSpec as P

norm_epsilon = 1e-06
MIB = 1 << 20
LANES = 128


def vmem():
    return pl.BlockSpec(memory_space=pltpu.VMEM)


def smem():
    return pl.BlockSpec(memory_space=pltpu.SMEM)


def params(size):
    return pltpu.CompilerParams(vmem_limit_bytes=size + size // 4 + 4 * MIB)


def cost(flops, bytes_accessed):
    return pl.CostEstimate(flops=flops, bytes_accessed=bytes_accessed, transcendentals=0)


def arrival_place(owner, me, n):
    step = lax.rem(lax.shift_right_logical(me, 1) - lax.shift_right_logical(owner, 1) + n // 2, n // 2)
    return 2 * step + ((owner ^ me) & 1)


def arrival_owner(place, me, n):
    return lax.rem((me ^ (place % 2)) - 2 * (place // 2) + n, n)


def build_kernel(own_rows, n_col, place_ref, count_ref, rows_ref, cols_ref, tiles_ref, dense_ref, degree_ref, acc_ref):
    row_me, col_me = place_ref[0], place_ref[1]
    size = tiles_ref.shape[1]
    per = own_rows // size
    dense_ref[...] = jnp.zeros_like(dense_ref)
    acc_ref[...] = jnp.zeros_like(acc_ref)

    def one(slot, carry):
        a, b = rows_ref[slot], cols_ref[slot]
        row = ((lax.div(a, per) ^ row_me) * per + lax.rem(a, per)) * size
        col = (arrival_place(lax.div(b, per), col_me, n_col) * per + lax.rem(b, per)) * size
        tile = tiles_ref[slot]
        dense_ref[pl.ds(pl.multiple_of(row, size), size), pl.ds(pl.multiple_of(col, size), size)] = tile
        wide = tile.astype(jnp.float32).reshape(size // 8, 8, size)
        acc_ref[b] += jnp.sum(wide, axis=0)
        return carry

    lax.fori_loop(0, count_ref[0], one, 0)
    degree_ref[...] = jnp.sum(acc_ref[...], axis=1)


def scale_kernel(own_rows, n_col, place_ref, degree_ref, scale_ref):
    col_me = place_ref[1]
    size = degree_ref.shape[1]
    per = own_rows // size
    for place in range(n_col):
        owner = arrival_owner(place, col_me, n_col)
        for half in range(per):
            line = lax.rsqrt(1.0 + degree_ref[pl.ds(owner * per + half, 1), :])
            spread = jnp.broadcast_to(line, (size, size)).T
            scale_ref[pl.ds((place * per + half) * size, size), :] = spread


def product_kernel(n_blocks, n_row, first, last, *refs):
    dense_ref, scale_ref = refs[:2]
    block_refs = refs[2 : 2 + n_blocks]
    sum_refs = () if first else refs[2 + n_blocks : 3 + n_blocks]
    panel_ref = refs[-1]
    out_refs = refs[2 + n_blocks + len(sum_refs) : -1]
    own_rows, width = block_refs[0].shape
    for place, block in enumerate(block_refs):
        rows = slice(place * own_rows, (place + 1) * own_rows)
        scale = scale_ref[rows, :]
        for left in range(0, width, LANES):
            cut = slice(left, left + LANES)
            panel_ref[rows, cut] = (block[:, cut].astype(jnp.float32) * scale).astype(jnp.bfloat16)
    for part in reversed(range(n_row)):
        rows = slice(part * own_rows, (part + 1) * own_rows)
        value = jnp.dot(dense_ref[rows, :], panel_ref[...], preferred_element_type=jnp.float32)
        if not first:
            value = value + sum_refs[0][rows, :]
        if last:
            out_refs[part][...] = value.astype(out_refs[part].dtype)
        else:
            out_refs[0][rows, :] = value


def sigmoid(x):
    return 0.5 * jnp.tanh(0.5 * x) + 0.5


def tail_kernel(*refs):
    (conv_ref, conv_bias_ref, input_ref, input_bias_ref, gates_ref, memory_ref), sums = refs[:6], refs[6:-1]
    out_ref = refs[-1]
    width = memory_ref.shape[1]
    owned = sums[0][...].astype(jnp.float32)
    for other in sums[1:]:
        owned = owned + other[...].astype(jnp.float32)
    spread = jnp.mean(owned * owned, axis=1, keepdims=True) + norm_epsilon
    normed = (owned / jnp.sqrt(spread)).astype(jnp.bfloat16)
    message = jnp.maximum(
        jnp.dot(normed, conv_ref[...], preferred_element_type=jnp.float32) + conv_bias_ref[...], 0.0
    ).astype(jnp.bfloat16)

    def gate(index):
        cut = slice(index * width, (index + 1) * width)
        dots = jnp.dot(message, input_ref[:, cut], preferred_element_type=jnp.float32)
        return dots + input_bias_ref[:, cut], gates_ref[:, cut]

    mine, held = gate(0)
    reset = sigmoid(mine + held)
    mine, held = gate(2)
    candidate = jnp.tanh(mine + reset * held)
    mine, held = gate(1)
    update = sigmoid(mine + held)
    out_ref[...] = (1.0 - update) * candidate + update * memory_ref[...]


def on_device(
    features,
    memory,
    tile_values,
    tile_rows,
    tile_cols,
    tile_count,
    conv_weight,
    conv_bias,
    input_weight,
    input_bias,
    hidden_weight,
    hidden_bias,
):
    own_rows, width = features.shape
    n_row, n_col = lax.axis_size("row"), lax.axis_size("col")
    slots, size = tile_values.shape[2], tile_values.shape[3]
    dst_rows, src_rows = own_rows * n_row, own_rows * n_col
    col_blocks = src_rows // size
    place = jnp.stack([lax.axis_index("row"), lax.axis_index("col")]).astype(jnp.int32)

    pair = [(i, i ^ 1) for i in range(n_col)]
    ring = [(i, (i + 2) % n_col) for i in range(n_col)]
    riding = [features]
    paired = []

    def ride():
        if len(riding) < n_col // 2:
            riding.append(lax.ppermute(riding[-1], "col", ring))
        if len(paired) < n_col // 2:
            paired.append(lax.ppermute(riding[len(paired)], "col", pair))

    ride()
    dense, degree = pl.pallas_call(
        functools.partial(build_kernel, own_rows, n_col),
        out_shape=(
            jax.ShapeDtypeStruct((dst_rows, src_rows), jnp.bfloat16),
            jax.ShapeDtypeStruct((col_blocks, size), jnp.float32),
        ),
        in_specs=[smem()] * 4 + [vmem()],
        out_specs=(vmem(), vmem()),
        scratch_shapes=[pltpu.VMEM((col_blocks, 8, size), jnp.float32)],
        compiler_params=params(2 * slots * size * size + 2 * dst_rows * src_rows),
        cost_estimate=cost(0, 2 * slots * size * size + 2 * dst_rows * src_rows),
        name="build",
    )(place, tile_count.reshape(1), tile_rows.reshape(slots), tile_cols.reshape(slots), tile_values.reshape(slots, size, size))

    riding[-1], paired[-1], degree = lax.optimization_barrier((riding[-1], paired[-1], degree))
    ride()
    bit = 1
    while bit < n_col:
        swap = [(i, i ^ bit) for i in range(n_col)]
        degree = degree + lax.ppermute(degree, "col", swap)
        if bit == 2:
            riding[-1], paired[-1], degree = lax.optimization_barrier((riding[-1], paired[-1], degree))
        bit *= 2
    scale = pl.pallas_call(
        functools.partial(scale_kernel, own_rows, n_col),
        out_shape=jax.ShapeDtypeStruct((src_rows, size), jnp.float32),
        in_specs=[smem(), vmem()],
        out_specs=vmem(),
        compiler_params=params(4 * src_rows * size),
        cost_estimate=cost(0, 4 * src_rows * size),
        name="scale",
    )(place, degree)
    gates = (
        jnp.dot(memory.astype(jnp.bfloat16), hidden_weight, preferred_element_type=jnp.float32) + hidden_bias
    )
    riding[-1], paired[-1], gates = lax.optimization_barrier((riding[-1], paired[-1], gates))
    ride()
    while len(paired) < n_col // 2:
        riding[-1], paired[-1], scale = lax.optimization_barrier((riding[-1], paired[-1], scale))
        ride()
    blocks = [block for both in zip(riding, paired) for block in both]

    kept = [part == 0 or (part & (part - 1)) == 0 and part > 1 for part in range(n_row)]
    sum_shape = jax.ShapeDtypeStruct((dst_rows, width), jnp.float32)
    part_shapes = tuple(
        jax.ShapeDtypeStruct((own_rows, width), jnp.float32 if keep else jnp.bfloat16) for keep in kept
    )

    def product(begin, count, running, last):
        whole = pl.BlockSpec((dst_rows, width), lambda i: (0, 0))
        depth = count * own_rows
        return pl.pallas_call(
            functools.partial(product_kernel, count, n_row, running is None, last),
            grid=(1,),
            out_shape=part_shapes if last else sum_shape,
            in_specs=[
                pl.BlockSpec((dst_rows, depth), lambda i: (0, begin // count)),
                pl.BlockSpec((depth, size), lambda i: (begin // count, 0)),
            ]
            + [pl.BlockSpec((own_rows, width), lambda i: (0, 0))] * count
            + ([] if running is None else [whole]),
            out_specs=tuple([pl.BlockSpec((own_rows, width), lambda i: (0, 0))] * n_row) if last else whole,
            scratch_shapes=[pltpu.VMEM((depth, width), jnp.bfloat16)],
            compiler_params=params(2 * dst_rows * depth + 4 * depth * width + 4 * depth * size + 8 * dst_rows * width),
            cost_estimate=cost(2 * dst_rows * depth * width, 2 * dst_rows * depth + 6 * dst_rows * width),
            name="product",
        )(dense, scale, *blocks[begin : begin + count], *([] if running is None else [running]))

    running = product(0, n_col // 2, None, False)
    running = product(n_col // 2, n_col // 4, running, False)
    parts = product(n_col - n_col // 4, n_col // 4, running, True)

    sums = [[part] for part in parts]
    bit = 1
    while bit < n_row:
        swap = [(i, i ^ bit) for i in range(n_row)]
        for part in reversed(range(n_row)):
            if part & bit and part & (bit - 1) == 0:
                total = functools.reduce(
                    lambda x, y: x.astype(jnp.float32) + y.astype(jnp.float32), sums[part]
                ).astype(jnp.bfloat16)
                sums[part ^ bit].append(lax.ppermute(total, "row", swap))
        bit *= 2

    return pl.pallas_call(
        tail_kernel,
        out_shape=jax.ShapeDtypeStruct((own_rows, width), jnp.float32),
        in_specs=[vmem()] * (6 + len(sums[0])),
        out_specs=vmem(),
        compiler_params=params(8 * width * width + 30 * own_rows * width),
        cost_estimate=cost(8 * own_rows * width * width, 8 * width * width + 20 * own_rows * width),
        name="tail",
    )(
        conv_weight,
        conv_bias.reshape(1, width),
        input_weight,
        input_bias.reshape(1, 3 * width),
        gates,
        memory,
        *sums[0],
    )


def solution(mesh):
    placed = (
        P(("row", "col"), None),
        P(("col", "row"), None),
        P("row", "col", None, None, None),
        P("row", "col", None),
        P("row", "col", None),
        P("row", "col"),
        P(),
        P(),
        P(),
        P(),
        P(),
        P(),
    )
    return jax.shard_map(
        on_device, mesh=mesh, in_specs=placed, out_specs=P(("col", "row"), None), check_vma=False
    )
```

```python
import functools

import jax
import jax.numpy as jnp
from jax import lax
from jax.experimental import pallas as pl
from jax.experimental.pallas import tpu as pltpu
from jax.sharding import PartitionSpec as P

norm_epsilon = 1e-06
MIB = 1 << 20
LANES = 128
BUILD_STEPS = 4


def vmem():
    return pl.BlockSpec(memory_space=pltpu.VMEM)


def smem():
    return pl.BlockSpec(memory_space=pltpu.SMEM)


def params(size):
    return pltpu.CompilerParams(vmem_limit_bytes=size + size // 4 + 4 * MIB)


def cost(flops, bytes_accessed):
    return pl.CostEstimate(flops=flops, bytes_accessed=bytes_accessed, transcendentals=0)


def arrival_place(owner, me, n):
    step = lax.rem(lax.shift_right_logical(me, 1) - lax.shift_right_logical(owner, 1) + n // 2, n // 2)
    return 2 * step + ((owner ^ me) & 1)


def arrival_owner(place, me, n):
    return lax.rem((me ^ (place % 2)) - 2 * (place // 2) + n, n)


def halving_place(owner, me, n):
    away, place = owner ^ me, n - 1
    for bit in range(n.bit_length() - 1):
        place = place - (lax.shift_right_logical(away, bit) & 1) * (n >> (bit + 1))
    return place


def build_kernel(own_rows, n_row, n_col, place_ref, count_any, rows_any, cols_any, tiles_any, dense_ref, degree_ref, *scratch):
    acc_ref, tiles_ref, count_ref, rows_ref, cols_ref, sems = scratch
    row_me, col_me = place_ref[0], place_ref[1]
    slots, size = tiles_ref.shape[:2]
    per = own_rows // size
    some = slots // BUILD_STEPS
    small = [
        pltpu.make_async_copy(count_any, count_ref, sems.at[0]),
        pltpu.make_async_copy(rows_any, rows_ref, sems.at[1]),
        pltpu.make_async_copy(cols_any, cols_ref, sems.at[2]),
    ]
    large = [
        pltpu.make_async_copy(
            tiles_any.at[0, 0, pl.ds(step * some, some)], tiles_ref.at[pl.ds(step * some, some)], sems.at[3 + step]
        )
        for step in range(BUILD_STEPS)
    ]
    for copy in small + large:
        copy.start()
    dense_ref[...] = jnp.zeros_like(dense_ref)
    acc_ref[...] = jnp.zeros_like(acc_ref)

    def one(slot, carry):
        a, b = rows_ref[0, 0, slot], cols_ref[0, 0, slot]
        row = (halving_place(lax.div(a, per), row_me, n_row) * per + lax.rem(a, per)) * size
        col = (arrival_place(lax.div(b, per), col_me, n_col) * per + lax.rem(b, per)) * size
        tile = tiles_ref[slot]
        dense_ref[pl.ds(pl.multiple_of(row, size), size), pl.ds(pl.multiple_of(col, size), size)] = tile
        wide = tile.astype(jnp.float32).reshape(size // 8, 8, size)
        acc_ref[b] += jnp.sum(wide, axis=0)
        return carry

    for copy in small:
        copy.wait()
    for step, copy in enumerate(large):
        copy.wait()
        lax.fori_loop(step * some, jnp.minimum(count_ref[0, 0], (step + 1) * some), one, 0)
    degree_ref[...] = jnp.sum(acc_ref[...], axis=1)


def scale_kernel(own_rows, n_col, place_ref, degree_ref, scale_ref):
    col_me = place_ref[1]
    size = degree_ref.shape[1]
    per = own_rows // size
    for place in range(n_col):
        owner = arrival_owner(place, col_me, n_col)
        for half in range(per):
            line = lax.rsqrt(1.0 + degree_ref[pl.ds(owner * per + half, 1), :])
            spread = jnp.broadcast_to(line, (size, size)).T
            scale_ref[pl.ds((place * per + half) * size, size), :] = spread


def product_kernel(n_blocks, first, last, *refs):
    dense_ref, scale_ref = refs[:2]
    block_refs = refs[2 : 2 + n_blocks]
    sum_refs = () if first else refs[2 + n_blocks : 3 + n_blocks]
    panel_ref = refs[-1]
    out_refs = refs[2 + n_blocks + len(sum_refs) : -1]
    own_rows, width = block_refs[0].shape
    dst_rows = dense_ref.shape[0]
    for place, block in enumerate(block_refs):
        rows = slice(place * own_rows, (place + 1) * own_rows)
        scale = scale_ref[rows, :]
        for left in range(0, width, LANES):
            cut = slice(left, left + LANES)
            panel_ref[rows, cut] = (block[:, cut].astype(jnp.float32) * scale).astype(jnp.bfloat16)
    for top in range(0, dst_rows, own_rows):
        rows = slice(top, top + own_rows)
        value = jnp.dot(dense_ref[rows, :], panel_ref[...], preferred_element_type=jnp.float32)
        if not first:
            value = value + sum_refs[0][rows, :]
        if not last:
            out_refs[0][rows, :] = value
        elif top < dst_rows // 2:
            out_refs[0][rows, :] = value.astype(jnp.bfloat16)
        else:
            out_refs[1][top - dst_rows // 2 : top - dst_rows // 2 + own_rows, :] = value


def sigmoid(x):
    return 0.5 * jnp.tanh(0.5 * x) + 0.5


def tail_kernel(n_terms, *refs):
    (conv_ref, conv_bias_ref, input_ref, input_bias_ref, gates_ref, memory_ref), sums = refs[:6], refs[6:-1]
    out_ref = refs[-1]
    width = memory_ref.shape[1]

    def total(terms):
        return functools.reduce(lambda x, y: x + y, [term[...].astype(jnp.float32) for term in terms])

    owned = jnp.concatenate([total(sums[at : at + n_terms]) for at in range(0, len(sums), n_terms)], axis=1)
    spread = jnp.mean(owned * owned, axis=1, keepdims=True) + norm_epsilon
    normed = (owned / jnp.sqrt(spread)).astype(jnp.bfloat16)
    message = jnp.maximum(
        jnp.dot(normed, conv_ref[...], preferred_element_type=jnp.float32) + conv_bias_ref[...], 0.0
    ).astype(jnp.bfloat16)

    def gate(index):
        cut = slice(index * width, (index + 1) * width)
        dots = jnp.dot(message, input_ref[:, cut], preferred_element_type=jnp.float32)
        return dots + input_bias_ref[:, cut], gates_ref[:, cut]

    mine, held = gate(0)
    reset = sigmoid(mine + held)
    mine, held = gate(2)
    candidate = jnp.tanh(mine + reset * held)
    mine, held = gate(1)
    update = sigmoid(mine + held)
    out_ref[...] = (1.0 - update) * candidate + update * memory_ref[...]


def on_device(
    features,
    memory,
    tile_values,
    tile_rows,
    tile_cols,
    tile_count,
    conv_weight,
    conv_bias,
    input_weight,
    input_bias,
    hidden_weight,
    hidden_bias,
):
    own_rows, width = features.shape
    n_row, n_col = lax.axis_size("row"), lax.axis_size("col")
    slots, size = tile_values.shape[2], tile_values.shape[3]
    dst_rows, src_rows = own_rows * n_row, own_rows * n_col
    col_blocks = src_rows // size
    place = jnp.stack([lax.axis_index("row"), lax.axis_index("col")]).astype(jnp.int32)

    pair = [(i, i ^ 1) for i in range(n_col)]
    ring = [(i, (i + 2) % n_col) for i in range(n_col)]
    chunk = width // 2
    last_step = n_col // 2 - 1

    def ride(block):
        return lax.ppermute(block, "col", ring)

    def swap(block):
        return lax.ppermute(block, "col", pair)

    first, second = features[:, :chunk], features[:, chunk:]
    riding = [[first], [second]]
    paired = [[], []]

    def step(which):
        at = len(paired[which])
        block = riding[which][at]
        if at < last_step:
            riding[which].append(ride(block))
            paired[which].append(swap(block))
        else:
            paired[which].append(swap(block) if which == 0 else ride(paired[which][-1]))

    def hold(which, *others):
        values = lax.optimization_barrier((riding[which][-1], paired[which][-1], *others))
        riding[which][-1], paired[which][-1] = values[:2]
        return values[2:] if len(others) != 1 else values[2]

    step(0)
    step(1)
    dense, degree = pl.pallas_call(
        functools.partial(build_kernel, own_rows, n_row, n_col),
        out_shape=(
            jax.ShapeDtypeStruct((dst_rows, src_rows), jnp.bfloat16),
            jax.ShapeDtypeStruct((col_blocks, size), jnp.float32),
        ),
        in_specs=[smem()] + [pl.BlockSpec(memory_space=pltpu.HBM)] * 4,
        out_specs=(vmem(), vmem()),
        scratch_shapes=[
            pltpu.VMEM((col_blocks, 8, size), jnp.float32),
            pltpu.VMEM((slots, size, size), jnp.bfloat16),
            pltpu.SMEM(tile_count.shape, jnp.int32),
            pltpu.SMEM(tile_rows.shape, jnp.int32),
            pltpu.SMEM(tile_cols.shape, jnp.int32),
            pltpu.SemaphoreType.DMA((3 + BUILD_STEPS,)),
        ],
        compiler_params=params(2 * slots * size * size + 2 * dst_rows * src_rows),
        cost_estimate=cost(0, 2 * slots * size * size + 2 * dst_rows * src_rows),
        name="build",
    )(place, tile_count, tile_rows, tile_cols, tile_values)

    degree = hold(0, degree)
    step(0)
    degree = degree + swap(degree)
    degree = hold(1, degree)
    step(1)
    gates = (
        jnp.dot(memory.astype(jnp.bfloat16), hidden_weight, preferred_element_type=jnp.float32) + hidden_bias
    )
    bit = 2
    while bit < n_col:
        far = [(i, i ^ bit) for i in range(n_col)]
        degree = degree + lax.ppermute(degree, "col", far)
        if bit == 2:
            degree, gates = hold(0, degree, gates)
            step(0)
        bit *= 2
    degree = hold(1, degree)
    step(1)
    scale = pl.pallas_call(
        functools.partial(scale_kernel, own_rows, n_col),
        out_shape=jax.ShapeDtypeStruct((src_rows, size), jnp.float32),
        in_specs=[smem(), vmem()],
        out_specs=vmem(),
        compiler_params=params(4 * src_rows * size),
        cost_estimate=cost(0, 4 * src_rows * size),
        name="scale",
    )(place, degree)
    while len(paired[0]) < n_col // 2:
        scale = hold(0, scale)
        step(0)
        hold(1)
        step(1)

    def product(which, begin, count, running):
        last = running is not None
        depth = count * own_rows
        blocks = [block for both in zip(riding[which], paired[which]) for block in both][begin : begin + count]
        unit = n_col // 4 * own_rows
        full = pl.BlockSpec((dst_rows, chunk), lambda i: (0, 0))
        half = pl.BlockSpec((dst_rows // 2, chunk), lambda i: (0, 0))
        return pl.pallas_call(
            functools.partial(product_kernel, count, not last, last),
            grid=(1,),
            out_shape=(
                jax.ShapeDtypeStruct((dst_rows // 2, chunk), jnp.bfloat16),
                jax.ShapeDtypeStruct((dst_rows // 2, chunk), jnp.float32),
            )
            if last
            else jax.ShapeDtypeStruct((dst_rows, chunk), jnp.float32),
            in_specs=[
                pl.BlockSpec((dst_rows, depth), lambda i: (0, begin // count)),
                pl.BlockSpec((depth, size), lambda i: (begin // count, 0)),
            ]
            + [pl.BlockSpec((own_rows, chunk), lambda i: (0, 0))] * count
            + [full] * last,
            out_specs=(half, half) if last else full,
            scratch_shapes=[pltpu.VMEM((depth, chunk), jnp.bfloat16)],
            compiler_params=params(2 * dst_rows * depth + 4 * depth * chunk + 4 * depth * size + 8 * dst_rows * chunk),
            cost_estimate=cost(2 * dst_rows * depth * chunk, 2 * dst_rows * depth + 6 * dst_rows * chunk),
            name="product",
        )(dense, scale, *blocks, *([running] if last else []))

    most = n_col - n_col // 4
    early = [product(0, 0, most, None), product(1, 0, most, None)]

    def reduce_over_row(which):
        sent, kept = product(which, most, n_col // 4, early[which])
        terms = [kept]
        bit = 1
        while True:
            terms.append(lax.ppermute(sent, "row", [(i, i ^ bit) for i in range(n_row)]))
            bit *= 2
            if bit == n_row:
                return terms
            held = own_rows * n_row // bit
            sent = functools.reduce(
                lambda x, y: x + y,
                [term[term.shape[0] - held : term.shape[0] - held // 2].astype(jnp.float32) for term in terms],
            ).astype(jnp.bfloat16)

    terms = reduce_over_row(0) + reduce_over_row(1)

    def own_block(term):
        at = term.shape[0] // own_rows - 1
        return pl.BlockSpec((own_rows, chunk), lambda i: (at, 0))

    def entire(array):
        return pl.BlockSpec(array.shape, lambda i: (0, 0))

    operands = (
        conv_weight,
        conv_bias.reshape(1, width),
        input_weight,
        input_bias.reshape(1, 3 * width),
        gates,
        memory,
    )
    return pl.pallas_call(
        functools.partial(tail_kernel, len(terms) // 2),
        grid=(1,),
        out_shape=jax.ShapeDtypeStruct((own_rows, width), jnp.float32),
        in_specs=[entire(array) for array in operands] + [own_block(term) for term in terms],
        out_specs=pl.BlockSpec((own_rows, width), lambda i: (0, 0)),
        compiler_params=params(8 * width * width + 40 * own_rows * width),
        cost_estimate=cost(8 * own_rows * width * width, 8 * width * width + 20 * own_rows * width),
        name="tail",
    )(*operands, *terms)


def solution(mesh):
    placed = (
        P(("row", "col"), None),
        P(("col", "row"), None),
        P("row", "col", None, None, None),
        P("row", "col", None),
        P("row", "col", None),
        P("row", "col"),
        P(),
        P(),
        P(),
        P(),
        P(),
        P(),
    )
    return jax.shard_map(
        on_device, mesh=mesh, in_specs=placed, out_specs=P(("col", "row"), None), check_vma=False
    )
```

```python
import functools

import jax
import jax.numpy as jnp
import numpy as np
from jax import lax
from jax.experimental import pallas as pl
from jax.experimental.pallas import tpu as pltpu
from jax.sharding import PartitionSpec as P

norm_epsilon = 1e-06
MIB = 1 << 20
LANES = 128
BUILD_STEPS = 4


def vmem():
    return pl.BlockSpec(memory_space=pltpu.VMEM)


def smem():
    return pl.BlockSpec(memory_space=pltpu.SMEM)


def params(size):
    return pltpu.CompilerParams(vmem_limit_bytes=size + size // 4 + 4 * MIB)


def cost(flops, bytes_accessed):
    return pl.CostEstimate(flops=flops, bytes_accessed=bytes_accessed, transcendentals=0)


def ring_order(count):
    return [0, *range(1, count, 2), *reversed(range(2, count, 2))]


def arrival_owners(n_col):
    order = ring_order(n_col // 2)
    owners = np.zeros((n_col, n_col), np.int32)
    for col in range(n_col):
        for place in range(n_col):
            back = order[order.index(col // 2) - place // 2]
            owners[col, place] = 2 * back + (col + place) % 2
    return owners


def halving_places(n_row):
    order = [0]
    while len(order) < n_row:
        order = [2 * away + low for low in (1, 0) for away in order]
    return np.array([[order.index(owner ^ row) for owner in range(n_row)] for row in range(n_row)], np.int32)


def build_kernel(own_rows, n_row, n_col, table_ref, count_any, rows_any, cols_any, tiles_any, dense_ref, degree_ref, *scratch):
    acc_ref, tiles_ref, count_ref, rows_ref, cols_ref, sems = scratch
    slots, size = tiles_ref.shape[:2]
    per = own_rows // size
    some = slots // BUILD_STEPS
    small = [
        pltpu.make_async_copy(count_any, count_ref, sems.at[0]),
        pltpu.make_async_copy(rows_any, rows_ref, sems.at[1]),
        pltpu.make_async_copy(cols_any, cols_ref, sems.at[2]),
    ]
    large = [
        pltpu.make_async_copy(
            tiles_any.at[0, 0, pl.ds(step * some, some)], tiles_ref.at[pl.ds(step * some, some)], sems.at[3 + step]
        )
        for step in range(BUILD_STEPS)
    ]
    for copy in small + large:
        copy.start()
    dense_ref[...] = jnp.zeros_like(dense_ref)
    acc_ref[...] = jnp.zeros_like(acc_ref)

    def one(slot, carry):
        a, b = rows_ref[0, 0, slot], cols_ref[0, 0, slot]
        row = (table_ref[2 * n_col + lax.div(a, per)] * per + lax.rem(a, per)) * size
        col = (table_ref[n_col + lax.div(b, per)] * per + lax.rem(b, per)) * size
        tile = tiles_ref[slot]
        dense_ref[pl.ds(pl.multiple_of(row, size), size), pl.ds(pl.multiple_of(col, size), size)] = tile
        wide = tile.astype(jnp.float32).reshape(size // 8, 8, size)
        acc_ref[b] += jnp.sum(wide, axis=0)
        return carry

    for copy in small:
        copy.wait()
    for step, copy in enumerate(large):
        copy.wait()
        lax.fori_loop(step * some, jnp.minimum(count_ref[0, 0], (step + 1) * some), one, 0)
    degree_ref[...] = jnp.sum(acc_ref[...], axis=1)


def scale_kernel(own_rows, n_col, table_ref, degree_ref, scale_ref):
    size = degree_ref.shape[1]
    per = own_rows // size
    for place in range(n_col):
        owner = table_ref[place]
        for half in range(per):
            line = lax.rsqrt(1.0 + degree_ref[pl.ds(owner * per + half, 1), :])
            spread = jnp.broadcast_to(line, (size, size)).T
            scale_ref[pl.ds((place * per + half) * size, size), :] = spread


def product_kernel(n_blocks, first, last, *refs):
    dense_ref, scale_ref = refs[:2]
    block_refs = refs[2 : 2 + n_blocks]
    sum_refs = () if first else refs[2 + n_blocks : 3 + n_blocks]
    panel_ref = refs[-1]
    out_refs = refs[2 + n_blocks + len(sum_refs) : -1]
    own_rows, width = block_refs[0].shape
    dst_rows = dense_ref.shape[0]
    for place, block in enumerate(block_refs):
        rows = slice(place * own_rows, (place + 1) * own_rows)
        scale = scale_ref[rows, :]
        for left in range(0, width, LANES):
            cut = slice(left, left + LANES)
            panel_ref[rows, cut] = (block[:, cut].astype(jnp.float32) * scale).astype(jnp.bfloat16)
    for top in range(0, dst_rows, own_rows):
        rows = slice(top, top + own_rows)
        value = jnp.dot(dense_ref[rows, :], panel_ref[...], preferred_element_type=jnp.float32)
        if not first:
            value = value + sum_refs[0][rows, :]
        if not last:
            out_refs[0][rows, :] = value
        elif top < dst_rows // 2:
            out_refs[0][rows, :] = value.astype(jnp.bfloat16)
        else:
            out_refs[1][top - dst_rows // 2 : top - dst_rows // 2 + own_rows, :] = value


def sigmoid(x):
    return 0.5 * jnp.tanh(0.5 * x) + 0.5


def tail_kernel(*refs):
    (conv_ref, conv_bias_ref, input_ref, input_bias_ref, gates_ref, memory_ref), sums = refs[:6], refs[6:-1]
    out_ref = refs[-1]
    width = memory_ref.shape[1]

    owned = functools.reduce(lambda x, y: x + y, [term[...].astype(jnp.float32) for term in sums])
    spread = jnp.mean(owned * owned, axis=1, keepdims=True) + norm_epsilon
    normed = (owned / jnp.sqrt(spread)).astype(jnp.bfloat16)
    message = jnp.maximum(
        jnp.dot(normed, conv_ref[...], preferred_element_type=jnp.float32) + conv_bias_ref[...], 0.0
    ).astype(jnp.bfloat16)

    def gate(index):
        cut = slice(index * width, (index + 1) * width)
        dots = jnp.dot(message, input_ref[:, cut], preferred_element_type=jnp.float32)
        return dots + input_bias_ref[:, cut], gates_ref[:, cut]

    mine, held = gate(0)
    reset = sigmoid(mine + held)
    mine, held = gate(2)
    candidate = jnp.tanh(mine + reset * held)
    mine, held = gate(1)
    update = sigmoid(mine + held)
    out_ref[...] = (1.0 - update) * candidate + update * memory_ref[...]


def on_device(
    features,
    memory,
    tile_values,
    tile_rows,
    tile_cols,
    tile_count,
    conv_weight,
    conv_bias,
    input_weight,
    input_bias,
    hidden_weight,
    hidden_bias,
):
    own_rows, width = features.shape
    n_row, n_col = lax.axis_size("row"), lax.axis_size("col")
    slots, size = tile_values.shape[2], tile_values.shape[3]
    dst_rows, src_rows = own_rows * n_row, own_rows * n_col
    col_blocks = src_rows // size
    owners = arrival_owners(n_col)
    by_col = np.concatenate([owners, np.argsort(owners, axis=1).astype(np.int32)], axis=1)
    table = jnp.concatenate(
        [
            jnp.asarray(by_col)[lax.axis_index("col")],
            jnp.asarray(halving_places(n_row))[lax.axis_index("row")],
        ]
    )

    pair = [(i, i ^ 1) for i in range(n_col)]
    order = ring_order(n_col // 2)
    ring = [
        (2 * order[at - 1] + odd, 2 * order[at] + odd) for at in range(n_col // 2) for odd in range(2)
    ]
    riding = [features]
    paired = []

    def tie(*values):
        return lax.optimization_barrier(values)

    def ride():
        if len(riding) < n_col // 2:
            riding.append(lax.ppermute(riding[-1], "col", ring))

    def swap(*others):
        at = len(paired)
        block = riding[at]
        if paired and at + 1 < n_col // 2:
            block, paired[-1], *others = tie(block, paired[-1], *others)
        paired.append(lax.ppermute(block, "col", pair))
        return others

    ride()
    swap()
    dense, degree = pl.pallas_call(
        functools.partial(build_kernel, own_rows, n_row, n_col),
        out_shape=(
            jax.ShapeDtypeStruct((dst_rows, src_rows), jnp.bfloat16),
            jax.ShapeDtypeStruct((col_blocks, size), jnp.float32),
        ),
        in_specs=[smem()] + [pl.BlockSpec(memory_space=pltpu.HBM)] * 4,
        out_specs=(vmem(), vmem()),
        scratch_shapes=[
            pltpu.VMEM((col_blocks, 8, size), jnp.float32),
            pltpu.VMEM((slots, size, size), jnp.bfloat16),
            pltpu.SMEM(tile_count.shape, jnp.int32),
            pltpu.SMEM(tile_rows.shape, jnp.int32),
            pltpu.SMEM(tile_cols.shape, jnp.int32),
            pltpu.SemaphoreType.DMA((3 + BUILD_STEPS,)),
        ],
        compiler_params=params(2 * slots * size * size + 2 * dst_rows * src_rows),
        cost_estimate=cost(0, 2 * slots * size * size + 2 * dst_rows * src_rows),
        name="build",
    )(table, tile_count, tile_rows, tile_cols, tile_values)

    riding[-1], degree = tie(riding[-1], degree)
    ride()
    degree, memory = swap(degree, memory)
    gates = (
        jnp.dot(memory.astype(jnp.bfloat16), hidden_weight, preferred_element_type=jnp.float32) + hidden_bias
    )
    degree, gates = tie(degree, gates)
    bit = 1
    while bit < n_col:
        far = [(i, i ^ bit) for i in range(n_col)]
        degree = degree + lax.ppermute(degree, "col", far)
        if bit == 2:
            riding[-1], degree = tie(riding[-1], degree)
            ride()
            (degree,) = swap(degree)
        bit *= 2
    scale = pl.pallas_call(
        functools.partial(scale_kernel, own_rows, n_col),
        out_shape=jax.ShapeDtypeStruct((src_rows, size), jnp.float32),
        in_specs=[smem(), vmem()],
        out_specs=vmem(),
        compiler_params=params(4 * src_rows * size),
        cost_estimate=cost(0, 4 * src_rows * size),
        name="scale",
    )(table, degree)
    while len(paired) < n_col // 2:
        riding[-1], scale = tie(riding[-1], scale)
        ride()
        swap()
    blocks = [block for both in zip(riding, paired) for block in both]

    def product(begin, count, running):
        last = running is not None
        depth = count * own_rows
        full = pl.BlockSpec((dst_rows, width), lambda i: (0, 0))
        half = pl.BlockSpec((dst_rows // 2, width), lambda i: (0, 0))
        return pl.pallas_call(
            functools.partial(product_kernel, count, not last, last),
            grid=(1,),
            out_shape=(
                jax.ShapeDtypeStruct((dst_rows // 2, width), jnp.bfloat16),
                jax.ShapeDtypeStruct((dst_rows // 2, width), jnp.float32),
            )
            if last
            else jax.ShapeDtypeStruct((dst_rows, width), jnp.float32),
            in_specs=[
                pl.BlockSpec((dst_rows, depth), lambda i: (0, begin // count)),
                pl.BlockSpec((depth, size), lambda i: (begin // count, 0)),
            ]
            + [pl.BlockSpec((own_rows, width), lambda i: (0, 0))] * count
            + [full] * last,
            out_specs=(half, half) if last else full,
            scratch_shapes=[pltpu.VMEM((depth, width), jnp.bfloat16)],
            compiler_params=params(2 * dst_rows * depth + 4 * depth * width + 4 * depth * size + 8 * dst_rows * width),
            cost_estimate=cost(2 * dst_rows * depth * width, 2 * dst_rows * depth + 6 * dst_rows * width),
            name="product",
        )(dense, scale, *blocks[begin : begin + count], *([running] if last else []))

    most = n_col - n_col // 4
    sent, kept = product(most, n_col // 4, product(0, most, None))
    terms = [kept]
    bit = 1
    while True:
        terms.append(lax.ppermute(sent, "row", [(i, i ^ bit) for i in range(n_row)]))
        bit *= 2
        if bit == n_row:
            break
        held = own_rows * n_row // bit
        sent = functools.reduce(
            lambda x, y: x + y,
            [term[term.shape[0] - held : term.shape[0] - held // 2].astype(jnp.float32) for term in terms],
        ).astype(jnp.bfloat16)

    def own_block(term):
        at = term.shape[0] // own_rows - 1
        return pl.BlockSpec((own_rows, width), lambda i: (at, 0))

    def entire(array):
        return pl.BlockSpec(array.shape, lambda i: (0, 0))

    operands = (
        conv_weight,
        conv_bias.reshape(1, width),
        input_weight,
        input_bias.reshape(1, 3 * width),
        gates,
        memory,
    )
    return pl.pallas_call(
        tail_kernel,
        grid=(1,),
        out_shape=jax.ShapeDtypeStruct((own_rows, width), jnp.float32),
        in_specs=[entire(array) for array in operands] + [own_block(term) for term in terms],
        out_specs=pl.BlockSpec((own_rows, width), lambda i: (0, 0)),
        compiler_params=params(8 * width * width + 40 * own_rows * width),
        cost_estimate=cost(8 * own_rows * width * width, 8 * width * width + 20 * own_rows * width),
        name="tail",
    )(*operands, *terms)


def solution(mesh):
    placed = (
        P(("row", "col"), None),
        P(("col", "row"), None),
        P("row", "col", None, None, None),
        P("row", "col", None),
        P("row", "col", None),
        P("row", "col"),
        P(),
        P(),
        P(),
        P(),
        P(),
        P(),
    )
    return jax.shard_map(
        on_device, mesh=mesh, in_specs=placed, out_specs=P(("col", "row"), None), check_vma=False
    )
```

```python
import functools

import jax
import jax.numpy as jnp
from jax import lax
from jax.experimental import pallas as pl
from jax.experimental.pallas import tpu as pltpu
from jax.sharding import PartitionSpec as P

norm_epsilon = 1e-06
MIB = 1 << 20
LANES = 128
BUILD_STEPS = 4


def vmem():
    return pl.BlockSpec(memory_space=pltpu.VMEM)


def smem():
    return pl.BlockSpec(memory_space=pltpu.SMEM)


def params(size):
    return pltpu.CompilerParams(vmem_limit_bytes=size + size // 4 + 4 * MIB)


def cost(flops, bytes_accessed):
    return pl.CostEstimate(flops=flops, bytes_accessed=bytes_accessed, transcendentals=0)


def ring_order(count):
    return [0, *range(1, count, 2), *reversed(range(2, count, 2))]


def ring_place(device, count):
    half = lax.shift_right_logical(device + 1, 1)
    return jnp.where((device & 1) == 1, half, lax.rem(count - half, count))


def ring_device(place, count):
    return jnp.where(place <= count // 2, jnp.maximum(2 * place - 1, 0), 2 * (count - place))


def arrival_place(owner, me, n):
    count = n // 2
    mine = ring_place(lax.shift_right_logical(me, 1), count)
    theirs = ring_place(lax.shift_right_logical(owner, 1), count)
    return 2 * lax.rem(mine - theirs + count, count) + ((owner ^ me) & 1)


def arrival_owner(place, me, n):
    count = n // 2
    mine = ring_place(lax.shift_right_logical(me, 1), count)
    back = lax.rem(mine - place // 2 + count, count)
    return 2 * ring_device(back, count) + ((me + place) & 1)


def halving_place(owner, me, n):
    away, place = owner ^ me, n - 1
    for bit in range(n.bit_length() - 1):
        place = place - (lax.shift_right_logical(away, bit) & 1) * (n >> (bit + 1))
    return place


def build_kernel(own_rows, n_row, n_col, place_ref, count_ref, rows_any, cols_any, tiles_any, dense_ref, degree_ref, *scratch):
    acc_ref, tiles_ref, rows_ref, cols_ref, sems = scratch
    row_me, col_me = place_ref[0], place_ref[1]
    slots, size = tiles_ref.shape[:2]
    per = own_rows // size
    some = slots // BUILD_STEPS
    small = [
        pltpu.make_async_copy(rows_any, rows_ref, sems.at[0]),
        pltpu.make_async_copy(cols_any, cols_ref, sems.at[1]),
    ]
    large = [
        pltpu.make_async_copy(
            tiles_any.at[0, 0, pl.ds(step * some, some)], tiles_ref.at[pl.ds(step * some, some)], sems.at[2 + step]
        )
        for step in range(BUILD_STEPS)
    ]
    for copy in small + large:
        copy.start()
    dense_ref[...] = jnp.zeros_like(dense_ref)
    acc_ref[...] = jnp.zeros_like(acc_ref)

    def one(slot, carry):
        a, b = rows_ref[0, 0, slot], cols_ref[0, 0, slot]
        row = (halving_place(lax.div(a, per), row_me, n_row) * per + lax.rem(a, per)) * size
        col = (arrival_place(lax.div(b, per), col_me, n_col) * per + lax.rem(b, per)) * size
        tile = tiles_ref[slot]
        dense_ref[pl.ds(pl.multiple_of(row, size), size), pl.ds(pl.multiple_of(col, size), size)] = tile
        wide = tile.astype(jnp.float32).reshape(size // 8, 8, size)
        acc_ref[b] += jnp.sum(wide, axis=0)
        return carry

    for copy in small:
        copy.wait()
    for step, copy in enumerate(large):
        copy.wait()
        lax.fori_loop(step * some, jnp.minimum(count_ref[0], (step + 1) * some), one, 0)
    degree_ref[...] = jnp.sum(acc_ref[...], axis=1)


def scale_kernel(own_rows, n_col, place_ref, degree_ref, scale_ref):
    col_me = place_ref[1]
    size = degree_ref.shape[1]
    per = own_rows // size
    for place in range(n_col):
        owner = arrival_owner(place, col_me, n_col)
        for half in range(per):
            line = lax.rsqrt(1.0 + degree_ref[pl.ds(owner * per + half, 1), :])
            spread = jnp.broadcast_to(line, (size, size)).T
            scale_ref[pl.ds((place * per + half) * size, size), :] = spread


def product_kernel(n_blocks, first, last, *refs):
    dense_ref, scale_ref = refs[:2]
    block_refs = refs[2 : 2 + n_blocks]
    sum_refs = () if first else refs[2 + n_blocks : 3 + n_blocks]
    panel_ref = refs[-1]
    out_refs = refs[2 + n_blocks + len(sum_refs) : -1]
    own_rows, width = block_refs[0].shape
    dst_rows = dense_ref.shape[0]
    for place, block in enumerate(block_refs):
        rows = slice(place * own_rows, (place + 1) * own_rows)
        scale = scale_ref[rows, :]
        for left in range(0, width, LANES):
            cut = slice(left, left + LANES)
            panel_ref[rows, cut] = (block[:, cut].astype(jnp.float32) * scale).astype(jnp.bfloat16)
    for top in range(0, dst_rows, own_rows):
        rows = slice(top, top + own_rows)
        value = jnp.dot(dense_ref[rows, :], panel_ref[...], preferred_element_type=jnp.float32)
        if not first:
            value = value + sum_refs[0][rows, :]
        if not last:
            out_refs[0][rows, :] = value
        elif top < dst_rows // 2:
            out_refs[0][rows, :] = value.astype(jnp.bfloat16)
        else:
            out_refs[1][top - dst_rows // 2 : top - dst_rows // 2 + own_rows, :] = value


def sigmoid(x):
    return 0.5 * jnp.tanh(0.5 * x) + 0.5


def tail_kernel(*refs):
    (conv_ref, conv_bias_ref, input_ref, input_bias_ref, gates_ref, memory_ref), sums = refs[:6], refs[6:-1]
    out_ref = refs[-1]
    width = memory_ref.shape[1]

    owned = functools.reduce(lambda x, y: x + y, [term[...].astype(jnp.float32) for term in sums])
    spread = jnp.mean(owned * owned, axis=1, keepdims=True) + norm_epsilon
    normed = (owned / jnp.sqrt(spread)).astype(jnp.bfloat16)
    message = jnp.maximum(
        jnp.dot(normed, conv_ref[...], preferred_element_type=jnp.float32) + conv_bias_ref[...], 0.0
    ).astype(jnp.bfloat16)

    def gate(index):
        cut = slice(index * width, (index + 1) * width)
        dots = jnp.dot(message, input_ref[:, cut], preferred_element_type=jnp.float32)
        return dots + input_bias_ref[:, cut], gates_ref[:, cut]

    mine, held = gate(0)
    reset = sigmoid(mine + held)
    mine, held = gate(2)
    candidate = jnp.tanh(mine + reset * held)
    mine, held = gate(1)
    update = sigmoid(mine + held)
    out_ref[...] = (1.0 - update) * candidate + update * memory_ref[...]


def on_device(
    features,
    memory,
    tile_values,
    tile_rows,
    tile_cols,
    tile_count,
    conv_weight,
    conv_bias,
    input_weight,
    input_bias,
    hidden_weight,
    hidden_bias,
):
    own_rows, width = features.shape
    n_row, n_col = lax.axis_size("row"), lax.axis_size("col")
    slots, size = tile_values.shape[2], tile_values.shape[3]
    dst_rows, src_rows = own_rows * n_row, own_rows * n_col
    col_blocks = src_rows // size
    place = jnp.stack([lax.axis_index("row"), lax.axis_index("col")]).astype(jnp.int32)

    pair = [(i, i ^ 1) for i in range(n_col)]
    order = ring_order(n_col // 2)
    ring = [
        (2 * order[at - 1] + odd, 2 * order[at] + odd) for at in range(n_col // 2) for odd in range(2)
    ]
    riding = [features]
    paired = []

    def tie(*values):
        return lax.optimization_barrier(values)

    def ride():
        if len(riding) < n_col // 2:
            riding.append(lax.ppermute(riding[-1], "col", ring))

    def swap(*others):
        at = len(paired)
        block = riding[at]
        if paired and at + 1 < n_col // 2:
            block, paired[-1], *others = tie(block, paired[-1], *others)
        paired.append(lax.ppermute(block, "col", pair))
        return others

    ride()
    swap()
    dense, degree = pl.pallas_call(
        functools.partial(build_kernel, own_rows, n_row, n_col),
        out_shape=(
            jax.ShapeDtypeStruct((dst_rows, src_rows), jnp.bfloat16),
            jax.ShapeDtypeStruct((col_blocks, size), jnp.float32),
        ),
        in_specs=[smem()] * 2 + [pl.BlockSpec(memory_space=pltpu.HBM)] * 3,
        out_specs=(vmem(), vmem()),
        scratch_shapes=[
            pltpu.VMEM((col_blocks, 8, size), jnp.float32),
            pltpu.VMEM((slots, size, size), jnp.bfloat16),
            pltpu.SMEM(tile_rows.shape, jnp.int32),
            pltpu.SMEM(tile_cols.shape, jnp.int32),
            pltpu.SemaphoreType.DMA((2 + BUILD_STEPS,)),
        ],
        compiler_params=params(2 * slots * size * size + 2 * dst_rows * src_rows),
        cost_estimate=cost(0, 2 * slots * size * size + 2 * dst_rows * src_rows),
        name="build",
    )(place, tile_count.reshape(1), *[pltpu.with_memory_space_constraint(x, pltpu.HBM) for x in (tile_rows, tile_cols, tile_values)])

    hop = 1
    while hop < n_col // 2:
        around = [
            (2 * order[at - hop] + odd, 2 * order[at] + odd) for at in range(n_col // 2) for odd in range(2)
        ]
        added = lax.ppermute(degree, "col", around)
        riding[-1], added = tie(riding[-1], added)
        ride()
        degree, memory = swap(degree + added, memory)
        hop *= 2
    riding[-1], added = tie(riding[-1], lax.ppermute(degree, "col", pair))
    degree = degree + added
    gates = (
        jnp.dot(memory.astype(jnp.bfloat16), hidden_weight, preferred_element_type=jnp.float32) + hidden_bias
    )
    scale = pl.pallas_call(
        functools.partial(scale_kernel, own_rows, n_col),
        out_shape=jax.ShapeDtypeStruct((src_rows, size), jnp.float32),
        in_specs=[smem(), vmem()],
        out_specs=vmem(),
        compiler_params=params(4 * src_rows * size),
        cost_estimate=cost(0, 4 * src_rows * size),
        name="scale",
    )(place, degree)
    while len(paired) < n_col // 2:
        ride()
        swap()
    blocks = [block for both in zip(riding, paired) for block in both]

    def product(begin, count, running):
        last = running is not None
        depth = count * own_rows
        full = pl.BlockSpec((dst_rows, width), lambda i: (0, 0))
        half = pl.BlockSpec((dst_rows // 2, width), lambda i: (0, 0))
        return pl.pallas_call(
            functools.partial(product_kernel, count, not last, last),
            grid=(1,),
            out_shape=(
                jax.ShapeDtypeStruct((dst_rows // 2, width), jnp.bfloat16),
                jax.ShapeDtypeStruct((dst_rows // 2, width), jnp.float32),
            )
            if last
            else jax.ShapeDtypeStruct((dst_rows, width), jnp.float32),
            in_specs=[
                pl.BlockSpec((dst_rows, depth), lambda i: (0, begin // count)),
                pl.BlockSpec((depth, size), lambda i: (begin // count, 0)),
            ]
            + [pl.BlockSpec((own_rows, width), lambda i: (0, 0))] * count
            + [full] * last,
            out_specs=(half, half) if last else full,
            scratch_shapes=[pltpu.VMEM((depth, width), jnp.bfloat16)],
            compiler_params=params(2 * dst_rows * depth + 4 * depth * width + 4 * depth * size + 8 * dst_rows * width),
            cost_estimate=cost(2 * dst_rows * depth * width, 2 * dst_rows * depth + 6 * dst_rows * width),
            name="product",
        )(dense, scale, *blocks[begin : begin + count], *([running] if last else []))

    most = n_col - n_col // 4
    sent, kept = product(most, n_col // 4, product(0, most, None))
    terms = [kept]
    bit = 1
    while True:
        terms.append(lax.ppermute(sent, "row", [(i, i ^ bit) for i in range(n_row)]))
        bit *= 2
        if bit == n_row:
            break
        held = own_rows * n_row // bit
        sent = functools.reduce(
            lambda x, y: x + y,
            [term[term.shape[0] - held : term.shape[0] - held // 2].astype(jnp.float32) for term in terms],
        ).astype(jnp.bfloat16)

    def own_block(term):
        at = term.shape[0] // own_rows - 1
        return pl.BlockSpec((own_rows, width), lambda i: (at, 0))

    def entire(array):
        return pl.BlockSpec(array.shape, lambda i: (0, 0))

    operands = (
        conv_weight,
        conv_bias.reshape(1, width),
        input_weight,
        input_bias.reshape(1, 3 * width),
        gates,
        memory,
    )
    return pl.pallas_call(
        tail_kernel,
        grid=(1,),
        out_shape=jax.ShapeDtypeStruct((own_rows, width), jnp.float32),
        in_specs=[entire(array) for array in operands] + [own_block(term) for term in terms],
        out_specs=pl.BlockSpec((own_rows, width), lambda i: (0, 0)),
        compiler_params=params(8 * width * width + 40 * own_rows * width),
        cost_estimate=cost(8 * own_rows * width * width, 8 * width * width + 20 * own_rows * width),
        name="tail",
    )(*operands, *terms)


def solution(mesh):
    placed = (
        P(("row", "col"), None),
        P(("col", "row"), None),
        P("row", "col", None, None, None),
        P("row", "col", None),
        P("row", "col", None),
        P("row", "col"),
        P(),
        P(),
        P(),
        P(),
        P(),
        P(),
    )
    return jax.shard_map(
        on_device, mesh=mesh, in_specs=placed, out_specs=P(("col", "row"), None), check_vma=False
    )
```

```python
import functools

import jax
import jax.numpy as jnp
from jax import lax
from jax.experimental import pallas as pl
from jax.experimental.pallas import tpu as pltpu
from jax.sharding import PartitionSpec as P

norm_epsilon = 1e-06
MIB = 1 << 20
LANES = 128
BUILD_STEPS = 4


def vmem():
    return pl.BlockSpec(memory_space=pltpu.VMEM)


def smem():
    return pl.BlockSpec(memory_space=pltpu.SMEM)


def params(size):
    return pltpu.CompilerParams(vmem_limit_bytes=size + size // 4 + 4 * MIB)


def cost(flops, bytes_accessed):
    return pl.CostEstimate(flops=flops, bytes_accessed=bytes_accessed, transcendentals=0)


def ring_order(count):
    return [0, *range(1, count, 2), *reversed(range(2, count, 2))]


def fold(place, count):
    return jnp.where(place <= count // 2, jnp.maximum(2 * place - 1, 0), 2 * (count - place))


def unfold(device, count):
    half = lax.shift_right_logical(device + 1, 1)
    return jnp.where((device & 1) == 1, half, lax.rem(count - half, count))


def arrival_place(owner, me, n):
    count = n // 2
    mine = unfold(lax.shift_right_logical(me, 1), count)
    theirs = unfold(lax.shift_right_logical(owner, 1), count)
    return 2 * fold(lax.rem(mine - theirs + count, count), count) + ((owner ^ me) & 1)


def arrival_owner(place, me, n):
    count = n // 2
    mine = unfold(lax.shift_right_logical(me, 1), count)
    back = lax.rem(mine - unfold(jnp.int32(place // 2), count) + count, count)
    return 2 * fold(back, count) + ((me + place) & 1)


def halving_place(owner, me, n):
    away, place = owner ^ me, n - 1
    for bit in range(n.bit_length() - 1):
        place = place - (lax.shift_right_logical(away, bit) & 1) * (n >> (bit + 1))
    return place


def build_kernel(own_rows, n_row, n_col, place_ref, count_ref, rows_any, cols_any, tiles_any, dense_ref, degree_ref, *scratch):
    acc_ref, tiles_ref, rows_ref, cols_ref, sems = scratch
    row_me, col_me = place_ref[0], place_ref[1]
    slots, size = tiles_ref.shape[:2]
    per = own_rows // size
    some = slots // BUILD_STEPS
    small = [
        pltpu.make_async_copy(rows_any, rows_ref, sems.at[0]),
        pltpu.make_async_copy(cols_any, cols_ref, sems.at[1]),
    ]
    large = [
        pltpu.make_async_copy(
            tiles_any.at[0, 0, pl.ds(step * some, some)], tiles_ref.at[pl.ds(step * some, some)], sems.at[2 + step]
        )
        for step in range(BUILD_STEPS)
    ]
    for copy in small + large:
        copy.start()
    dense_ref[...] = jnp.zeros_like(dense_ref)
    acc_ref[...] = jnp.zeros_like(acc_ref)

    def one(slot, carry):
        a, b = rows_ref[0, 0, slot], cols_ref[0, 0, slot]
        row = (halving_place(lax.div(a, per), row_me, n_row) * per + lax.rem(a, per)) * size
        col = (arrival_place(lax.div(b, per), col_me, n_col) * per + lax.rem(b, per)) * size
        tile = tiles_ref[slot]
        dense_ref[pl.ds(pl.multiple_of(row, size), size), pl.ds(pl.multiple_of(col, size), size)] = tile
        wide = tile.astype(jnp.float32).reshape(size // 8, 8, size)
        acc_ref[b] += jnp.sum(wide, axis=0)
        return carry

    for copy in small:
        copy.wait()
    for step, copy in enumerate(large):
        copy.wait()
        lax.fori_loop(step * some, jnp.minimum(count_ref[0], (step + 1) * some), one, 0)
    degree_ref[...] = jnp.sum(acc_ref[...], axis=1)


def scale_kernel(own_rows, n_col, place_ref, degree_ref, scale_ref):
    col_me = place_ref[1]
    size = degree_ref.shape[1]
    per = own_rows // size
    for place in range(n_col):
        owner = arrival_owner(place, col_me, n_col)
        for half in range(per):
            line = lax.rsqrt(1.0 + degree_ref[pl.ds(owner * per + half, 1), :])
            spread = jnp.broadcast_to(line, (size, size)).T
            scale_ref[pl.ds((place * per + half) * size, size), :] = spread


def product_kernel(n_blocks, first, last, *refs):
    dense_ref, scale_ref = refs[:2]
    block_refs = refs[2 : 2 + n_blocks]
    sum_refs = () if first else refs[2 + n_blocks : 3 + n_blocks]
    panel_ref = refs[-1]
    out_refs = refs[2 + n_blocks + len(sum_refs) : -1]
    own_rows, width = block_refs[0].shape
    dst_rows = dense_ref.shape[0]
    end = 0
    for block in block_refs:
        rows = slice(end, end + block.shape[0])
        end = rows.stop
        scale = scale_ref[rows, :]
        for left in range(0, width, LANES):
            cut = slice(left, left + LANES)
            panel_ref[rows, cut] = (block[:, cut].astype(jnp.float32) * scale).astype(jnp.bfloat16)
    for top in range(0, dst_rows, own_rows):
        rows = slice(top, top + own_rows)
        value = jnp.dot(dense_ref[rows, :], panel_ref[...], preferred_element_type=jnp.float32)
        if not first:
            value = value + sum_refs[0][rows, :]
        if not last:
            out_refs[0][rows, :] = value
        elif top < dst_rows // 2:
            out_refs[0][rows, :] = value.astype(jnp.bfloat16)
        else:
            out_refs[1][top - dst_rows // 2 : top - dst_rows // 2 + own_rows, :] = value


def sigmoid(x):
    return 0.5 * jnp.tanh(0.5 * x) + 0.5


def tail_kernel(*refs):
    (conv_ref, conv_bias_ref, input_ref, input_bias_ref, gates_ref, memory_ref), sums = refs[:6], refs[6:-1]
    out_ref = refs[-1]
    width = memory_ref.shape[1]

    owned = functools.reduce(lambda x, y: x + y, [term[...].astype(jnp.float32) for term in sums])
    spread = jnp.mean(owned * owned, axis=1, keepdims=True) + norm_epsilon
    normed = (owned / jnp.sqrt(spread)).astype(jnp.bfloat16)
    message = jnp.maximum(
        jnp.dot(normed, conv_ref[...], preferred_element_type=jnp.float32) + conv_bias_ref[...], 0.0
    ).astype(jnp.bfloat16)

    def gate(index):
        cut = slice(index * width, (index + 1) * width)
        dots = jnp.dot(message, input_ref[:, cut], preferred_element_type=jnp.float32)
        return dots + input_bias_ref[:, cut], gates_ref[:, cut]

    mine, held = gate(0)
    reset = sigmoid(mine + held)
    mine, held = gate(2)
    candidate = jnp.tanh(mine + reset * held)
    mine, held = gate(1)
    update = sigmoid(mine + held)
    out_ref[...] = (1.0 - update) * candidate + update * memory_ref[...]


def on_device(
    features,
    memory,
    tile_values,
    tile_rows,
    tile_cols,
    tile_count,
    conv_weight,
    conv_bias,
    input_weight,
    input_bias,
    hidden_weight,
    hidden_bias,
):
    own_rows, width = features.shape
    n_row, n_col = lax.axis_size("row"), lax.axis_size("col")
    slots, size = tile_values.shape[2], tile_values.shape[3]
    dst_rows, src_rows = own_rows * n_row, own_rows * n_col
    col_blocks = src_rows // size
    place = jnp.stack([lax.axis_index("row"), lax.axis_index("col")]).astype(jnp.int32)

    pair = [(i, i ^ 1) for i in range(n_col)]
    order = ring_order(n_col // 2)
    turns = n_col // 2
    half = own_rows // 2

    def around(hops):
        return [
            (2 * order[at] + odd, 2 * order[(at + hops) % turns] + odd) for at in range(turns) for odd in range(2)
        ]

    def move(block, to):
        return lax.ppermute(block, "col", to)

    def tie(*values):
        return lax.optimization_barrier(values)

    riding = [features, move(features, around(1))]
    paired = [move(features, pair)]
    riding.append(move(features, around(-1)))
    dense, degree = pl.pallas_call(
        functools.partial(build_kernel, own_rows, n_row, n_col),
        out_shape=(
            jax.ShapeDtypeStruct((dst_rows, src_rows), jnp.bfloat16),
            jax.ShapeDtypeStruct((col_blocks, size), jnp.float32),
        ),
        in_specs=[smem()] * 2 + [pl.BlockSpec(memory_space=pltpu.HBM)] * 3,
        out_specs=(vmem(), vmem()),
        scratch_shapes=[
            pltpu.VMEM((col_blocks, 8, size), jnp.float32),
            pltpu.VMEM((slots, size, size), jnp.bfloat16),
            pltpu.SMEM(tile_rows.shape, jnp.int32),
            pltpu.SMEM(tile_cols.shape, jnp.int32),
            pltpu.SemaphoreType.DMA((2 + BUILD_STEPS,)),
        ],
        compiler_params=params(2 * slots * size * size + 2 * dst_rows * src_rows),
        cost_estimate=cost(0, 2 * slots * size * size + 2 * dst_rows * src_rows),
        name="build",
    )(place, tile_count.reshape(1), *[pltpu.with_memory_space_constraint(x, pltpu.HBM) for x in (tile_rows, tile_cols, tile_values)])

    added = move(degree, pair)
    block, paired[0], degree = tie(riding[1], paired[0], degree)
    paired.append(move(block, pair))
    degree = degree + added
    hops = 1
    while hops < turns:
        added = move(degree, around(hops))
        if hops == 1:
            block, degree, memory = tie(riding[1], degree, memory)
            riding.append(move(block, around(1)))
            gates = (
                jnp.dot(memory.astype(jnp.bfloat16), hidden_weight, preferred_element_type=jnp.float32) + hidden_bias
            )
            block, added, gates = tie(riding[2], added, gates)
            paired.append(move(block, pair))
        degree = degree + added
        hops *= 2
    for turn in range(4, turns):
        paired.append(move(riding[turn - 1], pair))
        riding.append(move(riding[turn - 2], around(1 if turn % 2 else -1)))
    riding[-1], degree = tie(riding[-1], degree)
    last_pair = (move(riding[-1][:half], pair), move(paired[turns - 3][half:], around(1)))
    scale = pl.pallas_call(
        functools.partial(scale_kernel, own_rows, n_col),
        out_shape=jax.ShapeDtypeStruct((src_rows, size), jnp.float32),
        in_specs=[smem(), vmem()],
        out_specs=vmem(),
        compiler_params=params(4 * src_rows * size),
        cost_estimate=cost(0, 4 * src_rows * size),
        name="scale",
    )(place, degree)
    blocks = [block for both in zip(riding, paired) for block in both] + [riding[-1], *last_pair]

    def product(begin, count, blocks, running, last):
        depth = count * own_rows
        whole = pl.BlockSpec((dst_rows, width), lambda i: (0, 0))
        part = pl.BlockSpec((dst_rows // 2, width), lambda i: (0, 0))
        return pl.pallas_call(
            functools.partial(product_kernel, len(blocks), running is None, last),
            grid=(1,),
            out_shape=(
                jax.ShapeDtypeStruct((dst_rows // 2, width), jnp.bfloat16),
                jax.ShapeDtypeStruct((dst_rows // 2, width), jnp.float32),
            )
            if last
            else jax.ShapeDtypeStruct((dst_rows, width), jnp.float32),
            in_specs=[
                pl.BlockSpec((dst_rows, depth), lambda i: (0, begin // count)),
                pl.BlockSpec((depth, size), lambda i: (begin // count, 0)),
            ]
            + [pl.BlockSpec(block.shape, lambda i: (0, 0)) for block in blocks]
            + ([] if running is None else [whole]),
            out_specs=(part, part) if last else whole,
            scratch_shapes=[pltpu.VMEM((depth, width), jnp.bfloat16)],
            compiler_params=params(2 * dst_rows * depth + 4 * depth * width + 4 * depth * size + 8 * dst_rows * width),
            cost_estimate=cost(2 * dst_rows * depth * width, 2 * dst_rows * depth + 6 * dst_rows * width),
            name="product",
        )(dense, scale, *blocks, *([] if running is None else [running]))

    running = None
    many = n_col - 2 if n_col <= 8 else 6
    for begin in range(0, n_col - 2, many):
        running = product(begin, many, blocks[begin : begin + many], running, False)
    sent, kept = product(n_col - 2, 2, blocks[n_col - 2 :], running, True)
    terms = [kept]
    bit = 1
    while True:
        terms.append(lax.ppermute(sent, "row", [(i, i ^ bit) for i in range(n_row)]))
        bit *= 2
        if bit == n_row:
            break
        held = own_rows * n_row // bit
        sent = functools.reduce(
            lambda x, y: x + y,
            [term[term.shape[0] - held : term.shape[0] - held // 2].astype(jnp.float32) for term in terms],
        ).astype(jnp.bfloat16)

    def own_block(term):
        at = term.shape[0] // own_rows - 1
        return pl.BlockSpec((own_rows, width), lambda i: (at, 0))

    def entire(array):
        return pl.BlockSpec(array.shape, lambda i: (0, 0))

    operands = (
        conv_weight,
        conv_bias.reshape(1, width),
        input_weight,
        input_bias.reshape(1, 3 * width),
        gates,
        memory,
    )
    return pl.pallas_call(
        tail_kernel,
        grid=(1,),
        out_shape=jax.ShapeDtypeStruct((own_rows, width), jnp.float32),
        in_specs=[entire(array) for array in operands] + [own_block(term) for term in terms],
        out_specs=pl.BlockSpec((own_rows, width), lambda i: (0, 0)),
        compiler_params=params(8 * width * width + 40 * own_rows * width),
        cost_estimate=cost(8 * own_rows * width * width, 8 * width * width + 20 * own_rows * width),
        name="tail",
    )(*operands, *terms)


def solution(mesh):
    placed = (
        P(("row", "col"), None),
        P(("col", "row"), None),
        P("row", "col", None, None, None),
        P("row", "col", None),
        P("row", "col", None),
        P("row", "col"),
        P(),
        P(),
        P(),
        P(),
        P(),
        P(),
    )
    return jax.shard_map(
        on_device, mesh=mesh, in_specs=placed, out_specs=P(("col", "row"), None), check_vma=False
    )
```

```python
import functools

import jax
import jax.numpy as jnp
from jax import lax
from jax.experimental import pallas as pl
from jax.experimental.pallas import tpu as pltpu
from jax.sharding import PartitionSpec as P

norm_epsilon = 1e-06
MIB = 1 << 20
LANES = 128
BUILD_STEPS = 4


def vmem():
    return pl.BlockSpec(memory_space=pltpu.VMEM)


def smem():
    return pl.BlockSpec(memory_space=pltpu.SMEM)


def params(size):
    return pltpu.CompilerParams(vmem_limit_bytes=size + size // 4 + 4 * MIB)


def cost(flops, bytes_accessed):
    return pl.CostEstimate(flops=flops, bytes_accessed=bytes_accessed, transcendentals=0)


def ring_order(count):
    return [0, *range(1, count, 2), *reversed(range(2, count, 2))]


def ring_place(device, count):
    half = lax.shift_right_logical(device + 1, 1)
    return jnp.where((device & 1) == 1, half, lax.rem(count - half, count))


def ring_device(place, count):
    return jnp.where(place <= count // 2, jnp.maximum(2 * place - 1, 0), 2 * (count - place))


def arrival_place(owner, me, n):
    count = n // 2
    mine = ring_place(lax.shift_right_logical(me, 1), count)
    theirs = ring_place(lax.shift_right_logical(owner, 1), count)
    return 2 * lax.rem(mine - theirs + count, count) + ((owner ^ me) & 1)


def arrival_owner(place, me, n):
    count = n // 2
    mine = ring_place(lax.shift_right_logical(me, 1), count)
    back = lax.rem(mine - place // 2 + count, count)
    return 2 * ring_device(back, count) + ((me + place) & 1)


def halving_place(owner, me, n):
    away, place = owner ^ me, n - 1
    for bit in range(n.bit_length() - 1):
        place = place - (lax.shift_right_logical(away, bit) & 1) * (n >> (bit + 1))
    return place


def build_kernel(own_rows, n_row, n_col, place_ref, count_ref, rows_any, cols_any, tiles_any, dense_ref, degree_ref, *scratch):
    acc_ref, tiles_ref, rows_ref, cols_ref, sems = scratch
    row_me, col_me = place_ref[0], place_ref[1]
    slots, size = tiles_ref.shape[:2]
    per = own_rows // size
    some = slots // BUILD_STEPS
    small = [
        pltpu.make_async_copy(rows_any, rows_ref, sems.at[0]),
        pltpu.make_async_copy(cols_any, cols_ref, sems.at[1]),
    ]
    large = [
        pltpu.make_async_copy(
            tiles_any.at[0, 0, pl.ds(step * some, some)], tiles_ref.at[pl.ds(step * some, some)], sems.at[2 + step]
        )
        for step in range(BUILD_STEPS)
    ]
    for copy in small + large:
        copy.start()
    dense_ref[...] = jnp.zeros_like(dense_ref)
    acc_ref[...] = jnp.zeros_like(acc_ref)

    def one(slot, carry):
        a, b = rows_ref[0, 0, slot], cols_ref[0, 0, slot]
        row = (halving_place(lax.div(a, per), row_me, n_row) * per + lax.rem(a, per)) * size
        col = (arrival_place(lax.div(b, per), col_me, n_col) * per + lax.rem(b, per)) * size
        tile = tiles_ref[slot]
        dense_ref[pl.ds(pl.multiple_of(row, size), size), pl.ds(pl.multiple_of(col, size), size)] = tile
        wide = tile.astype(jnp.float32).reshape(size // 8, 8, size)
        acc_ref[b] += jnp.sum(wide, axis=0)
        return carry

    for copy in small:
        copy.wait()
    for step, copy in enumerate(large):
        copy.wait()
        lax.fori_loop(step * some, jnp.minimum(count_ref[0], (step + 1) * some), one, 0)
    degree_ref[...] = jnp.sum(acc_ref[...], axis=1)


def scale_kernel(own_rows, n_col, place_ref, degree_ref, scale_ref):
    col_me = place_ref[1]
    size = degree_ref.shape[1]
    per = own_rows // size
    for place in range(n_col):
        owner = arrival_owner(place, col_me, n_col)
        for half in range(per):
            line = lax.rsqrt(1.0 + degree_ref[pl.ds(owner * per + half, 1), :])
            spread = jnp.broadcast_to(line, (size, size)).T
            scale_ref[pl.ds((place * per + half) * size, size), :] = spread


def product_kernel(n_blocks, first, last, *refs):
    dense_ref, scale_ref = refs[:2]
    block_refs = refs[2 : 2 + n_blocks]
    sum_refs = () if first else refs[2 + n_blocks : 3 + n_blocks]
    panel_ref = refs[-1]
    out_refs = refs[2 + n_blocks + len(sum_refs) : -1]
    own_rows, width = block_refs[0].shape
    dst_rows = dense_ref.shape[0]
    for place, block in enumerate(block_refs):
        rows = slice(place * own_rows, (place + 1) * own_rows)
        scale = scale_ref[rows, :]
        for left in range(0, width, LANES):
            cut = slice(left, left + LANES)
            panel_ref[rows, cut] = (block[:, cut].astype(jnp.float32) * scale).astype(jnp.bfloat16)
    for top in range(0, dst_rows, own_rows):
        rows = slice(top, top + own_rows)
        value = jnp.dot(dense_ref[rows, :], panel_ref[...], preferred_element_type=jnp.float32)
        if not first:
            value = value + sum_refs[0][rows, :]
        if not last:
            out_refs[0][rows, :] = value
        elif top < dst_rows // 2:
            out_refs[0][rows, :] = value.astype(jnp.bfloat16)
        else:
            out_refs[1][top - dst_rows // 2 : top - dst_rows // 2 + own_rows, :] = value


def sigmoid(x):
    return 0.5 * jnp.tanh(0.5 * x) + 0.5


def tail_kernel(*refs):
    (conv_ref, conv_bias_ref, input_ref, input_bias_ref, gates_ref, memory_ref), sums = refs[:6], refs[6:-1]
    out_ref = refs[-1]
    width = memory_ref.shape[1]

    owned = functools.reduce(lambda x, y: x + y, [term[...].astype(jnp.float32) for term in sums])
    spread = jnp.mean(owned * owned, axis=1, keepdims=True) + norm_epsilon
    normed = (owned / jnp.sqrt(spread)).astype(jnp.bfloat16)
    message = jnp.maximum(
        jnp.dot(normed, conv_ref[...], preferred_element_type=jnp.float32) + conv_bias_ref[...], 0.0
    ).astype(jnp.bfloat16)

    def gate(index):
        cut = slice(index * width, (index + 1) * width)
        dots = jnp.dot(message, input_ref[:, cut], preferred_element_type=jnp.float32)
        return dots + input_bias_ref[:, cut], gates_ref[:, cut]

    mine, held = gate(0)
    reset = sigmoid(mine + held)
    mine, held = gate(2)
    candidate = jnp.tanh(mine + reset * held)
    mine, held = gate(1)
    update = sigmoid(mine + held)
    out_ref[...] = (1.0 - update) * candidate + update * memory_ref[...]


def on_device(
    features,
    memory,
    tile_values,
    tile_rows,
    tile_cols,
    tile_count,
    conv_weight,
    conv_bias,
    input_weight,
    input_bias,
    hidden_weight,
    hidden_bias,
):
    own_rows, width = features.shape
    n_row, n_col = lax.axis_size("row"), lax.axis_size("col")
    slots, size = tile_values.shape[2], tile_values.shape[3]
    dst_rows, src_rows = own_rows * n_row, own_rows * n_col
    col_blocks = src_rows // size
    place = jnp.stack([lax.axis_index("row"), lax.axis_index("col")]).astype(jnp.int32)

    pair = [(i, i ^ 1) for i in range(n_col)]
    order = ring_order(n_col // 2)
    ring = [
        (2 * order[at - 1] + odd, 2 * order[at] + odd) for at in range(n_col // 2) for odd in range(2)
    ]

    def tie(*values):
        return lax.optimization_barrier(values)

    def move(block, to):
        return lax.ppermute(block, "col", to)

    def around(hops):
        return [
            (2 * order[at - hops] + odd, 2 * order[at] + odd) for at in range(n_col // 2) for odd in range(2)
        ]

    riding = [features, move(features, ring)]
    paired = [move(features, pair)]
    dense, degree = pl.pallas_call(
        functools.partial(build_kernel, own_rows, n_row, n_col),
        out_shape=(
            jax.ShapeDtypeStruct((dst_rows, src_rows), jnp.bfloat16),
            jax.ShapeDtypeStruct((col_blocks, size), jnp.float32),
        ),
        in_specs=[smem()] * 2 + [pl.BlockSpec(memory_space=pltpu.HBM)] * 3,
        out_specs=(vmem(), vmem()),
        scratch_shapes=[
            pltpu.VMEM((col_blocks, 8, size), jnp.float32),
            pltpu.VMEM((slots, size, size), jnp.bfloat16),
            pltpu.SMEM(tile_rows.shape, jnp.int32),
            pltpu.SMEM(tile_cols.shape, jnp.int32),
            pltpu.SemaphoreType.DMA((2 + BUILD_STEPS,)),
        ],
        compiler_params=params(2 * slots * size * size + 2 * dst_rows * src_rows),
        cost_estimate=cost(0, 2 * slots * size * size + 2 * dst_rows * src_rows),
        name="build",
    )(place, tile_count.reshape(1), *[pltpu.with_memory_space_constraint(x, pltpu.HBM) for x in (tile_rows, tile_cols, tile_values)])

    added = [move(degree, around(hops)) for hops in range(1, n_col // 2)]
    riding[1], degree = tie(riding[1], degree)
    riding.append(move(riding[1], ring))
    block, paired[0], memory = tie(riding[1], paired[0], memory)
    paired.append(move(block, pair))
    gates = (
        jnp.dot(memory.astype(jnp.bfloat16), hidden_weight, preferred_element_type=jnp.float32) + hidden_bias
    )
    gates, *added = tie(gates, *added)
    degree = degree + functools.reduce(lambda x, y: x + y, added)
    added = move(degree, pair)
    for step in range(2, n_col // 2):
        block = riding[step]
        if step + 1 < n_col // 2:
            riding.append(move(block, ring))
            block, paired[-1], added = tie(block, paired[-1], added)
        paired.append(move(block, pair))
    degree = degree + added
    scale = pl.pallas_call(
        functools.partial(scale_kernel, own_rows, n_col),
        out_shape=jax.ShapeDtypeStruct((src_rows, size), jnp.float32),
        in_specs=[smem(), vmem()],
        out_specs=vmem(),
        compiler_params=params(4 * src_rows * size),
        cost_estimate=cost(0, 4 * src_rows * size),
        name="scale",
    )(place, degree)
    blocks = [block for both in zip(riding, paired) for block in both]

    def product(begin, count, running):
        last = running is not None
        depth = count * own_rows
        full = pl.BlockSpec((dst_rows, width), lambda i: (0, 0))
        half = pl.BlockSpec((dst_rows // 2, width), lambda i: (0, 0))
        return pl.pallas_call(
            functools.partial(product_kernel, count, not last, last),
            grid=(1,),
            out_shape=(
                jax.ShapeDtypeStruct((dst_rows // 2, width), jnp.bfloat16),
                jax.ShapeDtypeStruct((dst_rows // 2, width), jnp.float32),
            )
            if last
            else jax.ShapeDtypeStruct((dst_rows, width), jnp.float32),
            in_specs=[
                pl.BlockSpec((dst_rows, depth), lambda i: (0, begin // count)),
                pl.BlockSpec((depth, size), lambda i: (begin // count, 0)),
            ]
            + [pl.BlockSpec((own_rows, width), lambda i: (0, 0))] * count
            + [full] * last,
            out_specs=(half, half) if last else full,
            scratch_shapes=[pltpu.VMEM((depth, width), jnp.bfloat16)],
            compiler_params=params(2 * dst_rows * depth + 4 * depth * width + 4 * depth * size + 8 * dst_rows * width),
            cost_estimate=cost(2 * dst_rows * depth * width, 2 * dst_rows * depth + 6 * dst_rows * width),
            name="product",
        )(dense, scale, *blocks[begin : begin + count], *([running] if last else []))

    most = n_col - n_col // 4
    sent, kept = product(most, n_col // 4, product(0, most, None))
    terms = [kept]
    bit = 1
    while True:
        terms.append(lax.ppermute(sent, "row", [(i, i ^ bit) for i in range(n_row)]))
        bit *= 2
        if bit == n_row:
            break
        held = own_rows * n_row // bit
        sent = functools.reduce(
            lambda x, y: x + y,
            [term[term.shape[0] - held : term.shape[0] - held // 2].astype(jnp.float32) for term in terms],
        ).astype(jnp.bfloat16)

    def own_block(term):
        at = term.shape[0] // own_rows - 1
        return pl.BlockSpec((own_rows, width), lambda i: (at, 0))

    def entire(array):
        return pl.BlockSpec(array.shape, lambda i: (0, 0))

    operands = (
        conv_weight,
        conv_bias.reshape(1, width),
        input_weight,
        input_bias.reshape(1, 3 * width),
        gates,
        memory,
    )
    return pl.pallas_call(
        tail_kernel,
        grid=(1,),
        out_shape=jax.ShapeDtypeStruct((own_rows, width), jnp.float32),
        in_specs=[entire(array) for array in operands] + [own_block(term) for term in terms],
        out_specs=pl.BlockSpec((own_rows, width), lambda i: (0, 0)),
        compiler_params=params(8 * width * width + 40 * own_rows * width),
        cost_estimate=cost(8 * own_rows * width * width, 8 * width * width + 20 * own_rows * width),
        name="tail",
    )(*operands, *terms)


def solution(mesh):
    placed = (
        P(("row", "col"), None),
        P(("col", "row"), None),
        P("row", "col", None, None, None),
        P("row", "col", None),
        P("row", "col", None),
        P("row", "col"),
        P(),
        P(),
        P(),
        P(),
        P(),
        P(),
    )
    return jax.shard_map(
        on_device, mesh=mesh, in_specs=placed, out_specs=P(("col", "row"), None), check_vma=False
    )
```

```python
import functools

import jax
import jax.numpy as jnp
from jax import lax
from jax.experimental import pallas as pl
from jax.experimental.pallas import tpu as pltpu
from jax.sharding import PartitionSpec as P

norm_epsilon = 1e-06
MIB = 1 << 20
LANES = 128
BUILD_STEPS = 4


def vmem():
    return pl.BlockSpec(memory_space=pltpu.VMEM)


def smem():
    return pl.BlockSpec(memory_space=pltpu.SMEM)


def params(size):
    return pltpu.CompilerParams(vmem_limit_bytes=size + size // 4 + 4 * MIB)


def cost(flops, bytes_accessed):
    return pl.CostEstimate(flops=flops, bytes_accessed=bytes_accessed, transcendentals=0)


def ring_order(count):
    return [0, *range(1, count, 2), *reversed(range(2, count, 2))]


def ring_place(device, count):
    half = lax.shift_right_logical(device + 1, 1)
    return jnp.where((device & 1) == 1, half, lax.rem(count - half, count))


def ring_device(place, count):
    return jnp.where(place <= count // 2, jnp.maximum(2 * place - 1, 0), 2 * (count - place))


def arrival_place(owner, me, n):
    count = n // 2
    mine = ring_place(lax.shift_right_logical(me, 1), count)
    theirs = ring_place(lax.shift_right_logical(owner, 1), count)
    return 2 * lax.rem(mine - theirs + count, count) + ((owner ^ me) & 1)


def arrival_owner(place, me, n):
    count = n // 2
    mine = ring_place(lax.shift_right_logical(me, 1), count)
    back = lax.rem(mine - place // 2 + count, count)
    return 2 * ring_device(back, count) + ((me + place) & 1)


def halving_place(owner, me, n):
    away, place = owner ^ me, n - 1
    for bit in range(n.bit_length() - 1):
        place = place - (lax.shift_right_logical(away, bit) & 1) * (n >> (bit + 1))
    return place


def build_kernel(own_rows, n_row, n_col, place_ref, count_ref, rows_any, cols_any, tiles_any, dense_ref, degree_ref, *scratch):
    acc_ref, tiles_ref, rows_ref, cols_ref, sems = scratch
    row_me, col_me = place_ref[0], place_ref[1]
    slots, size = tiles_ref.shape[:2]
    per = own_rows // size
    some = slots // BUILD_STEPS
    small = [
        pltpu.make_async_copy(rows_any, rows_ref, sems.at[0]),
        pltpu.make_async_copy(cols_any, cols_ref, sems.at[1]),
    ]
    large = [
        pltpu.make_async_copy(
            tiles_any.at[0, 0, pl.ds(step * some, some)], tiles_ref.at[pl.ds(step * some, some)], sems.at[2 + step]
        )
        for step in range(BUILD_STEPS)
    ]
    for copy in small + large:
        copy.start()
    dense_ref[...] = jnp.zeros_like(dense_ref)
    acc_ref[...] = jnp.zeros_like(acc_ref)

    def one(slot, carry):
        a, b = rows_ref[0, 0, slot], cols_ref[0, 0, slot]
        row = (halving_place(lax.div(a, per), row_me, n_row) * per + lax.rem(a, per)) * size
        col = (arrival_place(lax.div(b, per), col_me, n_col) * per + lax.rem(b, per)) * size
        tile = tiles_ref[slot]
        dense_ref[pl.ds(pl.multiple_of(row, size), size), pl.ds(pl.multiple_of(col, size), size)] = tile
        wide = tile.astype(jnp.float32).reshape(size // 8, 8, size)
        acc_ref[b] += jnp.sum(wide, axis=0)
        return carry

    for copy in small:
        copy.wait()
    for step, copy in enumerate(large):
        copy.wait()
        lax.fori_loop(step * some, jnp.minimum(count_ref[0], (step + 1) * some), one, 0)
    degree_ref[...] = jnp.sum(acc_ref[...], axis=1)


def scale_kernel(own_rows, n_col, place_ref, degree_ref, scale_ref):
    col_me = place_ref[1]
    size = degree_ref.shape[1]
    per = own_rows // size
    for place in range(n_col):
        owner = arrival_owner(place, col_me, n_col)
        for half in range(per):
            line = lax.rsqrt(1.0 + degree_ref[pl.ds(owner * per + half, 1), :])
            spread = jnp.broadcast_to(line, (size, size)).T
            scale_ref[pl.ds((place * per + half) * size, size), :] = spread


def product_kernel(n_blocks, first, last, *refs):
    dense_ref, scale_ref = refs[:2]
    block_refs = refs[2 : 2 + n_blocks]
    sum_refs = () if first else refs[2 + n_blocks : 3 + n_blocks]
    panel_ref = refs[-1]
    out_refs = refs[2 + n_blocks + len(sum_refs) : -1]
    own_rows, width = block_refs[0].shape
    dst_rows = dense_ref.shape[0]
    end = 0
    for block in block_refs:
        rows = slice(end, end + block.shape[0])
        end = rows.stop
        scale = scale_ref[rows, :]
        for left in range(0, width, LANES):
            cut = slice(left, left + LANES)
            panel_ref[rows, cut] = (block[:, cut].astype(jnp.float32) * scale).astype(jnp.bfloat16)
    for top in range(0, dst_rows, own_rows):
        rows = slice(top, top + own_rows)
        value = jnp.dot(dense_ref[rows, :], panel_ref[...], preferred_element_type=jnp.float32)
        if not first:
            value = value + sum_refs[0][rows, :]
        if not last:
            out_refs[0][rows, :] = value
        elif top < dst_rows // 2:
            out_refs[0][rows, :] = value.astype(jnp.bfloat16)
        else:
            out_refs[1][top - dst_rows // 2 : top - dst_rows // 2 + own_rows, :] = value


def sigmoid(x):
    return 0.5 * jnp.tanh(0.5 * x) + 0.5


def tail_kernel(*refs):
    (conv_ref, conv_bias_ref, input_ref, input_bias_ref, gates_ref, memory_ref), sums = refs[:6], refs[6:-1]
    out_ref = refs[-1]
    width = memory_ref.shape[1]

    owned = functools.reduce(lambda x, y: x + y, [term[...].astype(jnp.float32) for term in sums])
    spread = jnp.mean(owned * owned, axis=1, keepdims=True) + norm_epsilon
    normed = (owned / jnp.sqrt(spread)).astype(jnp.bfloat16)
    message = jnp.maximum(
        jnp.dot(normed, conv_ref[...], preferred_element_type=jnp.float32) + conv_bias_ref[...], 0.0
    ).astype(jnp.bfloat16)

    def gate(index):
        cut = slice(index * width, (index + 1) * width)
        dots = jnp.dot(message, input_ref[:, cut], preferred_element_type=jnp.float32)
        return dots + input_bias_ref[:, cut], gates_ref[:, cut]

    mine, held = gate(0)
    reset = sigmoid(mine + held)
    mine, held = gate(2)
    candidate = jnp.tanh(mine + reset * held)
    mine, held = gate(1)
    update = sigmoid(mine + held)
    out_ref[...] = (1.0 - update) * candidate + update * memory_ref[...]


def on_device(
    features,
    memory,
    tile_values,
    tile_rows,
    tile_cols,
    tile_count,
    conv_weight,
    conv_bias,
    input_weight,
    input_bias,
    hidden_weight,
    hidden_bias,
):
    own_rows, width = features.shape
    n_row, n_col = lax.axis_size("row"), lax.axis_size("col")
    slots, size = tile_values.shape[2], tile_values.shape[3]
    dst_rows, src_rows = own_rows * n_row, own_rows * n_col
    col_blocks = src_rows // size
    place = jnp.stack([lax.axis_index("row"), lax.axis_index("col")]).astype(jnp.int32)

    pair = [(i, i ^ 1) for i in range(n_col)]
    order = ring_order(n_col // 2)
    ring = [
        (2 * order[at - 1] + odd, 2 * order[at] + odd) for at in range(n_col // 2) for odd in range(2)
    ]

    def tie(*values):
        return lax.optimization_barrier(values)

    def move(block, to):
        return lax.ppermute(block, "col", to)

    def around(hops):
        return [
            (2 * order[at - hops] + odd, 2 * order[at] + odd) for at in range(n_col // 2) for odd in range(2)
        ]

    riding = [features, move(features, ring)]
    paired = [move(features, pair)]
    dense, degree = pl.pallas_call(
        functools.partial(build_kernel, own_rows, n_row, n_col),
        out_shape=(
            jax.ShapeDtypeStruct((dst_rows, src_rows), jnp.bfloat16),
            jax.ShapeDtypeStruct((col_blocks, size), jnp.float32),
        ),
        in_specs=[smem()] * 2 + [pl.BlockSpec(memory_space=pltpu.HBM)] * 3,
        out_specs=(vmem(), vmem()),
        scratch_shapes=[
            pltpu.VMEM((col_blocks, 8, size), jnp.float32),
            pltpu.VMEM((slots, size, size), jnp.bfloat16),
            pltpu.SMEM(tile_rows.shape, jnp.int32),
            pltpu.SMEM(tile_cols.shape, jnp.int32),
            pltpu.SemaphoreType.DMA((2 + BUILD_STEPS,)),
        ],
        compiler_params=params(2 * slots * size * size + 2 * dst_rows * src_rows),
        cost_estimate=cost(0, 2 * slots * size * size + 2 * dst_rows * src_rows),
        name="build",
    )(place, tile_count.reshape(1), *[pltpu.with_memory_space_constraint(x, pltpu.HBM) for x in (tile_rows, tile_cols, tile_values)])

    added = [move(degree, around(hops)) for hops in range(1, n_col // 2)]
    riding[1], degree = tie(riding[1], degree)
    riding.append(move(riding[1], ring))
    block, paired[0], memory = tie(riding[1], paired[0], memory)
    paired.append(move(block, pair))
    gates = (
        jnp.dot(memory.astype(jnp.bfloat16), hidden_weight, preferred_element_type=jnp.float32) + hidden_bias
    )
    gates, *added = tie(gates, *added)
    degree = degree + functools.reduce(lambda x, y: x + y, added)
    added = move(degree, pair)
    for step in range(2, n_col // 2 - 1):
        if step == 2:
            riding[2], degree = tie(riding[2], degree + added)
        block = riding[step]
        riding.append(move(block, ring))
        block, paired[-1] = tie(block, paired[-1])
        paired.append(move(block, pair))
    half = own_rows // 2
    upper = riding[-1][:half]
    paired[-1], after = tie(paired[-1], upper)
    last_pair = (move(upper, pair), move(paired[-1][half:], ring))
    scale = pl.pallas_call(
        functools.partial(scale_kernel, own_rows, n_col),
        out_shape=jax.ShapeDtypeStruct((src_rows, size), jnp.float32),
        in_specs=[smem(), vmem()],
        out_specs=vmem(),
        compiler_params=params(4 * src_rows * size),
        cost_estimate=cost(0, 4 * src_rows * size),
        name="scale",
    )(place, degree)
    blocks = [block for both in zip(riding, paired) for block in both] + [riding[-1], *last_pair]

    def product(begin, count, blocks, running, last):
        depth = count * own_rows
        whole = pl.BlockSpec((dst_rows, width), lambda i: (0, 0))
        part = pl.BlockSpec((dst_rows // 2, width), lambda i: (0, 0))
        return pl.pallas_call(
            functools.partial(product_kernel, len(blocks), running is None, last),
            grid=(1,),
            out_shape=(
                jax.ShapeDtypeStruct((dst_rows // 2, width), jnp.bfloat16),
                jax.ShapeDtypeStruct((dst_rows // 2, width), jnp.float32),
            )
            if last
            else jax.ShapeDtypeStruct((dst_rows, width), jnp.float32),
            in_specs=[
                pl.BlockSpec((dst_rows, depth), lambda i: (0, begin // count)),
                pl.BlockSpec((depth, size), lambda i: (begin // count, 0)),
            ]
            + [pl.BlockSpec(block.shape, lambda i: (0, 0)) for block in blocks]
            + ([] if running is None else [whole]),
            out_specs=(part, part) if last else whole,
            scratch_shapes=[pltpu.VMEM((depth, width), jnp.bfloat16)],
            compiler_params=params(2 * dst_rows * depth + 4 * depth * width + 4 * depth * size + 8 * dst_rows * width),
            cost_estimate=cost(2 * dst_rows * depth * width, 2 * dst_rows * depth + 6 * dst_rows * width),
            name="product",
        )(dense, scale, *blocks, *([] if running is None else [running]))

    running = None
    many = n_col - 2 if n_col <= 8 else 6
    for begin in range(0, n_col - 2, many):
        running = product(begin, many, blocks[begin : begin + many], running, False)
    sent, kept = product(n_col - 2, 2, blocks[n_col - 2 :], running, True)
    terms = [kept]
    bit = 1
    while True:
        terms.append(lax.ppermute(sent, "row", [(i, i ^ bit) for i in range(n_row)]))
        bit *= 2
        if bit == n_row:
            break
        held = own_rows * n_row // bit
        sent = functools.reduce(
            lambda x, y: x + y,
            [term[term.shape[0] - held : term.shape[0] - held // 2].astype(jnp.float32) for term in terms],
        ).astype(jnp.bfloat16)

    def own_block(term):
        at = term.shape[0] // own_rows - 1
        return pl.BlockSpec((own_rows, width), lambda i: (at, 0))

    def entire(array):
        return pl.BlockSpec(array.shape, lambda i: (0, 0))

    operands = (
        conv_weight,
        conv_bias.reshape(1, width),
        input_weight,
        input_bias.reshape(1, 3 * width),
        gates,
        memory,
    )
    return pl.pallas_call(
        tail_kernel,
        grid=(1,),
        out_shape=jax.ShapeDtypeStruct((own_rows, width), jnp.float32),
        in_specs=[entire(array) for array in operands] + [own_block(term) for term in terms],
        out_specs=pl.BlockSpec((own_rows, width), lambda i: (0, 0)),
        compiler_params=params(8 * width * width + 40 * own_rows * width),
        cost_estimate=cost(8 * own_rows * width * width, 8 * width * width + 20 * own_rows * width),
        name="tail",
    )(*operands, *terms)


def solution(mesh):
    placed = (
        P(("row", "col"), None),
        P(("col", "row"), None),
        P("row", "col", None, None, None),
        P("row", "col", None),
        P("row", "col", None),
        P("row", "col"),
        P(),
        P(),
        P(),
        P(),
        P(),
        P(),
    )
    return jax.shard_map(
        on_device, mesh=mesh, in_specs=placed, out_specs=P(("col", "row"), None), check_vma=False
    )
```

```python
import functools

import jax
import jax.numpy as jnp
from jax import lax
from jax.experimental import pallas as pl
from jax.experimental.pallas import tpu as pltpu
from jax.sharding import PartitionSpec as P

norm_epsilon = 1e-06
MIB = 1 << 20
LANES = 128
BUILD_STEPS = 4


def vmem():
    return pl.BlockSpec(memory_space=pltpu.VMEM)


def smem():
    return pl.BlockSpec(memory_space=pltpu.SMEM)


def params(size):
    return pltpu.CompilerParams(vmem_limit_bytes=size + size // 4 + 4 * MIB)


def cost(flops, bytes_accessed):
    return pl.CostEstimate(flops=flops, bytes_accessed=bytes_accessed, transcendentals=0)


def ring_order(count):
    return [0, *range(1, count, 2), *reversed(range(2, count, 2))]


def ring_place(device, count):
    half = lax.shift_right_logical(device + 1, 1)
    return jnp.where((device & 1) == 1, half, lax.rem(count - half, count))


def ring_device(place, count):
    return jnp.where(place <= count // 2, jnp.maximum(2 * place - 1, 0), 2 * (count - place))


def arrival_place(owner, me, n):
    count = n // 2
    mine = ring_place(lax.shift_right_logical(me, 1), count)
    theirs = ring_place(lax.shift_right_logical(owner, 1), count)
    return 2 * lax.rem(mine - theirs + count, count) + ((owner ^ me) & 1)


def arrival_owner(place, me, n):
    count = n // 2
    mine = ring_place(lax.shift_right_logical(me, 1), count)
    back = lax.rem(mine - place // 2 + count, count)
    return 2 * ring_device(back, count) + ((me + place) & 1)


def halving_place(owner, me, n):
    away, place = owner ^ me, n - 1
    for bit in range(n.bit_length() - 1):
        place = place - (lax.shift_right_logical(away, bit) & 1) * (n >> (bit + 1))
    return place


def build_kernel(own_rows, n_row, n_col, place_ref, count_ref, rows_any, cols_any, tiles_any, dense_ref, degree_ref, *scratch):
    acc_ref, tiles_ref, rows_ref, cols_ref, sems = scratch
    row_me, col_me = place_ref[0], place_ref[1]
    slots, size = tiles_ref.shape[:2]
    per = own_rows // size
    some = slots // BUILD_STEPS
    small = [
        pltpu.make_async_copy(rows_any, rows_ref, sems.at[0]),
        pltpu.make_async_copy(cols_any, cols_ref, sems.at[1]),
    ]
    large = [
        pltpu.make_async_copy(
            tiles_any.at[0, 0, pl.ds(step * some, some)], tiles_ref.at[pl.ds(step * some, some)], sems.at[2 + step]
        )
        for step in range(BUILD_STEPS)
    ]
    for copy in small + large:
        copy.start()
    dense_ref[...] = jnp.zeros_like(dense_ref)
    acc_ref[...] = jnp.zeros_like(acc_ref)

    def one(slot, carry):
        a, b = rows_ref[0, 0, slot], cols_ref[0, 0, slot]
        row = (halving_place(lax.div(a, per), row_me, n_row) * per + lax.rem(a, per)) * size
        col = (arrival_place(lax.div(b, per), col_me, n_col) * per + lax.rem(b, per)) * size
        tile = tiles_ref[slot]
        dense_ref[pl.ds(pl.multiple_of(row, size), size), pl.ds(pl.multiple_of(col, size), size)] = tile
        wide = tile.astype(jnp.float32).reshape(size // 8, 8, size)
        acc_ref[b] += jnp.sum(wide, axis=0)
        return carry

    for copy in small:
        copy.wait()
    for step, copy in enumerate(large):
        copy.wait()
        lax.fori_loop(step * some, jnp.minimum(count_ref[0], (step + 1) * some), one, 0)
    degree_ref[...] = jnp.sum(acc_ref[...], axis=1)


def scale_kernel(own_rows, n_col, place_ref, degree_ref, scale_ref):
    col_me = place_ref[1]
    size = degree_ref.shape[1]
    per = own_rows // size
    for place in range(n_col):
        owner = arrival_owner(place, col_me, n_col)
        for half in range(per):
            line = lax.rsqrt(1.0 + degree_ref[pl.ds(owner * per + half, 1), :])
            spread = jnp.broadcast_to(line, (size, size)).T
            scale_ref[pl.ds((place * per + half) * size, size), :] = spread


def product_kernel(n_blocks, first, last, *refs):
    dense_ref, scale_ref = refs[:2]
    block_refs = refs[2 : 2 + n_blocks]
    sum_refs = () if first else refs[2 + n_blocks : 3 + n_blocks]
    panel_ref = refs[-1]
    out_refs = refs[2 + n_blocks + len(sum_refs) : -1]
    own_rows, width = block_refs[0].shape
    dst_rows = dense_ref.shape[0]
    for place, block in enumerate(block_refs):
        rows = slice(place * own_rows, (place + 1) * own_rows)
        scale = scale_ref[rows, :]
        for left in range(0, width, LANES):
            cut = slice(left, left + LANES)
            panel_ref[rows, cut] = (block[:, cut].astype(jnp.float32) * scale).astype(jnp.bfloat16)
    for top in range(0, dst_rows, own_rows):
        rows = slice(top, top + own_rows)
        value = jnp.dot(dense_ref[rows, :], panel_ref[...], preferred_element_type=jnp.float32)
        if not first:
            value = value + sum_refs[0][rows, :]
        if not last:
            out_refs[0][rows, :] = value
        elif top < dst_rows // 2:
            out_refs[0][rows, :] = value.astype(jnp.bfloat16)
        else:
            out_refs[1][top - dst_rows // 2 : top - dst_rows // 2 + own_rows, :] = value


def sigmoid(x):
    return 0.5 * jnp.tanh(0.5 * x) + 0.5


def tail_kernel(*refs):
    (conv_ref, conv_bias_ref, input_ref, input_bias_ref, gates_ref, memory_ref), sums = refs[:6], refs[6:-1]
    out_ref = refs[-1]
    width = memory_ref.shape[1]

    owned = functools.reduce(lambda x, y: x + y, [term[...].astype(jnp.float32) for term in sums])
    spread = jnp.mean(owned * owned, axis=1, keepdims=True) + norm_epsilon
    normed = (owned / jnp.sqrt(spread)).astype(jnp.bfloat16)
    message = jnp.maximum(
        jnp.dot(normed, conv_ref[...], preferred_element_type=jnp.float32) + conv_bias_ref[...], 0.0
    ).astype(jnp.bfloat16)

    def gate(index):
        cut = slice(index * width, (index + 1) * width)
        dots = jnp.dot(message, input_ref[:, cut], preferred_element_type=jnp.float32)
        return dots + input_bias_ref[:, cut], gates_ref[:, cut]

    mine, held = gate(0)
    reset = sigmoid(mine + held)
    mine, held = gate(2)
    candidate = jnp.tanh(mine + reset * held)
    mine, held = gate(1)
    update = sigmoid(mine + held)
    out_ref[...] = (1.0 - update) * candidate + update * memory_ref[...]


def on_device(
    features,
    memory,
    tile_values,
    tile_rows,
    tile_cols,
    tile_count,
    conv_weight,
    conv_bias,
    input_weight,
    input_bias,
    hidden_weight,
    hidden_bias,
):
    own_rows, width = features.shape
    n_row, n_col = lax.axis_size("row"), lax.axis_size("col")
    slots, size = tile_values.shape[2], tile_values.shape[3]
    dst_rows, src_rows = own_rows * n_row, own_rows * n_col
    col_blocks = src_rows // size
    place = jnp.stack([lax.axis_index("row"), lax.axis_index("col")]).astype(jnp.int32)

    pair = [(i, i ^ 1) for i in range(n_col)]
    order = ring_order(n_col // 2)
    ring = [
        (2 * order[at - 1] + odd, 2 * order[at] + odd) for at in range(n_col // 2) for odd in range(2)
    ]

    def tie(*values):
        return lax.optimization_barrier(values)

    def move(block, to):
        return lax.ppermute(block, "col", to)

    def around(hops):
        return [
            (2 * order[at - hops] + odd, 2 * order[at] + odd) for at in range(n_col // 2) for odd in range(2)
        ]

    riding = [features, move(features, ring)]
    paired = [move(features, pair)]
    dense, degree = pl.pallas_call(
        functools.partial(build_kernel, own_rows, n_row, n_col),
        out_shape=(
            jax.ShapeDtypeStruct((dst_rows, src_rows), jnp.bfloat16),
            jax.ShapeDtypeStruct((col_blocks, size), jnp.float32),
        ),
        in_specs=[smem()] * 2 + [pl.BlockSpec(memory_space=pltpu.HBM)] * 3,
        out_specs=(vmem(), vmem()),
        scratch_shapes=[
            pltpu.VMEM((col_blocks, 8, size), jnp.float32),
            pltpu.VMEM((slots, size, size), jnp.bfloat16),
            pltpu.SMEM(tile_rows.shape, jnp.int32),
            pltpu.SMEM(tile_cols.shape, jnp.int32),
            pltpu.SemaphoreType.DMA((2 + BUILD_STEPS,)),
        ],
        compiler_params=params(2 * slots * size * size + 2 * dst_rows * src_rows),
        cost_estimate=cost(0, 2 * slots * size * size + 2 * dst_rows * src_rows),
        name="build",
    )(place, tile_count.reshape(1), *[pltpu.with_memory_space_constraint(x, pltpu.HBM) for x in (tile_rows, tile_cols, tile_values)])

    degree = jnp.sum(
        lax.all_to_all(jnp.broadcast_to(degree, (n_col, col_blocks, size)), "col", 0, 0, tiled=True), axis=0
    )
    riding[1], degree = tie(riding[1], degree)
    for step in range(1, n_col // 2):
        block = riding[step]
        if step + 1 < n_col // 2:
            riding.append(move(block, ring))
            block, paired[-1], memory = tie(block, paired[-1], memory)
            if step == 1:
                gates = (
                    jnp.dot(memory.astype(jnp.bfloat16), hidden_weight, preferred_element_type=jnp.float32)
                    + hidden_bias
                )
        paired.append(move(block, pair))
    scale = pl.pallas_call(
        functools.partial(scale_kernel, own_rows, n_col),
        out_shape=jax.ShapeDtypeStruct((src_rows, size), jnp.float32),
        in_specs=[smem(), vmem()],
        out_specs=vmem(),
        compiler_params=params(4 * src_rows * size),
        cost_estimate=cost(0, 4 * src_rows * size),
        name="scale",
    )(place, degree)
    blocks = [block for both in zip(riding, paired) for block in both]

    def product(begin, count, running):
        last = running is not None
        depth = count * own_rows
        full = pl.BlockSpec((dst_rows, width), lambda i: (0, 0))
        half = pl.BlockSpec((dst_rows // 2, width), lambda i: (0, 0))
        return pl.pallas_call(
            functools.partial(product_kernel, count, not last, last),
            grid=(1,),
            out_shape=(
                jax.ShapeDtypeStruct((dst_rows // 2, width), jnp.bfloat16),
                jax.ShapeDtypeStruct((dst_rows // 2, width), jnp.float32),
            )
            if last
            else jax.ShapeDtypeStruct((dst_rows, width), jnp.float32),
            in_specs=[
                pl.BlockSpec((dst_rows, depth), lambda i: (0, begin // count)),
                pl.BlockSpec((depth, size), lambda i: (begin // count, 0)),
            ]
            + [pl.BlockSpec((own_rows, width), lambda i: (0, 0))] * count
            + [full] * last,
            out_specs=(half, half) if last else full,
            scratch_shapes=[pltpu.VMEM((depth, width), jnp.bfloat16)],
            compiler_params=params(2 * dst_rows * depth + 4 * depth * width + 4 * depth * size + 8 * dst_rows * width),
            cost_estimate=cost(2 * dst_rows * depth * width, 2 * dst_rows * depth + 6 * dst_rows * width),
            name="product",
        )(dense, scale, *blocks[begin : begin + count], *([running] if last else []))

    most = n_col - n_col // 4
    sent, kept = product(most, n_col // 4, product(0, most, None))
    terms = [kept]
    bit = 1
    while True:
        terms.append(lax.ppermute(sent, "row", [(i, i ^ bit) for i in range(n_row)]))
        bit *= 2
        if bit == n_row:
            break
        held = own_rows * n_row // bit
        sent = functools.reduce(
            lambda x, y: x + y,
            [term[term.shape[0] - held : term.shape[0] - held // 2].astype(jnp.float32) for term in terms],
        ).astype(jnp.bfloat16)

    def own_block(term):
        at = term.shape[0] // own_rows - 1
        return pl.BlockSpec((own_rows, width), lambda i: (at, 0))

    def entire(array):
        return pl.BlockSpec(array.shape, lambda i: (0, 0))

    operands = (
        conv_weight,
        conv_bias.reshape(1, width),
        input_weight,
        input_bias.reshape(1, 3 * width),
        gates,
        memory,
    )
    return pl.pallas_call(
        tail_kernel,
        grid=(1,),
        out_shape=jax.ShapeDtypeStruct((own_rows, width), jnp.float32),
        in_specs=[entire(array) for array in operands] + [own_block(term) for term in terms],
        out_specs=pl.BlockSpec((own_rows, width), lambda i: (0, 0)),
        compiler_params=params(8 * width * width + 40 * own_rows * width),
        cost_estimate=cost(8 * own_rows * width * width, 8 * width * width + 20 * own_rows * width),
        name="tail",
    )(*operands, *terms)


def solution(mesh):
    placed = (
        P(("row", "col"), None),
        P(("col", "row"), None),
        P("row", "col", None, None, None),
        P("row", "col", None),
        P("row", "col", None),
        P("row", "col"),
        P(),
        P(),
        P(),
        P(),
        P(),
        P(),
    )
    return jax.shard_map(
        on_device, mesh=mesh, in_specs=placed, out_specs=P(("col", "row"), None), check_vma=False
    )
```

```python
import functools

import jax
import jax.numpy as jnp
from jax import lax
from jax.experimental import pallas as pl
from jax.experimental.pallas import tpu as pltpu
from jax.sharding import PartitionSpec as P

norm_epsilon = 1e-06
MIB = 1 << 20
LANES = 128
BUILD_STEPS = 4
TAIL_STEPS = 2


def vmem():
    return pl.BlockSpec(memory_space=pltpu.VMEM)


def smem():
    return pl.BlockSpec(memory_space=pltpu.SMEM)


def params(size):
    return pltpu.CompilerParams(vmem_limit_bytes=size + size // 4 + 4 * MIB)


def cost(flops, bytes_accessed):
    return pl.CostEstimate(flops=flops, bytes_accessed=bytes_accessed, transcendentals=0)


def ring_order(count):
    return [0, *range(1, count, 2), *reversed(range(2, count, 2))]


def ring_place(device, count):
    half = lax.shift_right_logical(device + 1, 1)
    return jnp.where((device & 1) == 1, half, lax.rem(count - half, count))


def ring_device(place, count):
    return jnp.where(place <= count // 2, jnp.maximum(2 * place - 1, 0), 2 * (count - place))


def arrival_place(owner, me, n):
    count = n // 2
    mine = ring_place(lax.shift_right_logical(me, 1), count)
    theirs = ring_place(lax.shift_right_logical(owner, 1), count)
    return 2 * lax.rem(mine - theirs + count, count) + ((owner ^ me) & 1)


def arrival_owner(place, me, n):
    count = n // 2
    mine = ring_place(lax.shift_right_logical(me, 1), count)
    back = lax.rem(mine - place // 2 + count, count)
    return 2 * ring_device(back, count) + ((me + place) & 1)


def part_place(owner, me, n):
    return n - 1 - (owner ^ me)


def copy_kernel(from_ref, to_ref, sem):
    copy = pltpu.make_async_copy(from_ref, to_ref, sem)
    copy.start()
    copy.wait()


def build_kernel(own_rows, n_row, n_col, place_ref, count_ref, rows_any, cols_any, tiles_any, dense_ref, degree_ref, *scratch):
    acc_ref, tiles_ref, rows_ref, cols_ref, sems = scratch
    row_me, col_me = place_ref[0], place_ref[1]
    slots, size = tiles_ref.shape[:2]
    per = own_rows // size
    some = slots // BUILD_STEPS
    small = [
        pltpu.make_async_copy(rows_any, rows_ref, sems.at[0]),
        pltpu.make_async_copy(cols_any, cols_ref, sems.at[1]),
    ]
    large = [
        pltpu.make_async_copy(
            tiles_any.at[0, 0, pl.ds(step * some, some)], tiles_ref.at[pl.ds(step * some, some)], sems.at[2 + step]
        )
        for step in range(BUILD_STEPS)
    ]
    for copy in small + large:
        copy.start()
    dense_ref[...] = jnp.zeros_like(dense_ref)
    acc_ref[...] = jnp.zeros_like(acc_ref)

    def one(slot, carry):
        a, b = rows_ref[0, 0, slot], cols_ref[0, 0, slot]
        row = (part_place(lax.div(a, per), row_me, n_row) * per + lax.rem(a, per)) * size
        col = (arrival_place(lax.div(b, per), col_me, n_col) * per + lax.rem(b, per)) * size
        tile = tiles_ref[slot]
        dense_ref[pl.ds(pl.multiple_of(row, size), size), pl.ds(pl.multiple_of(col, size), size)] = tile
        wide = tile.astype(jnp.float32).reshape(size // 8, 8, size)
        acc_ref[b] += jnp.sum(wide, axis=0)
        return carry

    for copy in small:
        copy.wait()
    for step, copy in enumerate(large):
        copy.wait()
        lax.fori_loop(step * some, jnp.minimum(count_ref[0], (step + 1) * some), one, 0)
    degree_ref[...] = jnp.sum(acc_ref[...], axis=1)


def scale_kernel(own_rows, n_col, place_ref, degree_ref, scale_ref):
    col_me = place_ref[1]
    size = degree_ref.shape[1]
    per = own_rows // size
    for place in range(n_col):
        owner = arrival_owner(place, col_me, n_col)
        for half in range(per):
            line = lax.rsqrt(1.0 + degree_ref[pl.ds(owner * per + half, 1), :])
            spread = jnp.broadcast_to(line, (size, size)).T
            scale_ref[pl.ds((place * per + half) * size, size), :] = spread


def product_kernel(n_blocks, first, *refs):
    dense_ref, scale_ref = refs[:2]
    block_refs = refs[2 : 2 + n_blocks]
    sum_refs = () if first else refs[2 + n_blocks : 3 + n_blocks]
    panel_ref = refs[-1]
    out_refs = refs[2 + n_blocks + len(sum_refs) : -1]
    own_rows, width = block_refs[0].shape
    for place, block in enumerate(block_refs):
        rows = slice(place * own_rows, (place + 1) * own_rows)
        scale = scale_ref[rows, :]
        for left in range(0, width, LANES):
            cut = slice(left, left + LANES)
            panel_ref[rows, cut] = (block[:, cut].astype(jnp.float32) * scale).astype(jnp.bfloat16)
    for place in range(dense_ref.shape[0] // own_rows):
        rows = slice(place * own_rows, (place + 1) * own_rows)
        value = jnp.dot(dense_ref[rows, :], panel_ref[...], preferred_element_type=jnp.float32)
        if not first:
            value = value + sum_refs[0][rows, :]
        if len(out_refs) == 1:
            out_refs[0][rows, :] = value
        else:
            out_refs[place][...] = value.astype(out_refs[place].dtype)


def sigmoid(x):
    return 0.5 * jnp.tanh(0.5 * x) + 0.5


def tail_kernel(*refs):
    (conv_ref, conv_bias_ref, input_ref, input_bias_ref, gates_ref, memory_ref), sums = refs[:6], refs[6:-1]
    out_ref = refs[-1]
    height, width = memory_ref.shape
    for top in range(0, height, height // TAIL_STEPS):
        rows = slice(top, top + height // TAIL_STEPS)
        owned = functools.reduce(lambda x, y: x + y, [term[rows, :].astype(jnp.float32) for term in sums])
        spread = jnp.mean(owned * owned, axis=1, keepdims=True) + norm_epsilon
        normed = (owned * lax.rsqrt(spread)).astype(jnp.bfloat16)
        message = jnp.maximum(
            jnp.dot(normed, conv_ref[...], preferred_element_type=jnp.float32) + conv_bias_ref[...], 0.0
        ).astype(jnp.bfloat16)

        def gate(index):
            cut = slice(index * width, (index + 1) * width)
            dots = jnp.dot(message, input_ref[:, cut], preferred_element_type=jnp.float32)
            return dots + input_bias_ref[:, cut], gates_ref[rows, cut]

        mine, held = gate(0)
        reset = sigmoid(mine + held)
        mine, held = gate(2)
        candidate = jnp.tanh(mine + reset * held)
        mine, held = gate(1)
        update = sigmoid(mine + held)
        out_ref[rows, :] = (1.0 - update) * candidate + update * memory_ref[rows, :]


def on_device(
    features,
    memory,
    tile_values,
    tile_rows,
    tile_cols,
    tile_count,
    conv_weight,
    conv_bias,
    input_weight,
    input_bias,
    hidden_weight,
    hidden_bias,
):
    own_rows, width = features.shape
    n_row, n_col = lax.axis_size("row"), lax.axis_size("col")
    slots, size = tile_values.shape[2], tile_values.shape[3]
    dst_rows, src_rows = own_rows * n_row, own_rows * n_col
    col_blocks = src_rows // size
    place = jnp.stack([lax.axis_index("row"), lax.axis_index("col")]).astype(jnp.int32)

    pair = [(i, i ^ 1) for i in range(n_col)]
    order = ring_order(n_col // 2)
    ring = [
        (2 * order[at - 1] + odd, 2 * order[at] + odd) for at in range(n_col // 2) for odd in range(2)
    ]
    features = pl.pallas_call(
        copy_kernel,
        out_shape=jax.ShapeDtypeStruct(features.shape, features.dtype),
        in_specs=[pl.BlockSpec(memory_space=pltpu.HBM)],
        out_specs=vmem(),
        scratch_shapes=[pltpu.SemaphoreType.DMA(())],
        cost_estimate=cost(0, 4 * own_rows * width),
        name="load",
    )(pltpu.with_memory_space_constraint(features, pltpu.HBM))
    riding = [features]
    paired = []

    def tie(*values):
        return lax.optimization_barrier(values)

    def ride():
        if len(riding) < n_col // 2:
            riding.append(lax.ppermute(riding[-1], "col", ring))

    def swap(*others):
        at = len(paired)
        block = riding[at]
        if paired and at + 1 < n_col // 2:
            block, paired[-1], *others = tie(block, paired[-1], *others)
        paired.append(lax.ppermute(block, "col", pair))
        return others

    ride()
    swap()
    dense, degree = pl.pallas_call(
        functools.partial(build_kernel, own_rows, n_row, n_col),
        out_shape=(
            jax.ShapeDtypeStruct((dst_rows, src_rows), jnp.bfloat16),
            jax.ShapeDtypeStruct((col_blocks, size), jnp.float32),
        ),
        in_specs=[smem()] * 2 + [pl.BlockSpec(memory_space=pltpu.HBM)] * 3,
        out_specs=(vmem(), vmem()),
        scratch_shapes=[
            pltpu.VMEM((col_blocks, 8, size), jnp.float32),
            pltpu.VMEM((slots, size, size), jnp.bfloat16),
            pltpu.SMEM(tile_rows.shape, jnp.int32),
            pltpu.SMEM(tile_cols.shape, jnp.int32),
            pltpu.SemaphoreType.DMA((2 + BUILD_STEPS,)),
        ],
        compiler_params=params(2 * slots * size * size + 2 * dst_rows * src_rows),
        cost_estimate=cost(0, 2 * slots * size * size + 2 * dst_rows * src_rows),
        name="build",
    )(place, tile_count.reshape(1), *[pltpu.with_memory_space_constraint(x, pltpu.HBM) for x in (tile_rows, tile_cols, tile_values)])

    hop = 1
    while hop < n_col // 2:
        around = [
            (2 * order[at - hop] + odd, 2 * order[at] + odd) for at in range(n_col // 2) for odd in range(2)
        ]
        added = lax.ppermute(degree, "col", around)
        riding[-1], added = tie(riding[-1], added)
        ride()
        degree, memory = swap(degree + added, memory)
        hop *= 2
    riding[-1], added = tie(riding[-1], lax.ppermute(degree, "col", pair))
    degree = degree + added
    gates = (
        jnp.dot(memory.astype(jnp.bfloat16), hidden_weight, preferred_element_type=jnp.float32) + hidden_bias
    )
    scale = pl.pallas_call(
        functools.partial(scale_kernel, own_rows, n_col),
        out_shape=jax.ShapeDtypeStruct((src_rows, size), jnp.float32),
        in_specs=[smem(), vmem()],
        out_specs=vmem(),
        compiler_params=params(4 * src_rows * size),
        cost_estimate=cost(0, 4 * src_rows * size),
        name="scale",
    )(place, degree)
    while len(paired) < n_col // 2:
        ride()
        swap()
    blocks = [block for both in zip(riding, paired) for block in both]

    def product(begin, count, running, half=None):
        depth = count * own_rows
        at = 0 if half is None else half
        rows = dst_rows if half is None else dst_rows // 2
        tall = pl.BlockSpec((rows, width), lambda i: (at, 0))
        one = pl.BlockSpec((own_rows, width), lambda i: (0, 0))
        n_out = n_row // 2
        return pl.pallas_call(
            functools.partial(product_kernel, count, running is None),
            grid=(1,),
            out_shape=jax.ShapeDtypeStruct((dst_rows, width), jnp.float32)
            if half is None
            else tuple(
                jax.ShapeDtypeStruct((own_rows, width), jnp.float32 if part % 2 else jnp.bfloat16)
                for part in range(n_out)
            ),
            in_specs=[
                pl.BlockSpec((rows, depth), lambda i: (at, begin // count)),
                pl.BlockSpec((depth, size), lambda i: (begin // count, 0)),
            ]
            + [one] * count
            + ([] if running is None else [tall]),
            out_specs=tall if half is None else (one,) * n_out,
            scratch_shapes=[pltpu.VMEM((depth, width), jnp.bfloat16)],
            compiler_params=params(2 * rows * depth + 4 * depth * width + 4 * depth * size + 8 * rows * width),
            cost_estimate=cost(2 * rows * depth * width, 2 * rows * depth + 6 * rows * width),
            name="product",
        )(dense, scale, *blocks[begin : begin + count], *([] if running is None else [running]))

    running = None
    many = 6
    for begin in range(0, n_col - 2, many):
        running = product(begin, many, running)
    running = product(n_col - 2, 1, running)

    upper, lower = product(n_col - 1, 1, running, 0), product(n_col - 1, 1, running, 1)
    sums = {n_row - 1 - at: [part] for at, part in enumerate((*upper, *lower))}
    total = None
    for part in range(n_row - 1, 0, -1):
        bit = part & -part
        if part == n_row // 2 - 1:
            sums[part][0], _ = tie(sums[part][0], total)
        total = functools.reduce(lambda x, y: x.astype(jnp.float32) + y.astype(jnp.float32), sums[part])
        total = total.astype(jnp.bfloat16)
        sums[part ^ bit].append(lax.ppermute(total, "row", [(i, i ^ bit) for i in range(n_row)]))
    terms = sums[0]

    def own_block(term):
        at = term.shape[0] // own_rows - 1
        return pl.BlockSpec((own_rows, width), lambda i: (at, 0))

    def entire(array):
        return pl.BlockSpec(array.shape, lambda i: (0, 0))

    operands = (
        conv_weight,
        conv_bias.reshape(1, width),
        input_weight,
        input_bias.reshape(1, 3 * width),
        gates,
        memory,
    )
    return pl.pallas_call(
        tail_kernel,
        grid=(1,),
        out_shape=jax.ShapeDtypeStruct((own_rows, width), jnp.float32),
        in_specs=[entire(array) for array in operands] + [own_block(term) for term in terms],
        out_specs=pl.BlockSpec((own_rows, width), lambda i: (0, 0)),
        compiler_params=params(8 * width * width + 40 * own_rows * width),
        cost_estimate=cost(8 * own_rows * width * width, 8 * width * width + 20 * own_rows * width),
        name="tail",
    )(*operands, *terms)


def solution(mesh):
    placed = (
        P(("row", "col"), None),
        P(("col", "row"), None),
        P("row", "col", None, None, None),
        P("row", "col", None),
        P("row", "col", None),
        P("row", "col"),
        P(),
        P(),
        P(),
        P(),
        P(),
        P(),
    )
    return jax.shard_map(
        on_device, mesh=mesh, in_specs=placed, out_specs=P(("col", "row"), None), check_vma=False
    )
```

```python
import functools

import jax
import jax.numpy as jnp
from jax import lax
from jax.experimental import pallas as pl
from jax.experimental.pallas import tpu as pltpu
from jax.sharding import PartitionSpec as P

norm_epsilon = 1e-06
MIB = 1 << 20
LANES = 128
BUILD_STEPS = 4
TAIL_STEPS = 1


def vmem():
    return pl.BlockSpec(memory_space=pltpu.VMEM)


def smem():
    return pl.BlockSpec(memory_space=pltpu.SMEM)


def params(size):
    return pltpu.CompilerParams(vmem_limit_bytes=size + size // 4 + 4 * MIB)


def cost(flops, bytes_accessed):
    return pl.CostEstimate(flops=flops, bytes_accessed=bytes_accessed, transcendentals=0)


def cycle_place(col, n):
    level = lax.shift_right_logical(col, 1)
    return jnp.where((col & 1) == 0, level, n - 1 - level)


def cycle_column(place, n):
    return jnp.where(place < n // 2, 2 * place, 2 * (n - 1 - place) + 1)


def arrival_place(owner, me, n):
    back = lax.rem(cycle_place(me, n) - cycle_place(owner, n) + n, n)
    return jnp.where(back <= n // 2, jnp.maximum(2 * back - 1, 0), 2 * (n - back))


def arrival_owner(place, me, n):
    back = (place + 1) // 2 if place % 2 else (n - place // 2) % n
    return cycle_column(lax.rem(cycle_place(me, n) - back + n, n), n)


def part_place(owner, me, n):
    return n - 1 - (owner ^ me)


def build_kernel(own_rows, n_row, n_col, place_ref, count_ref, rows_any, cols_any, tiles_any, dense_ref, degree_ref, *scratch):
    acc_ref, tiles_ref, rows_ref, cols_ref, sems = scratch
    row_me, col_me = place_ref[0], place_ref[1]
    slots, size = tiles_ref.shape[:2]
    per = own_rows // size
    some = slots // BUILD_STEPS
    small = [
        pltpu.make_async_copy(rows_any, rows_ref, sems.at[0]),
        pltpu.make_async_copy(cols_any, cols_ref, sems.at[1]),
    ]
    large = [
        pltpu.make_async_copy(
            tiles_any.at[0, 0, pl.ds(step * some, some)], tiles_ref.at[pl.ds(step * some, some)], sems.at[2 + step]
        )
        for step in range(BUILD_STEPS)
    ]
    for copy in small + large:
        copy.start()
    dense_ref[...] = jnp.zeros_like(dense_ref)
    acc_ref[...] = jnp.zeros_like(acc_ref)

    def one(slot, carry):
        a, b = rows_ref[0, 0, slot], cols_ref[0, 0, slot]
        row = (part_place(lax.div(a, per), row_me, n_row) * per + lax.rem(a, per)) * size
        col = (arrival_place(lax.div(b, per), col_me, n_col) * per + lax.rem(b, per)) * size
        tile = tiles_ref[slot]
        dense_ref[pl.ds(pl.multiple_of(row, size), size), pl.ds(pl.multiple_of(col, size), size)] = tile
        wide = tile.astype(jnp.float32).reshape(size // 8, 8, size)
        acc_ref[b] += jnp.sum(wide, axis=0)
        return carry

    for copy in small:
        copy.wait()
    for step, copy in enumerate(large):
        copy.wait()
        lax.fori_loop(step * some, jnp.minimum(count_ref[0], (step + 1) * some), one, 0)
    degree_ref[...] = jnp.sum(acc_ref[...], axis=1)


def scale_kernel(own_rows, n_col, place_ref, degree_ref, scale_ref):
    col_me = place_ref[1]
    size = degree_ref.shape[1]
    per = own_rows // size
    for place in range(n_col):
        owner = arrival_owner(place, col_me, n_col)
        for half in range(per):
            line = lax.rsqrt(1.0 + degree_ref[pl.ds(owner * per + half, 1), :])
            spread = jnp.broadcast_to(line, (size, size)).T
            scale_ref[pl.ds((place * per + half) * size, size), :] = spread


def product_kernel(n_blocks, first, *refs):
    dense_ref, scale_ref = refs[:2]
    block_refs = refs[2 : 2 + n_blocks]
    sum_refs = () if first else refs[2 + n_blocks : 3 + n_blocks]
    panel_ref = refs[-1]
    out_refs = refs[2 + n_blocks + len(sum_refs) : -1]
    width = panel_ref.shape[1]
    own_rows = out_refs[0].shape[0] if len(out_refs) > 1 else block_refs[0].shape[0]
    end = 0
    for block in block_refs:
        rows = slice(end, end + block.shape[0])
        end = rows.stop
        scale = scale_ref[rows, :]
        for left in range(0, width, LANES):
            cut = slice(left, left + LANES)
            panel_ref[rows, cut] = (block[:, cut].astype(jnp.float32) * scale).astype(jnp.bfloat16)
    for place in range(dense_ref.shape[0] // own_rows):
        rows = slice(place * own_rows, (place + 1) * own_rows)
        value = jnp.dot(dense_ref[rows, :], panel_ref[...], preferred_element_type=jnp.float32)
        if not first:
            value = value + sum_refs[0][rows, :]
        if len(out_refs) == 1:
            out_refs[0][rows, :] = value
        else:
            out_refs[place][...] = value.astype(out_refs[place].dtype)


def sigmoid(x):
    return 0.5 * jnp.tanh(0.5 * x) + 0.5


def tail_kernel(*refs):
    (conv_ref, conv_bias_ref, input_ref, input_bias_ref, gates_ref, memory_ref), sums = refs[:6], refs[6:-1]
    out_ref = refs[-1]
    height, width = memory_ref.shape
    for top in range(0, height, height // TAIL_STEPS):
        rows = slice(top, top + height // TAIL_STEPS)
        owned = functools.reduce(lambda x, y: x + y, [term[rows, :].astype(jnp.float32) for term in sums])
        spread = jnp.mean(owned * owned, axis=1, keepdims=True) + norm_epsilon
        normed = (owned * lax.rsqrt(spread)).astype(jnp.bfloat16)
        message = jnp.maximum(
            jnp.dot(normed, conv_ref[...], preferred_element_type=jnp.float32) + conv_bias_ref[...], 0.0
        ).astype(jnp.bfloat16)

        def gate(index):
            cut = slice(index * width, (index + 1) * width)
            dots = jnp.dot(message, input_ref[:, cut], preferred_element_type=jnp.float32)
            return dots + input_bias_ref[:, cut], gates_ref[rows, cut]

        mine, held = gate(0)
        reset = sigmoid(mine + held)
        mine, held = gate(2)
        candidate = jnp.tanh(mine + reset * held)
        mine, held = gate(1)
        update = sigmoid(mine + held)
        out_ref[rows, :] = (1.0 - update) * candidate + update * memory_ref[rows, :]


def on_device(
    features,
    memory,
    tile_values,
    tile_rows,
    tile_cols,
    tile_count,
    conv_weight,
    conv_bias,
    input_weight,
    input_bias,
    hidden_weight,
    hidden_bias,
):
    own_rows, width = features.shape
    n_row, n_col = lax.axis_size("row"), lax.axis_size("col")
    slots, size = tile_values.shape[2], tile_values.shape[3]
    dst_rows, src_rows = own_rows * n_row, own_rows * n_col
    col_blocks = src_rows // size
    place = jnp.stack([lax.axis_index("row"), lax.axis_index("col")]).astype(jnp.int32)

    cycle = [*range(0, n_col, 2), *range(n_col - 1, 0, -2)]
    ahead = [(cycle[at - 1], cycle[at]) for at in range(n_col)]
    behind = [(to, at) for at, to in ahead]

    def tie(*values):
        return lax.optimization_barrier(values)

    def move(block, to):
        return lax.ppermute(block, "col", to)

    blocks = [features, move(features, ahead), move(features, behind)]
    dense, degree = pl.pallas_call(
        functools.partial(build_kernel, own_rows, n_row, n_col),
        out_shape=(
            jax.ShapeDtypeStruct((dst_rows, src_rows), jnp.bfloat16),
            jax.ShapeDtypeStruct((col_blocks, size), jnp.float32),
        ),
        in_specs=[smem()] * 2 + [pl.BlockSpec(memory_space=pltpu.HBM)] * 3,
        out_specs=(vmem(), vmem()),
        scratch_shapes=[
            pltpu.VMEM((col_blocks, 8, size), jnp.float32),
            pltpu.VMEM((slots, size, size), jnp.bfloat16),
            pltpu.SMEM(tile_rows.shape, jnp.int32),
            pltpu.SMEM(tile_cols.shape, jnp.int32),
            pltpu.SemaphoreType.DMA((2 + BUILD_STEPS,)),
        ],
        compiler_params=params(2 * slots * size * size + 2 * dst_rows * src_rows),
        cost_estimate=cost(0, 2 * slots * size * size + 2 * dst_rows * src_rows),
        name="build",
    )(place, tile_count.reshape(1), *[pltpu.with_memory_space_constraint(x, pltpu.HBM) for x in (tile_rows, tile_cols, tile_values)])

    added = [move(degree, [(i, i ^ (2 * hops)) for i in range(n_col)]) for hops in range(1, n_col // 2)]
    blocks[1], degree = tie(blocks[1], degree)
    blocks.append(move(blocks[1], ahead))
    blocks[2], memory = tie(blocks[2], memory)
    blocks.append(move(blocks[2], behind))
    gates = (
        jnp.dot(memory.astype(jnp.bfloat16), hidden_weight, preferred_element_type=jnp.float32) + hidden_bias
    )
    gates, *added = tie(gates, *added)
    degree = degree + functools.reduce(lambda x, y: x + y, added)
    added = move(degree, [(i, i ^ 1) for i in range(n_col)])
    blocks[3], degree = tie(blocks[3], degree + added)
    while len(blocks) < n_col - 1:
        blocks.append(move(blocks[-2], ahead))
        blocks.append(move(blocks[-2], behind))
    half = own_rows // 2
    blocks += [move(blocks[-2][:half], ahead), move(blocks[-1][half:], behind)]
    scale = pl.pallas_call(
        functools.partial(scale_kernel, own_rows, n_col),
        out_shape=jax.ShapeDtypeStruct((src_rows, size), jnp.float32),
        in_specs=[smem(), vmem()],
        out_specs=vmem(),
        compiler_params=params(4 * src_rows * size),
        cost_estimate=cost(0, 4 * src_rows * size),
        name="scale",
    )(place, degree)

    def product(begin, count, blocks, running, half=None):
        depth = count * own_rows
        at = 0 if half is None else half
        rows = dst_rows if half is None else dst_rows // 2
        tall = pl.BlockSpec((rows, width), lambda i: (at, 0))
        one = pl.BlockSpec((own_rows, width), lambda i: (0, 0))
        n_out = n_row // 2
        return pl.pallas_call(
            functools.partial(product_kernel, len(blocks), running is None),
            grid=(1,),
            out_shape=jax.ShapeDtypeStruct((dst_rows, width), jnp.float32)
            if half is None
            else tuple(
                jax.ShapeDtypeStruct((own_rows, width), jnp.float32 if part % 2 else jnp.bfloat16)
                for part in range(n_out)
            ),
            in_specs=[
                pl.BlockSpec((rows, depth), lambda i: (at, begin // count)),
                pl.BlockSpec((depth, size), lambda i: (begin // count, 0)),
            ]
            + [pl.BlockSpec(block.shape, lambda i: (0, 0)) for block in blocks]
            + ([] if running is None else [tall]),
            out_specs=tall if half is None else (one,) * n_out,
            scratch_shapes=[pltpu.VMEM((depth, width), jnp.bfloat16)],
            compiler_params=params(2 * rows * depth + 4 * depth * width + 4 * depth * size + 8 * rows * width),
            cost_estimate=cost(2 * rows * depth * width, 2 * rows * depth + 6 * rows * width),
            name="product",
        )(dense, scale, *blocks, *([] if running is None else [running]))

    running, begin = None, 0
    while begin < n_col - 1:
        count = n_col - 1 if n_col <= 8 else (n_col - begin) // 2
        running = product(begin, count, blocks[begin : begin + count], running)
        begin += count
    upper, lower = (product(n_col - 1, 1, blocks[-2:], running, at) for at in range(2))
    sums = {n_row - 1 - at: [part] for at, part in enumerate((*upper, *lower))}
    total = None
    for part in range(n_row - 1, 0, -1):
        bit = part & -part
        if part == n_row // 2 - 1:
            sums[part][0], _ = tie(sums[part][0], total)
        total = functools.reduce(lambda x, y: x.astype(jnp.float32) + y.astype(jnp.float32), sums[part])
        total = total.astype(jnp.bfloat16)
        sums[part ^ bit].append(lax.ppermute(total, "row", [(i, i ^ bit) for i in range(n_row)]))
    terms = sums[0]

    def own_block(term):
        at = term.shape[0] // own_rows - 1
        return pl.BlockSpec((own_rows, width), lambda i: (at, 0))

    def entire(array):
        return pl.BlockSpec(array.shape, lambda i: (0, 0))

    operands = (
        conv_weight,
        conv_bias.reshape(1, width),
        input_weight,
        input_bias.reshape(1, 3 * width),
        gates,
        memory,
    )
    return pl.pallas_call(
        tail_kernel,
        grid=(1,),
        out_shape=jax.ShapeDtypeStruct((own_rows, width), jnp.float32),
        in_specs=[entire(array) for array in operands] + [own_block(term) for term in terms],
        out_specs=pl.BlockSpec((own_rows, width), lambda i: (0, 0)),
        compiler_params=params(8 * width * width + 40 * own_rows * width),
        cost_estimate=cost(8 * own_rows * width * width, 8 * width * width + 20 * own_rows * width),
        name="tail",
    )(*operands, *terms)


def solution(mesh):
    placed = (
        P(("row", "col"), None),
        P(("col", "row"), None),
        P("row", "col", None, None, None),
        P("row", "col", None),
        P("row", "col", None),
        P("row", "col"),
        P(),
        P(),
        P(),
        P(),
        P(),
        P(),
    )
    return jax.shard_map(
        on_device, mesh=mesh, in_specs=placed, out_specs=P(("col", "row"), None), check_vma=False
    )
```

```python
import functools

import jax
import jax.numpy as jnp
from jax import lax
from jax.experimental import pallas as pl
from jax.experimental.pallas import tpu as pltpu
from jax.sharding import PartitionSpec as P

norm_epsilon = 1e-06
MIB = 1 << 20
LANES = 128
BUILD_STEPS = 4
TAIL_STEPS = 1


def vmem():
    return pl.BlockSpec(memory_space=pltpu.VMEM)


def smem():
    return pl.BlockSpec(memory_space=pltpu.SMEM)


def params(size):
    return pltpu.CompilerParams(vmem_limit_bytes=size + size // 4 + 4 * MIB)


def cost(flops, bytes_accessed):
    return pl.CostEstimate(flops=flops, bytes_accessed=bytes_accessed, transcendentals=0)


def cycle_place(col, n):
    level = lax.shift_right_logical(col, 1)
    return jnp.where((col & 1) == 0, level, n - 1 - level)


def cycle_column(place, n):
    return jnp.where(place < n // 2, 2 * place, 2 * (n - 1 - place) + 1)


def arrival_place(owner, me, n):
    back = lax.rem(cycle_place(me, n) - cycle_place(owner, n) + n, n)
    return jnp.where(back <= n // 2, jnp.maximum(2 * back - 1, 0), 2 * (n - back))


def arrival_owner(place, me, n):
    back = (place + 1) // 2 if place % 2 else (n - place // 2) % n
    return cycle_column(lax.rem(cycle_place(me, n) - back + n, n), n)


def part_place(owner, me, n):
    return n - 1 - (owner ^ me)


def build_kernel(own_rows, n_row, n_col, place_ref, count_ref, rows_any, cols_any, tiles_any, dense_ref, degree_ref, *scratch):
    acc_ref, tiles_ref, rows_ref, cols_ref, sems = scratch
    row_me, col_me = place_ref[0], place_ref[1]
    slots, size = tiles_ref.shape[:2]
    per = own_rows // size
    some = slots // BUILD_STEPS
    small = [
        pltpu.make_async_copy(rows_any, rows_ref, sems.at[0]),
        pltpu.make_async_copy(cols_any, cols_ref, sems.at[1]),
    ]
    large = [
        pltpu.make_async_copy(
            tiles_any.at[0, 0, pl.ds(step * some, some)], tiles_ref.at[pl.ds(step * some, some)], sems.at[2 + step]
        )
        for step in range(BUILD_STEPS)
    ]
    for copy in small + large:
        copy.start()
    dense_ref[...] = jnp.zeros_like(dense_ref)
    acc_ref[...] = jnp.zeros_like(acc_ref)

    def one(slot, carry):
        a, b = rows_ref[0, 0, slot], cols_ref[0, 0, slot]
        row = (part_place(lax.div(a, per), row_me, n_row) * per + lax.rem(a, per)) * size
        col = (arrival_place(lax.div(b, per), col_me, n_col) * per + lax.rem(b, per)) * size
        tile = tiles_ref[slot]
        dense_ref[pl.ds(pl.multiple_of(row, size), size), pl.ds(pl.multiple_of(col, size), size)] = tile
        wide = tile.astype(jnp.float32).reshape(size // 8, 8, size)
        acc_ref[b] += jnp.sum(wide, axis=0)
        return carry

    for copy in small:
        copy.wait()
    for step, copy in enumerate(large):
        copy.wait()
        lax.fori_loop(step * some, jnp.minimum(count_ref[0], (step + 1) * some), one, 0)
    degree_ref[...] = jnp.sum(acc_ref[...], axis=1)


def scale_kernel(own_rows, n_col, place_ref, degree_ref, scale_ref):
    col_me = place_ref[1]
    size = degree_ref.shape[1]
    per = own_rows // size
    for place in range(n_col):
        owner = arrival_owner(place, col_me, n_col)
        for half in range(per):
            line = lax.rsqrt(1.0 + degree_ref[pl.ds(owner * per + half, 1), :])
            spread = jnp.broadcast_to(line, (size, size)).T
            scale_ref[pl.ds((place * per + half) * size, size), :] = spread


def product_kernel(n_blocks, first, *refs):
    dense_ref, scale_ref = refs[:2]
    block_refs = refs[2 : 2 + n_blocks]
    sum_refs = () if first else refs[2 + n_blocks : 3 + n_blocks]
    panel_ref = refs[-1]
    out_refs = refs[2 + n_blocks + len(sum_refs) : -1]
    width = panel_ref.shape[1]
    own_rows = out_refs[0].shape[0] if len(out_refs) > 1 else block_refs[0].shape[0]
    end = 0
    for block in block_refs:
        rows = slice(end, end + block.shape[0])
        end = rows.stop
        scale = scale_ref[rows, :]
        for left in range(0, width, LANES):
            cut = slice(left, left + LANES)
            panel_ref[rows, cut] = (block[:, cut].astype(jnp.float32) * scale).astype(jnp.bfloat16)
    for place in range(dense_ref.shape[0] // own_rows):
        rows = slice(place * own_rows, (place + 1) * own_rows)
        value = jnp.dot(dense_ref[rows, :], panel_ref[...], preferred_element_type=jnp.float32)
        if not first:
            value = value + sum_refs[0][rows, :]
        if len(out_refs) == 1:
            out_refs[0][rows, :] = value
        else:
            out_refs[place][...] = value.astype(out_refs[place].dtype)


def sigmoid(x):
    return 0.5 * jnp.tanh(0.5 * x) + 0.5


def tail_kernel(*refs):
    (conv_ref, conv_bias_ref, input_ref, input_bias_ref, gates_ref, memory_ref), sums = refs[:6], refs[6:-1]
    out_ref = refs[-1]
    height, width = memory_ref.shape
    for top in range(0, height, height // TAIL_STEPS):
        rows = slice(top, top + height // TAIL_STEPS)
        owned = functools.reduce(lambda x, y: x + y, [term[rows, :].astype(jnp.float32) for term in sums])
        spread = jnp.mean(owned * owned, axis=1, keepdims=True) + norm_epsilon
        normed = (owned * lax.rsqrt(spread)).astype(jnp.bfloat16)
        message = jnp.maximum(
            jnp.dot(normed, conv_ref[...], preferred_element_type=jnp.float32) + conv_bias_ref[...], 0.0
        ).astype(jnp.bfloat16)

        def gate(index):
            cut = slice(index * width, (index + 1) * width)
            dots = jnp.dot(message, input_ref[:, cut], preferred_element_type=jnp.float32)
            return dots + input_bias_ref[:, cut], gates_ref[rows, cut]

        mine, held = gate(0)
        reset = sigmoid(mine + held)
        mine, held = gate(2)
        candidate = jnp.tanh(mine + reset * held)
        mine, held = gate(1)
        update = sigmoid(mine + held)
        out_ref[rows, :] = (1.0 - update) * candidate + update * memory_ref[rows, :]


def on_device(
    features,
    memory,
    tile_values,
    tile_rows,
    tile_cols,
    tile_count,
    conv_weight,
    conv_bias,
    input_weight,
    input_bias,
    hidden_weight,
    hidden_bias,
):
    own_rows, width = features.shape
    n_row, n_col = lax.axis_size("row"), lax.axis_size("col")
    slots, size = tile_values.shape[2], tile_values.shape[3]
    dst_rows, src_rows = own_rows * n_row, own_rows * n_col
    col_blocks = src_rows // size
    place = jnp.stack([lax.axis_index("row"), lax.axis_index("col")]).astype(jnp.int32)

    cycle = [*range(0, n_col, 2), *range(n_col - 1, 0, -2)]
    ahead = [(cycle[at - 1], cycle[at]) for at in range(n_col)]
    behind = [(to, at) for at, to in ahead]

    def tie(*values):
        return lax.optimization_barrier(values)

    def move(block, to):
        return lax.ppermute(block, "col", to)

    blocks = [features, move(features, ahead), move(features, behind)]
    dense, degree = pl.pallas_call(
        functools.partial(build_kernel, own_rows, n_row, n_col),
        out_shape=(
            jax.ShapeDtypeStruct((dst_rows, src_rows), jnp.bfloat16),
            jax.ShapeDtypeStruct((col_blocks, size), jnp.float32),
        ),
        in_specs=[smem()] * 2 + [pl.BlockSpec(memory_space=pltpu.HBM)] * 3,
        out_specs=(vmem(), vmem()),
        scratch_shapes=[
            pltpu.VMEM((col_blocks, 8, size), jnp.float32),
            pltpu.VMEM((slots, size, size), jnp.bfloat16),
            pltpu.SMEM(tile_rows.shape, jnp.int32),
            pltpu.SMEM(tile_cols.shape, jnp.int32),
            pltpu.SemaphoreType.DMA((2 + BUILD_STEPS,)),
        ],
        compiler_params=params(2 * slots * size * size + 2 * dst_rows * src_rows),
        cost_estimate=cost(0, 2 * slots * size * size + 2 * dst_rows * src_rows),
        name="build",
    )(place, tile_count.reshape(1), *[pltpu.with_memory_space_constraint(x, pltpu.HBM) for x in (tile_rows, tile_cols, tile_values)])

    added = move(degree, [(i, i ^ 1) for i in range(n_col)])
    blocks[1], degree = tie(blocks[1], degree)
    blocks.append(move(blocks[1], ahead))
    blocks[2], memory = tie(blocks[2], memory)
    blocks.append(move(blocks[2], behind))
    gates = (
        jnp.dot(memory.astype(jnp.bfloat16), hidden_weight, preferred_element_type=jnp.float32) + hidden_bias
    )
    gates, added = tie(gates, added)
    degree = degree + added
    bit = 2
    while len(blocks) < n_col - 1 or bit < n_col:
        if bit < n_col:
            added = move(degree, [(i, i ^ bit) for i in range(n_col)])
            blocks[-2], added = tie(blocks[-2], added)
            degree = degree + added
            bit *= 2
        if len(blocks) < n_col - 1:
            blocks.append(move(blocks[-2], ahead))
            blocks.append(move(blocks[-2], behind))
    half = own_rows // 2
    upper, lower = blocks[-2][:half], blocks[-1][half:]
    blocks += [move(upper, ahead), move(lower, behind)]
    degree, upper, lower = tie(degree, upper, lower)
    scale = pl.pallas_call(
        functools.partial(scale_kernel, own_rows, n_col),
        out_shape=jax.ShapeDtypeStruct((src_rows, size), jnp.float32),
        in_specs=[smem(), vmem()],
        out_specs=vmem(),
        compiler_params=params(4 * src_rows * size),
        cost_estimate=cost(0, 4 * src_rows * size),
        name="scale",
    )(place, degree)

    def product(begin, count, blocks, running, half=None):
        depth = count * own_rows
        at = 0 if half is None else half
        rows = dst_rows if half is None else dst_rows // 2
        tall = pl.BlockSpec((rows, width), lambda i: (at, 0))
        one = pl.BlockSpec((own_rows, width), lambda i: (0, 0))
        n_out = n_row // 2
        return pl.pallas_call(
            functools.partial(product_kernel, len(blocks), running is None),
            grid=(1,),
            out_shape=jax.ShapeDtypeStruct((dst_rows, width), jnp.float32)
            if half is None
            else tuple(
                jax.ShapeDtypeStruct((own_rows, width), jnp.float32 if part % 2 else jnp.bfloat16)
                for part in range(n_out)
            ),
            in_specs=[
                pl.BlockSpec((rows, depth), lambda i: (at, begin // count)),
                pl.BlockSpec((depth, size), lambda i: (begin // count, 0)),
            ]
            + [pl.BlockSpec(block.shape, lambda i: (0, 0)) for block in blocks]
            + ([] if running is None else [tall]),
            out_specs=tall if half is None else (one,) * n_out,
            scratch_shapes=[pltpu.VMEM((depth, width), jnp.bfloat16)],
            compiler_params=params(2 * rows * depth + 4 * depth * width + 4 * depth * size + 8 * rows * width),
            cost_estimate=cost(2 * rows * depth * width, 2 * rows * depth + 6 * rows * width),
            name="product",
        )(dense, scale, *blocks, *([] if running is None else [running]))

    running, begin = None, 0
    while begin < n_col - 1:
        count = n_col - 1 if n_col <= 8 else (n_col - begin) // 2
        running = product(begin, count, blocks[begin : begin + count], running)
        begin += count
    upper, lower = (product(n_col - 1, 1, blocks[-2:], running, at) for at in range(2))
    sums = {n_row - 1 - at: [part] for at, part in enumerate((*upper, *lower))}
    total = None
    for part in range(n_row - 1, 0, -1):
        bit = part & -part
        if part == n_row // 2 - 1:
            sums[part][0], _ = tie(sums[part][0], total)
        total = functools.reduce(lambda x, y: x.astype(jnp.float32) + y.astype(jnp.float32), sums[part])
        total = total.astype(jnp.bfloat16)
        sums[part ^ bit].append(lax.ppermute(total, "row", [(i, i ^ bit) for i in range(n_row)]))
    terms = sums[0]

    def own_block(term):
        at = term.shape[0] // own_rows - 1
        return pl.BlockSpec((own_rows, width), lambda i: (at, 0))

    def entire(array):
        return pl.BlockSpec(array.shape, lambda i: (0, 0))

    operands = (
        conv_weight,
        conv_bias.reshape(1, width),
        input_weight,
        input_bias.reshape(1, 3 * width),
        gates,
        memory,
    )
    return pl.pallas_call(
        tail_kernel,
        grid=(1,),
        out_shape=jax.ShapeDtypeStruct((own_rows, width), jnp.float32),
        in_specs=[entire(array) for array in operands] + [own_block(term) for term in terms],
        out_specs=pl.BlockSpec((own_rows, width), lambda i: (0, 0)),
        compiler_params=params(8 * width * width + 40 * own_rows * width),
        cost_estimate=cost(8 * own_rows * width * width, 8 * width * width + 20 * own_rows * width),
        name="tail",
    )(*operands, *terms)


def solution(mesh):
    placed = (
        P(("row", "col"), None),
        P(("col", "row"), None),
        P("row", "col", None, None, None),
        P("row", "col", None),
        P("row", "col", None),
        P("row", "col"),
        P(),
        P(),
        P(),
        P(),
        P(),
        P(),
    )
    return jax.shard_map(
        on_device, mesh=mesh, in_specs=placed, out_specs=P(("col", "row"), None), check_vma=False
    )
```

```python
import functools

import jax
import jax.numpy as jnp
from jax import lax
from jax.experimental import pallas as pl
from jax.experimental.pallas import tpu as pltpu
from jax.sharding import PartitionSpec as P

norm_epsilon = 1e-06
MIB = 1 << 20
LANES = 128
BUILD_STEPS = 4
PIECES = 1


def vmem():
    return pl.BlockSpec(memory_space=pltpu.VMEM)


def smem():
    return pl.BlockSpec(memory_space=pltpu.SMEM)


def params(size):
    return pltpu.CompilerParams(vmem_limit_bytes=size + size // 4 + 4 * MIB)


def cost(flops, bytes_accessed):
    return pl.CostEstimate(flops=flops, bytes_accessed=bytes_accessed, transcendentals=0)


def cycle_place(col, n):
    level = lax.shift_right_logical(col, 1)
    return jnp.where((col & 1) == 0, level, n - 1 - level)


def cycle_column(place, n):
    return jnp.where(place < n // 2, 2 * place, 2 * (n - 1 - place) + 1)


def arrival_place(owner, me, n):
    back = lax.rem(cycle_place(me, n) - cycle_place(owner, n) + n, n)
    return jnp.where(back <= n // 2, jnp.maximum(2 * back - 1, 0), 2 * (n - back))


def arrival_owner(place, me, n):
    back = (place + 1) // 2 if place % 2 else (n - place // 2) % n
    return cycle_column(lax.rem(cycle_place(me, n) - back + n, n), n)


def part_place(owner, me, n):
    return n - 1 - (owner ^ me)


def build_kernel(own_rows, n_row, n_col, place_ref, count_ref, rows_any, cols_any, tiles_any, dense_ref, degree_ref, *scratch):
    acc_ref, tiles_ref, rows_ref, cols_ref, sems = scratch
    row_me, col_me = place_ref[0], place_ref[1]
    slots, size = tiles_ref.shape[:2]
    per = own_rows // size
    some = slots // BUILD_STEPS
    small = [
        pltpu.make_async_copy(rows_any, rows_ref, sems.at[0]),
        pltpu.make_async_copy(cols_any, cols_ref, sems.at[1]),
    ]
    large = [
        pltpu.make_async_copy(
            tiles_any.at[0, 0, pl.ds(step * some, some)], tiles_ref.at[pl.ds(step * some, some)], sems.at[2 + step]
        )
        for step in range(BUILD_STEPS)
    ]
    for copy in small + large:
        copy.start()
    dense_ref[...] = jnp.zeros_like(dense_ref)
    acc_ref[...] = jnp.zeros_like(acc_ref)

    def one(slot, carry):
        a, b = rows_ref[0, 0, slot], cols_ref[0, 0, slot]
        row = (part_place(lax.div(a, per), row_me, n_row) * per + lax.rem(a, per)) * size
        col = (arrival_place(lax.div(b, per), col_me, n_col) * per + lax.rem(b, per)) * size
        tile = tiles_ref[slot]
        dense_ref[pl.ds(pl.multiple_of(row, size), size), pl.ds(pl.multiple_of(col, size), size)] = tile
        wide = tile.astype(jnp.float32).reshape(size // 8, 8, size)
        acc_ref[b] += jnp.sum(wide, axis=0)
        return carry

    for copy in small:
        copy.wait()
    for step, copy in enumerate(large):
        copy.wait()
        lax.fori_loop(step * some, jnp.minimum(count_ref[0], (step + 1) * some), one, 0)
    degree_ref[...] = jnp.sum(acc_ref[...], axis=1)


def scale_kernel(own_rows, n_col, place_ref, degree_ref, scale_ref):
    col_me = place_ref[1]
    size = degree_ref.shape[1]
    per = own_rows // size
    for place in range(n_col):
        owner = arrival_owner(place, col_me, n_col)
        for half in range(per):
            line = lax.rsqrt(1.0 + degree_ref[pl.ds(owner * per + half, 1), :])
            spread = jnp.broadcast_to(line, (size, size)).T
            scale_ref[pl.ds((place * per + half) * size, size), :] = spread


def product_kernel(n_row, n_blocks, first, *refs):
    dense_ref, scale_ref = refs[:2]
    block_refs = refs[2 : 2 + n_blocks]
    sum_refs = () if first else refs[2 + n_blocks : 3 + n_blocks]
    panel_ref = refs[-1]
    out_refs = refs[2 + n_blocks + len(sum_refs) : -1]
    width = panel_ref.shape[1]
    own_rows = out_refs[0].shape[0] if len(out_refs) > 1 else dense_ref.shape[0] // n_row
    end = 0
    for block in block_refs:
        rows = slice(end, end + block.shape[0])
        end = rows.stop
        scale = scale_ref[rows, :]
        for left in range(0, width, LANES):
            cut = slice(left, left + LANES)
            panel_ref[rows, cut] = (block[:, cut].astype(jnp.float32) * scale).astype(jnp.bfloat16)
    for place in range(dense_ref.shape[0] // own_rows):
        rows = slice(place * own_rows, (place + 1) * own_rows)
        value = jnp.dot(dense_ref[rows, :], panel_ref[...], preferred_element_type=jnp.float32)
        if not first:
            value = value + sum_refs[0][rows, :]
        if len(out_refs) == 1:
            out_refs[0][rows, :] = value
        else:
            out_refs[place][...] = value.astype(out_refs[place].dtype)


def sigmoid(x):
    return 0.5 * jnp.tanh(0.5 * x) + 0.5


def tail_kernel(*refs):
    (conv_ref, conv_bias_ref, input_ref, input_bias_ref, memory_ref), gate_refs, sums = refs[:5], refs[5:8], refs[8:-1]
    out_ref = refs[-1]
    width = memory_ref.shape[1]
    owned = functools.reduce(lambda x, y: x + y, [term[...].astype(jnp.float32) for term in sums])
    spread = jnp.mean(owned * owned, axis=1, keepdims=True) + norm_epsilon
    normed = (owned * lax.rsqrt(spread)).astype(jnp.bfloat16)
    message = jnp.maximum(
        jnp.dot(normed, conv_ref[...], preferred_element_type=jnp.float32) + conv_bias_ref[...], 0.0
    ).astype(jnp.bfloat16)

    def gate(index):
        cut = slice(index * width, (index + 1) * width)
        dots = jnp.dot(message, input_ref[:, cut], preferred_element_type=jnp.float32)
        return dots + input_bias_ref[:, cut], gate_refs[index][...]

    mine, held = gate(0)
    reset = sigmoid(mine + held)
    mine, held = gate(2)
    candidate = jnp.tanh(mine + reset * held)
    mine, held = gate(1)
    update = sigmoid(mine + held)
    out_ref[...] = (1.0 - update) * candidate + update * memory_ref[...]


def on_device(
    features,
    memory,
    tile_values,
    tile_rows,
    tile_cols,
    tile_count,
    conv_weight,
    conv_bias,
    input_weight,
    input_bias,
    hidden_weight,
    hidden_bias,
):
    own_rows, width = features.shape
    n_row, n_col = lax.axis_size("row"), lax.axis_size("col")
    slots, size = tile_values.shape[2], tile_values.shape[3]
    dst_rows, src_rows = own_rows * n_row, own_rows * n_col
    col_blocks = src_rows // size
    place = jnp.stack([lax.axis_index("row"), lax.axis_index("col")]).astype(jnp.int32)

    cycle = [*range(0, n_col, 2), *range(n_col - 1, 0, -2)]
    ahead = [(cycle[at - 1], cycle[at]) for at in range(n_col)]
    behind = [(to, at) for at, to in ahead]

    def tie(*values):
        return lax.optimization_barrier(values)

    def move(block, to):
        return lax.ppermute(block, "col", to)

    half, height = own_rows // 2, own_rows // PIECES
    rides = [[features[top : top + height]] for top in range(0, own_rows, height)]
    for ride in rides:
        ride += [move(ride[0], ahead), move(ride[0], behind)]
    dense, degree = pl.pallas_call(
        functools.partial(build_kernel, own_rows, n_row, n_col),
        out_shape=(
            jax.ShapeDtypeStruct((dst_rows, src_rows), jnp.bfloat16),
            jax.ShapeDtypeStruct((col_blocks, size), jnp.float32),
        ),
        in_specs=[smem()] * 2 + [pl.BlockSpec(memory_space=pltpu.HBM)] * 3,
        out_specs=(vmem(), vmem()),
        scratch_shapes=[
            pltpu.VMEM((col_blocks, 8, size), jnp.float32),
            pltpu.VMEM((slots, size, size), jnp.bfloat16),
            pltpu.SMEM(tile_rows.shape, jnp.int32),
            pltpu.SMEM(tile_cols.shape, jnp.int32),
            pltpu.SemaphoreType.DMA((2 + BUILD_STEPS,)),
        ],
        compiler_params=params(2 * slots * size * size + 2 * dst_rows * src_rows),
        cost_estimate=cost(0, 2 * slots * size * size + 2 * dst_rows * src_rows),
        name="build",
    )(place, tile_count.reshape(1), *[pltpu.with_memory_space_constraint(x, pltpu.HBM) for x in (tile_rows, tile_cols, tile_values)])

    gates = []

    def gate_product(block):
        nonlocal memory
        block, memory = tie(block, memory)
        cut = slice(len(gates) * width, (len(gates) + 1) * width)
        gates.append(
            jnp.dot(memory.astype(jnp.bfloat16), hidden_weight[:, cut], preferred_element_type=jnp.float32)
            + hidden_bias[cut]
        )
        return block

    added = move(degree, [(i, i ^ 1) for i in range(n_col)])
    rides[0][1], degree = tie(rides[0][1], degree)
    bit = 2
    while len(rides[0]) < n_col - 1:
        for ride in rides:
            ride.append(move(ride[-2], ahead))
            if ride is rides[-1]:
                if len(gates) < 2:
                    ride[-2] = gate_product(ride[-2])
                    gates[-1], added = tie(gates[-1], added)
                elif bit < n_col:
                    ride[-2], added = tie(ride[-2], added)
            ride.append(move(ride[-2], behind))
        if bit < n_col:
            degree = degree + added
            added = move(degree, [(i, i ^ bit) for i in range(n_col)])
            bit *= 2
    upper, lower = rides[0][-2][:half], rides[-1][-1][height - half :]
    across = (move(upper, ahead), move(lower, behind))
    upper, lower, memory = tie(upper, lower, memory)
    gate_product(upper)
    gates[-1], added = tie(gates[-1], added)
    degree = degree + added
    blocks = [tuple(ride[at] for ride in rides) for at in range(n_col - 1)] + [across]
    scale = pl.pallas_call(
        functools.partial(scale_kernel, own_rows, n_col),
        out_shape=jax.ShapeDtypeStruct((src_rows, size), jnp.float32),
        in_specs=[smem(), vmem()],
        out_specs=vmem(),
        compiler_params=params(4 * src_rows * size),
        cost_estimate=cost(0, 4 * src_rows * size),
        name="scale",
    )(place, degree)

    def product(begin, count, blocks, running, half=None):
        depth = count * own_rows
        at = 0 if half is None else half
        rows = dst_rows if half is None else dst_rows // 2
        tall = pl.BlockSpec((rows, width), lambda i: (at, 0))
        one = pl.BlockSpec((own_rows, width), lambda i: (0, 0))
        n_out = n_row // 2
        return pl.pallas_call(
            functools.partial(product_kernel, n_row, len(blocks), running is None),
            grid=(1,),
            out_shape=jax.ShapeDtypeStruct((dst_rows, width), jnp.float32)
            if half is None
            else tuple(
                jax.ShapeDtypeStruct((own_rows, width), jnp.float32 if part % 2 else jnp.bfloat16)
                for part in range(n_out)
            ),
            in_specs=[
                pl.BlockSpec((rows, depth), lambda i: (at, begin // count)),
                pl.BlockSpec((depth, size), lambda i: (begin // count, 0)),
            ]
            + [pl.BlockSpec(block.shape, lambda i: (0, 0)) for block in blocks]
            + ([] if running is None else [tall]),
            out_specs=tall if half is None else (one,) * n_out,
            scratch_shapes=[pltpu.VMEM((depth, width), jnp.bfloat16)],
            compiler_params=params(2 * rows * depth + 4 * depth * width + 4 * depth * size + 8 * rows * width),
            cost_estimate=cost(2 * rows * depth * width, 2 * rows * depth + 6 * rows * width),
            name="product",
        )(dense, scale, *blocks, *([] if running is None else [running]))

    running, begin = None, 0
    while begin < n_col - 1:
        count = n_col - 1 if n_col <= 8 else (n_col - begin) // 2
        running = product(begin, count, sum(blocks[begin : begin + count], ()), running)
        begin += count
    upper, lower = (product(n_col - 1, 1, blocks[-1], running, at) for at in range(2))
    sums = {n_row - 1 - at: [part] for at, part in enumerate((*upper, *lower))}
    total = None
    for part in range(n_row - 1, 0, -1):
        bit = part & -part
        if part == n_row // 2 - 1:
            sums[part][0], _ = tie(sums[part][0], total)
        total = functools.reduce(lambda x, y: x.astype(jnp.float32) + y.astype(jnp.float32), sums[part])
        total = total.astype(jnp.bfloat16)
        sums[part ^ bit].append(lax.ppermute(total, "row", [(i, i ^ bit) for i in range(n_row)]))
    terms = sums[0]

    def own_block(term):
        at = term.shape[0] // own_rows - 1
        return pl.BlockSpec((own_rows, width), lambda i: (at, 0))

    def entire(array):
        return pl.BlockSpec(array.shape, lambda i: (0, 0))

    operands = (
        conv_weight,
        conv_bias.reshape(1, width),
        input_weight,
        input_bias.reshape(1, 3 * width),
        memory,
        *gates,
    )
    return pl.pallas_call(
        tail_kernel,
        grid=(1,),
        out_shape=jax.ShapeDtypeStruct((own_rows, width), jnp.float32),
        in_specs=[entire(array) for array in operands] + [own_block(term) for term in terms],
        out_specs=pl.BlockSpec((own_rows, width), lambda i: (0, 0)),
        compiler_params=params(8 * width * width + 40 * own_rows * width),
        cost_estimate=cost(8 * own_rows * width * width, 8 * width * width + 20 * own_rows * width),
        name="tail",
    )(*operands, *terms)


def solution(mesh):
    placed = (
        P(("row", "col"), None),
        P(("col", "row"), None),
        P("row", "col", None, None, None),
        P("row", "col", None),
        P("row", "col", None),
        P("row", "col"),
        P(),
        P(),
        P(),
        P(),
        P(),
        P(),
    )
    return jax.shard_map(
        on_device, mesh=mesh, in_specs=placed, out_specs=P(("col", "row"), None), check_vma=False
    )
```

```python
import functools

import jax
import jax.numpy as jnp
from jax import lax
from jax.experimental import pallas as pl
from jax.experimental.pallas import tpu as pltpu
from jax.sharding import PartitionSpec as P

norm_epsilon = 1e-06
MIB = 1 << 20
LANES = 128
BUILD_STEPS = 4


def vmem():
    return pl.BlockSpec(memory_space=pltpu.VMEM)


def smem():
    return pl.BlockSpec(memory_space=pltpu.SMEM)


def params(size):
    return pltpu.CompilerParams(vmem_limit_bytes=size + size // 4 + 4 * MIB)


def cost(flops, bytes_accessed):
    return pl.CostEstimate(flops=flops, bytes_accessed=bytes_accessed, transcendentals=0)


def cycle_place(col, n):
    level = lax.shift_right_logical(col, 1)
    return jnp.where((col & 1) == 0, level, n - 1 - level)


def cycle_column(place, n):
    return jnp.where(place < n // 2, 2 * place, 2 * (n - 1 - place) + 1)


def arrival_place(owner, me, n):
    back = lax.rem(cycle_place(me, n) - cycle_place(owner, n) + n, n)
    return jnp.where(back <= n // 2, jnp.maximum(2 * back - 1, 0), 2 * (n - back))


def arrival_owner(place, me, n):
    back = (place + 1) // 2 if place % 2 else (n - place // 2) % n
    return cycle_column(lax.rem(cycle_place(me, n) - back + n, n), n)


def part_place(owner, me, n):
    return n - 1 - (owner ^ me)


def build_kernel(own_rows, n_row, n_col, place_ref, count_ref, rows_any, cols_any, tiles_any, dense_ref, degree_ref, *scratch):
    acc_ref, tiles_ref, rows_ref, cols_ref, sems = scratch
    row_me, col_me = place_ref[0], place_ref[1]
    slots, size = tiles_ref.shape[:2]
    per = own_rows // size
    some = slots // BUILD_STEPS
    small = [
        pltpu.make_async_copy(rows_any, rows_ref, sems.at[0]),
        pltpu.make_async_copy(cols_any, cols_ref, sems.at[1]),
    ]
    large = [
        pltpu.make_async_copy(
            tiles_any.at[0, 0, pl.ds(step * some, some)], tiles_ref.at[pl.ds(step * some, some)], sems.at[2 + step]
        )
        for step in range(BUILD_STEPS)
    ]
    for copy in small + large:
        copy.start()
    dense_ref[...] = jnp.zeros_like(dense_ref)
    acc_ref[...] = jnp.zeros_like(acc_ref)

    def one(slot, carry):
        a, b = rows_ref[0, 0, slot], cols_ref[0, 0, slot]
        row = (part_place(lax.div(a, per), row_me, n_row) * per + lax.rem(a, per)) * size
        col = (arrival_place(lax.div(b, per), col_me, n_col) * per + lax.rem(b, per)) * size
        tile = tiles_ref[slot]
        dense_ref[pl.ds(pl.multiple_of(row, size), size), pl.ds(pl.multiple_of(col, size), size)] = tile
        wide = tile.astype(jnp.float32).reshape(size // 8, 8, size)
        acc_ref[b] += jnp.sum(wide, axis=0)
        return carry

    for copy in small:
        copy.wait()
    for step, copy in enumerate(large):
        copy.wait()
        lax.fori_loop(step * some, jnp.minimum(count_ref[0], (step + 1) * some), one, 0)
    degree_ref[...] = jnp.sum(acc_ref[...], axis=1)


def product_kernel(n_row, n_col, begin, n_blocks, first, *refs):
    place_ref, dense_ref, degree_ref = refs[:3]
    block_refs = refs[3 : 3 + n_blocks]
    sum_refs = () if first else refs[3 + n_blocks : 4 + n_blocks]
    panel_ref = refs[-1]
    sum_out_ref, scale_ref = refs[-3:-1]
    width, size = panel_ref.shape[1], degree_ref.shape[1]
    own_rows = dense_ref.shape[0] // n_row

    def scale(row):
        owner = arrival_owner(begin + row // own_rows, place_ref[1], n_col)
        index = owner * (own_rows // size) + row % own_rows // size
        line = lax.rsqrt(1.0 + degree_ref[pl.ds(index, 1), :])
        return jnp.broadcast_to(line, (size, size)).T

    for place, block in enumerate(block_refs):
        for top in range(0, own_rows, size):
            row = place * own_rows + top
            spread = scale(row)
            for left in range(0, width, LANES):
                cut = slice(left, left + LANES)
                value = block[top : top + size, cut].astype(jnp.float32) * spread
                panel_ref[row : row + size, cut] = value.astype(jnp.bfloat16)
    for top in range(0, own_rows, size):
        scale_ref[top : top + size, :] = scale((n_col - 1 - begin) * own_rows + top)
    for part in range(n_row):
        rows = slice(part * own_rows, (part + 1) * own_rows)
        value = jnp.dot(dense_ref[rows, :], panel_ref[...], preferred_element_type=jnp.float32)
        if not first:
            value = value + sum_refs[0][rows, :]
        sum_out_ref[rows, :] = value


def last_kernel(*refs):
    dense_ref, scale_ref, upper_ref, lower_ref, sum_ref, *out_refs, panel_ref = refs
    own_rows, width = panel_ref.shape
    for block, top in ((upper_ref, 0), (lower_ref, own_rows // 2)):
        rows = slice(top, top + own_rows // 2)
        for left in range(0, width, LANES):
            cut = slice(left, left + LANES)
            panel_ref[rows, cut] = (block[:, cut].astype(jnp.float32) * scale_ref[rows, :]).astype(jnp.bfloat16)
    for place, out_ref in enumerate(out_refs):
        rows = slice(place * own_rows, (place + 1) * own_rows)
        value = jnp.dot(dense_ref[rows, :], panel_ref[...], preferred_element_type=jnp.float32)
        out_ref[...] = (value + sum_ref[rows, :]).astype(out_ref.dtype)


def sigmoid(x):
    return 0.5 * jnp.tanh(0.5 * x) + 0.5


def tail_kernel(*refs):
    (conv_ref, conv_bias_ref, input_ref, input_bias_ref, memory_ref), gate_refs, sums = refs[:5], refs[5:8], refs[8:-1]
    out_ref = refs[-1]
    width = memory_ref.shape[1]
    owned = functools.reduce(lambda x, y: x + y, [term[...].astype(jnp.float32) for term in sums])
    spread = jnp.mean(owned * owned, axis=1, keepdims=True) + norm_epsilon
    normed = (owned * lax.rsqrt(spread)).astype(jnp.bfloat16)
    message = jnp.maximum(
        jnp.dot(normed, conv_ref[...], preferred_element_type=jnp.float32) + conv_bias_ref[...], 0.0
    ).astype(jnp.bfloat16)

    def gate(index):
        cut = slice(index * width, (index + 1) * width)
        dots = jnp.dot(message, input_ref[:, cut], preferred_element_type=jnp.float32)
        return dots + input_bias_ref[:, cut], gate_refs[index][...]

    mine, held = gate(0)
    reset = sigmoid(mine + held)
    mine, held = gate(2)
    candidate = jnp.tanh(mine + reset * held)
    mine, held = gate(1)
    update = sigmoid(mine + held)
    out_ref[...] = (1.0 - update) * candidate + update * memory_ref[...]


def on_device(
    features,
    memory,
    tile_values,
    tile_rows,
    tile_cols,
    tile_count,
    conv_weight,
    conv_bias,
    input_weight,
    input_bias,
    hidden_weight,
    hidden_bias,
):
    own_rows, width = features.shape
    n_row, n_col = lax.axis_size("row"), lax.axis_size("col")
    slots, size = tile_values.shape[2], tile_values.shape[3]
    dst_rows, src_rows = own_rows * n_row, own_rows * n_col
    col_blocks = src_rows // size
    place = jnp.stack([lax.axis_index("row"), lax.axis_index("col")]).astype(jnp.int32)

    cycle = [*range(0, n_col, 2), *range(n_col - 1, 0, -2)]
    ahead = [(cycle[at - 1], cycle[at]) for at in range(n_col)]
    behind = [(to, at) for at, to in ahead]

    def tie(*values):
        return lax.optimization_barrier(values)

    def move(block, to):
        return lax.ppermute(block, "col", to)

    blocks = [features, move(features, ahead), move(features, behind)]
    half = own_rows // 2
    dense, degree = pl.pallas_call(
        functools.partial(build_kernel, own_rows, n_row, n_col),
        out_shape=(
            jax.ShapeDtypeStruct((dst_rows, src_rows), jnp.bfloat16),
            jax.ShapeDtypeStruct((col_blocks, size), jnp.float32),
        ),
        in_specs=[smem()] * 2 + [pl.BlockSpec(memory_space=pltpu.HBM)] * 3,
        out_specs=(vmem(), vmem()),
        scratch_shapes=[
            pltpu.VMEM((col_blocks, 8, size), jnp.float32),
            pltpu.VMEM((slots, size, size), jnp.bfloat16),
            pltpu.SMEM(tile_rows.shape, jnp.int32),
            pltpu.SMEM(tile_cols.shape, jnp.int32),
            pltpu.SemaphoreType.DMA((2 + BUILD_STEPS,)),
        ],
        compiler_params=params(2 * slots * size * size + 2 * dst_rows * src_rows),
        cost_estimate=cost(0, 2 * slots * size * size + 2 * dst_rows * src_rows),
        name="build",
    )(place, tile_count.reshape(1), *[pltpu.with_memory_space_constraint(x, pltpu.HBM) for x in (tile_rows, tile_cols, tile_values)])

    gates = []

    def gate_product(block):
        nonlocal memory
        block, memory = tie(block, memory)
        cut = slice(len(gates) * width, (len(gates) + 1) * width)
        gates.append(
            jnp.dot(memory.astype(jnp.bfloat16), hidden_weight[:, cut], preferred_element_type=jnp.float32)
            + hidden_bias[cut]
        )
        return block

    added = move(degree, [(i, i ^ 1) for i in range(n_col)])
    blocks[2], degree = tie(blocks[2], degree)
    bit = 2
    while len(blocks) < n_col - 1:
        blocks.append(move(blocks[-2], ahead))
        if len(gates) < 2:
            blocks[-2] = gate_product(blocks[-2])
            gates[-1], added = tie(gates[-1], added)
        elif bit < n_col:
            blocks[-2], added = tie(blocks[-2], added)
        blocks.append(move(blocks[-2], behind))
        if bit < n_col:
            degree = degree + added
            added = move(degree, [(i, i ^ bit) for i in range(n_col)])
            bit *= 2
    upper, lower = blocks[-2][:half], blocks[-1][half:]
    across = (move(upper, ahead), move(lower, behind))
    upper, lower, memory = tie(upper, lower, memory)
    gate_product(upper)
    gates[-1], added = tie(gates[-1], added)
    degree = degree + added

    def whole(*shape):
        return pl.BlockSpec(shape, lambda i: (0, 0))

    def product(begin, count, running):
        depth = count * own_rows
        return pl.pallas_call(
            functools.partial(product_kernel, n_row, n_col, begin, count, running is None),
            grid=(1,),
            out_shape=(
                jax.ShapeDtypeStruct((dst_rows, width), jnp.float32),
                jax.ShapeDtypeStruct((own_rows, size), jnp.float32),
            ),
            in_specs=[
                smem(),
                pl.BlockSpec((dst_rows, depth), lambda i: (0, begin // count)),
                whole(col_blocks, size),
            ]
            + [whole(own_rows, width)] * count
            + ([] if running is None else [whole(dst_rows, width)]),
            out_specs=(whole(dst_rows, width), whole(own_rows, size)),
            scratch_shapes=[pltpu.VMEM((depth, width), jnp.bfloat16)],
            compiler_params=params(2 * dst_rows * depth + 4 * depth * width + 8 * dst_rows * width + 2 * MIB),
            cost_estimate=cost(2 * dst_rows * depth * width, 2 * dst_rows * depth + 6 * dst_rows * width),
            name="product",
        )(place, dense, degree, *blocks[begin : begin + count], *([] if running is None else [running]))

    def last_product(at):
        rows = dst_rows // 2
        dtypes = [jnp.float32 if part % 2 else jnp.bfloat16 for part in range(n_row // 2)]
        return pl.pallas_call(
            last_kernel,
            grid=(1,),
            out_shape=tuple(jax.ShapeDtypeStruct((own_rows, width), dtype) for dtype in dtypes),
            in_specs=[
                pl.BlockSpec((rows, own_rows), lambda i: (at, n_col - 1)),
                whole(own_rows, size),
                whole(half, width),
                whole(half, width),
                pl.BlockSpec((rows, width), lambda i: (at, 0)),
            ],
            out_specs=(whole(own_rows, width),) * len(dtypes),
            scratch_shapes=[pltpu.VMEM((own_rows, width), jnp.bfloat16)],
            compiler_params=params(2 * rows * own_rows + 6 * own_rows * width + 8 * rows * width + 2 * MIB),
            cost_estimate=cost(2 * rows * own_rows * width, 2 * rows * own_rows + 6 * rows * width),
            name="last_product",
        )(dense, scale, *across, running)

    running, begin = None, 0
    while begin < n_col - 1:
        count = n_col - 1 if n_col <= 8 else (n_col - begin) // 2
        running, scale = product(begin, count, running)
        begin += count
    sums = {n_row - 1 - at: [part] for at, part in enumerate((*last_product(0), *last_product(1)))}
    total = None
    for part in range(n_row - 1, 0, -1):
        bit = part & -part
        if part == n_row // 2 - 1:
            sums[part][0], _ = tie(sums[part][0], total)
        total = functools.reduce(lambda x, y: x.astype(jnp.float32) + y.astype(jnp.float32), sums[part])
        total = total.astype(jnp.bfloat16)
        sums[part ^ bit].append(lax.ppermute(total, "row", [(i, i ^ bit) for i in range(n_row)]))
    terms = sums[0]

    def own_block(term):
        at = term.shape[0] // own_rows - 1
        return pl.BlockSpec((own_rows, width), lambda i: (at, 0))

    def entire(array):
        return pl.BlockSpec(array.shape, lambda i: (0, 0))

    operands = (
        conv_weight,
        conv_bias.reshape(1, width),
        input_weight,
        input_bias.reshape(1, 3 * width),
        memory,
        *gates,
    )
    return pl.pallas_call(
        tail_kernel,
        grid=(1,),
        out_shape=jax.ShapeDtypeStruct((own_rows, width), jnp.float32),
        in_specs=[entire(array) for array in operands] + [own_block(term) for term in terms],
        out_specs=pl.BlockSpec((own_rows, width), lambda i: (0, 0)),
        compiler_params=params(8 * width * width + 40 * own_rows * width),
        cost_estimate=cost(8 * own_rows * width * width, 8 * width * width + 20 * own_rows * width),
        name="tail",
    )(*operands, *terms)


def solution(mesh):
    placed = (
        P(("row", "col"), None),
        P(("col", "row"), None),
        P("row", "col", None, None, None),
        P("row", "col", None),
        P("row", "col", None),
        P("row", "col"),
        P(),
        P(),
        P(),
        P(),
        P(),
        P(),
    )
    return jax.shard_map(
        on_device, mesh=mesh, in_specs=placed, out_specs=P(("col", "row"), None), check_vma=False
    )
```

```python
import functools

import jax
import jax.numpy as jnp
from jax import lax
from jax.experimental import pallas as pl
from jax.experimental.pallas import tpu as pltpu
from jax.sharding import PartitionSpec as P

norm_epsilon = 1e-06
MIB = 1 << 20
LANES = 128
BUILD_STEPS = 4


def vmem():
    return pl.BlockSpec(memory_space=pltpu.VMEM)


def smem():
    return pl.BlockSpec(memory_space=pltpu.SMEM)


def params(size):
    return pltpu.CompilerParams(vmem_limit_bytes=size + size // 4 + 4 * MIB)


def cost(flops, bytes_accessed):
    return pl.CostEstimate(flops=flops, bytes_accessed=bytes_accessed, transcendentals=0)


def cycle_place(col, n):
    level = lax.shift_right_logical(col, 1)
    return jnp.where((col & 1) == 0, level, n - 1 - level)


def cycle_column(place, n):
    return jnp.where(place < n // 2, 2 * place, 2 * (n - 1 - place) + 1)


def arrival_place(owner, me, turned, n):
    back = lax.rem(cycle_place(me, n) - cycle_place(owner, n) + n, n)
    back = jnp.where(turned, lax.rem(n - back, n), back)
    return jnp.where(back <= n // 2, jnp.maximum(2 * back - 1, 0), 2 * (n - back))


def arrival_owner(place, me, turned, n):
    back = (place + 1) // 2 if place % 2 else (n - place // 2) % n
    back = jnp.where(turned, (n - back) % n, back)
    return cycle_column(lax.rem(cycle_place(me, n) - back + n, n), n)


def part_place(owner, me, n):
    return n - 1 - (owner ^ me)


def build_kernel(own_rows, n_row, n_col, place_ref, count_ref, rows_any, cols_any, tiles_any, dense_ref, degree_ref, *scratch):
    acc_ref, tiles_ref, rows_ref, cols_ref, sems = scratch
    row_me, col_me = place_ref[0], place_ref[1]
    slots, size = tiles_ref.shape[:2]
    per = own_rows // size
    some = slots // BUILD_STEPS
    small = [
        pltpu.make_async_copy(rows_any, rows_ref, sems.at[0]),
        pltpu.make_async_copy(cols_any, cols_ref, sems.at[1]),
    ]
    large = [
        pltpu.make_async_copy(
            tiles_any.at[0, 0, pl.ds(step * some, some)], tiles_ref.at[pl.ds(step * some, some)], sems.at[2 + step]
        )
        for step in range(BUILD_STEPS)
    ]
    for copy in small + large:
        copy.start()
    dense_ref[...] = jnp.zeros_like(dense_ref)
    acc_ref[...] = jnp.zeros_like(acc_ref)

    def one(slot, carry):
        a, b = rows_ref[0, 0, slot], cols_ref[0, 0, slot]
        row = (part_place(lax.div(a, per), row_me, n_row) * per + lax.rem(a, per)) * size
        col = (arrival_place(lax.div(b, per), col_me, (row_me & 1) == 1, n_col) * per + lax.rem(b, per)) * size
        tile = tiles_ref[slot]
        dense_ref[pl.ds(pl.multiple_of(row, size), size), pl.ds(pl.multiple_of(col, size), size)] = tile
        wide = tile.astype(jnp.float32).reshape(size // 8, 8, size)
        acc_ref[b] += jnp.sum(wide, axis=0)
        return carry

    for copy in small:
        copy.wait()
    for step, copy in enumerate(large):
        copy.wait()
        lax.fori_loop(step * some, jnp.minimum(count_ref[0], (step + 1) * some), one, 0)
    degree_ref[...] = jnp.sum(acc_ref[...], axis=1)


def product_kernel(n_row, n_col, begin, n_blocks, first, *refs):
    place_ref, dense_ref, degree_ref = refs[:3]
    block_refs = refs[3 : 3 + n_blocks]
    sum_refs = () if first else refs[3 + n_blocks : 4 + n_blocks]
    panel_ref = refs[-1]
    sum_out_ref, scale_ref = refs[-3:-1]
    width, size = panel_ref.shape[1], degree_ref.shape[1]
    own_rows = dense_ref.shape[0] // n_row

    def scale(row):
        owner = arrival_owner(begin + row // own_rows, place_ref[1], (place_ref[0] & 1) == 1, n_col)
        index = owner * (own_rows // size) + row % own_rows // size
        line = lax.rsqrt(1.0 + degree_ref[pl.ds(index, 1), :])
        return jnp.broadcast_to(line, (size, size)).T

    for place, block in enumerate(block_refs):
        for top in range(0, own_rows, size):
            row = place * own_rows + top
            spread = scale(row)
            for left in range(0, width, LANES):
                cut = slice(left, left + LANES)
                value = block[top : top + size, cut].astype(jnp.float32) * spread
                panel_ref[row : row + size, cut] = value.astype(jnp.bfloat16)
    for top in range(0, own_rows, size):
        scale_ref[top : top + size, :] = scale((n_col - 1 - begin) * own_rows + top)
    for part in range(n_row):
        rows = slice(part * own_rows, (part + 1) * own_rows)
        value = jnp.dot(dense_ref[rows, :], panel_ref[...], preferred_element_type=jnp.float32)
        if not first:
            value = value + sum_refs[0][rows, :]
        sum_out_ref[rows, :] = value


def last_kernel(*refs):
    dense_ref, scale_ref, upper_ref, lower_ref, sum_ref, *out_refs, panel_ref = refs
    own_rows, width = panel_ref.shape
    for block, top in ((upper_ref, 0), (lower_ref, own_rows // 2)):
        rows = slice(top, top + own_rows // 2)
        for left in range(0, width, LANES):
            cut = slice(left, left + LANES)
            panel_ref[rows, cut] = (block[:, cut].astype(jnp.float32) * scale_ref[rows, :]).astype(jnp.bfloat16)
    for place, out_ref in enumerate(out_refs):
        rows = slice(place * own_rows, (place + 1) * own_rows)
        value = jnp.dot(dense_ref[rows, :], panel_ref[...], preferred_element_type=jnp.float32)
        out_ref[...] = (value + sum_ref[rows, :]).astype(out_ref.dtype)


def sigmoid(x):
    return 0.5 * jnp.tanh(0.5 * x) + 0.5


def tail_kernel(*refs):
    (conv_ref, conv_bias_ref, input_ref, input_bias_ref, memory_ref), gate_refs, sums = refs[:5], refs[5:8], refs[8:-1]
    out_ref = refs[-1]
    width = memory_ref.shape[1]
    owned = functools.reduce(lambda x, y: x + y, [term[...].astype(jnp.float32) for term in sums])
    spread = jnp.mean(owned * owned, axis=1, keepdims=True) + norm_epsilon
    normed = (owned * lax.rsqrt(spread)).astype(jnp.bfloat16)
    message = jnp.maximum(
        jnp.dot(normed, conv_ref[...], preferred_element_type=jnp.float32) + conv_bias_ref[...], 0.0
    ).astype(jnp.bfloat16)

    def gate(index):
        cut = slice(index * width, (index + 1) * width)
        dots = jnp.dot(message, input_ref[:, cut], preferred_element_type=jnp.float32)
        return dots + input_bias_ref[:, cut], gate_refs[index][...]

    mine, held = gate(0)
    reset = sigmoid(mine + held)
    mine, held = gate(2)
    candidate = jnp.tanh(mine + reset * held)
    mine, held = gate(1)
    update = sigmoid(mine + held)
    out_ref[...] = (1.0 - update) * candidate + update * memory_ref[...]


def on_device(
    features,
    memory,
    tile_values,
    tile_rows,
    tile_cols,
    tile_count,
    conv_weight,
    conv_bias,
    input_weight,
    input_bias,
    hidden_weight,
    hidden_bias,
):
    own_rows, width = features.shape
    n_row, n_col = lax.axis_size("row"), lax.axis_size("col")
    slots, size = tile_values.shape[2], tile_values.shape[3]
    dst_rows, src_rows = own_rows * n_row, own_rows * n_col
    col_blocks = src_rows // size
    place = jnp.stack([lax.axis_index("row"), lax.axis_index("col")]).astype(jnp.int32)

    cycle = [*range(0, n_col, 2), *range(n_col - 1, 0, -2)]
    once = [(cycle[at - 1], cycle[at]) for at in range(n_col)]
    ahead, behind = [], []
    for row in range(n_row):
        for first, second in once:
            first, second = row * n_col + first, row * n_col + second
            ahead.append((second, first) if row % 2 else (first, second))
            behind.append((first, second) if row % 2 else (second, first))

    def ride(block, to):
        return lax.ppermute(block, ("row", "col"), to)

    def tie(*values):
        return lax.optimization_barrier(values)

    def move(block, to):
        return lax.ppermute(block, "col", to)

    blocks = [features, ride(features, ahead), ride(features, behind)]
    half = own_rows // 2
    dense, degree = pl.pallas_call(
        functools.partial(build_kernel, own_rows, n_row, n_col),
        out_shape=(
            jax.ShapeDtypeStruct((dst_rows, src_rows), jnp.bfloat16),
            jax.ShapeDtypeStruct((col_blocks, size), jnp.float32),
        ),
        in_specs=[smem()] * 2 + [pl.BlockSpec(memory_space=pltpu.HBM)] * 3,
        out_specs=(vmem(), vmem()),
        scratch_shapes=[
            pltpu.VMEM((col_blocks, 8, size), jnp.float32),
            pltpu.VMEM((slots, size, size), jnp.bfloat16),
            pltpu.SMEM(tile_rows.shape, jnp.int32),
            pltpu.SMEM(tile_cols.shape, jnp.int32),
            pltpu.SemaphoreType.DMA((2 + BUILD_STEPS,)),
        ],
        compiler_params=params(2 * slots * size * size + 2 * dst_rows * src_rows),
        cost_estimate=cost(0, 2 * slots * size * size + 2 * dst_rows * src_rows),
        name="build",
    )(place, tile_count.reshape(1), *[pltpu.with_memory_space_constraint(x, pltpu.HBM) for x in (tile_rows, tile_cols, tile_values)])

    gates = []

    def gate_product(block):
        nonlocal memory
        block, memory = tie(block, memory)
        cut = slice(len(gates) * width, (len(gates) + 1) * width)
        gates.append(
            jnp.dot(memory.astype(jnp.bfloat16), hidden_weight[:, cut], preferred_element_type=jnp.float32)
            + hidden_bias[cut]
        )
        return block

    added = move(degree, [(i, i ^ 1) for i in range(n_col)])
    blocks[2], degree = tie(blocks[2], degree)
    bit = 2
    while len(blocks) < n_col - 1:
        blocks.append(ride(blocks[-2], ahead))
        if len(gates) < 2:
            blocks[-2] = gate_product(blocks[-2])
            gates[-1], added = tie(gates[-1], added)
        elif bit < n_col:
            blocks[-2], added = tie(blocks[-2], added)
        blocks.append(ride(blocks[-2], behind))
        if bit < n_col:
            degree = degree + added
            added = move(degree, [(i, i ^ bit) for i in range(n_col)])
            bit *= 2
    upper, lower = blocks[-2][:half], blocks[-1][half:]
    across = (ride(upper, ahead), ride(lower, behind))
    upper, lower, memory = tie(upper, lower, memory)
    gate_product(upper)
    gates[-1], added = tie(gates[-1], added)
    degree = degree + added

    def whole(*shape):
        return pl.BlockSpec(shape, lambda i: (0, 0))

    def product(begin, count, running):
        depth = count * own_rows
        return pl.pallas_call(
            functools.partial(product_kernel, n_row, n_col, begin, count, running is None),
            grid=(1,),
            out_shape=(
                jax.ShapeDtypeStruct((dst_rows, width), jnp.float32),
                jax.ShapeDtypeStruct((own_rows, size), jnp.float32),
            ),
            in_specs=[
                smem(),
                pl.BlockSpec((dst_rows, depth), lambda i: (0, begin // count)),
                whole(col_blocks, size),
            ]
            + [whole(own_rows, width)] * count
            + ([] if running is None else [whole(dst_rows, width)]),
            out_specs=(whole(dst_rows, width), whole(own_rows, size)),
            scratch_shapes=[pltpu.VMEM((depth, width), jnp.bfloat16)],
            compiler_params=params(2 * dst_rows * depth + 4 * depth * width + 8 * dst_rows * width + 2 * MIB),
            cost_estimate=cost(2 * dst_rows * depth * width, 2 * dst_rows * depth + 6 * dst_rows * width),
            name="product",
        )(place, dense, degree, *blocks[begin : begin + count], *([] if running is None else [running]))

    def last_product(at):
        rows = dst_rows // 2
        dtypes = [jnp.float32 if part % 2 else jnp.bfloat16 for part in range(n_row // 2)]
        return pl.pallas_call(
            last_kernel,
            grid=(1,),
            out_shape=tuple(jax.ShapeDtypeStruct((own_rows, width), dtype) for dtype in dtypes),
            in_specs=[
                pl.BlockSpec((rows, own_rows), lambda i: (at, n_col - 1)),
                whole(own_rows, size),
                whole(half, width),
                whole(half, width),
                pl.BlockSpec((rows, width), lambda i: (at, 0)),
            ],
            out_specs=(whole(own_rows, width),) * len(dtypes),
            scratch_shapes=[pltpu.VMEM((own_rows, width), jnp.bfloat16)],
            compiler_params=params(2 * rows * own_rows + 6 * own_rows * width + 8 * rows * width + 2 * MIB),
            cost_estimate=cost(2 * rows * own_rows * width, 2 * rows * own_rows + 6 * rows * width),
            name="last_product",
        )(dense, scale, *across, running)

    running, begin = None, 0
    while begin < n_col - 1:
        count = n_col - 1 if n_col <= 8 else (n_col - begin) // 2
        running, scale = product(begin, count, running)
        begin += count
    sums = {n_row - 1 - at: [part] for at, part in enumerate((*last_product(0), *last_product(1)))}
    for part in range(n_row - 1, 0, -1):
        bit = part & -part
        total = functools.reduce(lambda x, y: x.astype(jnp.float32) + y.astype(jnp.float32), sums[part])
        total = total.astype(jnp.bfloat16)
        sums[part ^ bit].append(lax.ppermute(total, "row", [(i, i ^ bit) for i in range(n_row)]))
    terms = sums[0]

    def own_block(term):
        at = term.shape[0] // own_rows - 1
        return pl.BlockSpec((own_rows, width), lambda i: (at, 0))

    def entire(array):
        return pl.BlockSpec(array.shape, lambda i: (0, 0))

    operands = (
        conv_weight,
        conv_bias.reshape(1, width),
        input_weight,
        input_bias.reshape(1, 3 * width),
        memory,
        *gates,
    )
    return pl.pallas_call(
        tail_kernel,
        grid=(1,),
        out_shape=jax.ShapeDtypeStruct((own_rows, width), jnp.float32),
        in_specs=[entire(array) for array in operands] + [own_block(term) for term in terms],
        out_specs=pl.BlockSpec((own_rows, width), lambda i: (0, 0)),
        compiler_params=params(8 * width * width + 40 * own_rows * width),
        cost_estimate=cost(8 * own_rows * width * width, 8 * width * width + 20 * own_rows * width),
        name="tail",
    )(*operands, *terms)


def solution(mesh):
    placed = (
        P(("row", "col"), None),
        P(("col", "row"), None),
        P("row", "col", None, None, None),
        P("row", "col", None),
        P("row", "col", None),
        P("row", "col"),
        P(),
        P(),
        P(),
        P(),
        P(),
        P(),
    )
    return jax.shard_map(
        on_device, mesh=mesh, in_specs=placed, out_specs=P(("col", "row"), None), check_vma=False
    )
```

```python
import functools

import jax
import jax.numpy as jnp
from jax import lax
from jax.experimental import pallas as pl
from jax.experimental.pallas import tpu as pltpu
from jax.sharding import PartitionSpec as P

norm_epsilon = 1e-06
MIB = 1 << 20
LANES = 128
BUILD_STEPS = 4


def vmem():
    return pl.BlockSpec(memory_space=pltpu.VMEM)


def smem():
    return pl.BlockSpec(memory_space=pltpu.SMEM)


def params(size):
    return pltpu.CompilerParams(vmem_limit_bytes=size + size // 4 + 4 * MIB)


def cost(flops, bytes_accessed):
    return pl.CostEstimate(flops=flops, bytes_accessed=bytes_accessed, transcendentals=0)


def cycle_place(col, n):
    level = lax.shift_right_logical(col, 1)
    return jnp.where((col & 1) == 0, level, n - 1 - level)


def cycle_column(place, n):
    return jnp.where(place < n // 2, 2 * place, 2 * (n - 1 - place) + 1)


def arrival_place(owner, me, n):
    back = lax.rem(cycle_place(me, n) - cycle_place(owner, n) + n, n)
    return jnp.where(back <= n // 2, jnp.maximum(2 * back - 1, 0), 2 * (n - back))


def arrival_owner(place, me, n):
    back = (place + 1) // 2 if place % 2 else (n - place // 2) % n
    return cycle_column(lax.rem(cycle_place(me, n) - back + n, n), n)


def part_place(owner, me, n):
    return n - 1 - (owner ^ me)


def build_kernel(own_rows, n_row, n_col, place_ref, count_ref, rows_any, cols_any, tiles_any, dense_ref, degree_ref, *scratch):
    acc_ref, tiles_ref, rows_ref, cols_ref, sems = scratch
    row_me, col_me = place_ref[0], place_ref[1]
    slots, size = tiles_ref.shape[:2]
    per = own_rows // size
    some = slots // BUILD_STEPS
    small = [
        pltpu.make_async_copy(rows_any, rows_ref, sems.at[0]),
        pltpu.make_async_copy(cols_any, cols_ref, sems.at[1]),
    ]
    large = [
        pltpu.make_async_copy(
            tiles_any.at[0, 0, pl.ds(step * some, some)], tiles_ref.at[pl.ds(step * some, some)], sems.at[2 + step]
        )
        for step in range(BUILD_STEPS)
    ]
    for copy in small + large:
        copy.start()
    dense_ref[...] = jnp.zeros_like(dense_ref)
    acc_ref[...] = jnp.zeros_like(acc_ref)

    def one(slot, carry):
        a, b = rows_ref[0, 0, slot], cols_ref[0, 0, slot]
        row = (part_place(lax.div(a, per), row_me, n_row) * per + lax.rem(a, per)) * size
        col = (arrival_place(lax.div(b, per), col_me, n_col) * per + lax.rem(b, per)) * size
        tile = tiles_ref[slot]
        dense_ref[pl.ds(pl.multiple_of(row, size), size), pl.ds(pl.multiple_of(col, size), size)] = tile
        wide = tile.astype(jnp.float32).reshape(size // 8, 8, size)
        acc_ref[b] += jnp.sum(wide, axis=0)
        return carry

    for copy in small:
        copy.wait()
    for step, copy in enumerate(large):
        copy.wait()
        lax.fori_loop(step * some, jnp.minimum(count_ref[0], (step + 1) * some), one, 0)
    degree_ref[...] = jnp.sum(acc_ref[...], axis=1)


def product_kernel(n_row, n_col, begin, n_blocks, first, *refs):
    place_ref, dense_ref, degree_ref = refs[:3]
    block_refs = refs[3 : 3 + n_blocks]
    sum_refs = () if first else refs[3 + n_blocks : 4 + n_blocks]
    panel_ref = refs[-1]
    sum_out_ref, scale_ref = refs[-3:-1]
    width, size = panel_ref.shape[1], degree_ref.shape[1]
    own_rows = dense_ref.shape[0] // n_row

    def scale(row):
        owner = arrival_owner(begin + row // own_rows, place_ref[1], n_col)
        index = owner * (own_rows // size) + row % own_rows // size
        line = lax.rsqrt(1.0 + degree_ref[pl.ds(index, 1), :])
        return jnp.broadcast_to(line, (size, size)).T

    for place, block in enumerate(block_refs):
        for top in range(0, own_rows, size):
            row = place * own_rows + top
            spread = scale(row)
            for left in range(0, width, LANES):
                cut = slice(left, left + LANES)
                value = block[top : top + size, cut].astype(jnp.float32) * spread
                panel_ref[row : row + size, cut] = value.astype(jnp.bfloat16)
    for top in range(0, own_rows, size):
        scale_ref[top : top + size, :] = scale((n_col - 1 - begin) * own_rows + top)
    for part in range(n_row):
        rows = slice(part * own_rows, (part + 1) * own_rows)
        value = jnp.dot(dense_ref[rows, :], panel_ref[...], preferred_element_type=jnp.float32)
        if not first:
            value = value + sum_refs[0][rows, :]
        sum_out_ref[rows, :] = value


def last_kernel(*refs):
    dense_ref, scale_ref, upper_ref, lower_ref, sum_ref, *out_refs, panel_ref = refs
    own_rows, width = panel_ref.shape
    for block, top in ((upper_ref, 0), (lower_ref, own_rows // 2)):
        rows = slice(top, top + own_rows // 2)
        for left in range(0, width, LANES):
            cut = slice(left, left + LANES)
            panel_ref[rows, cut] = (block[:, cut].astype(jnp.float32) * scale_ref[rows, :]).astype(jnp.bfloat16)
    for place, out_ref in enumerate(out_refs):
        rows = slice(place * own_rows, (place + 1) * own_rows)
        value = jnp.dot(dense_ref[rows, :], panel_ref[...], preferred_element_type=jnp.float32)
        out_ref[...] = (value + sum_ref[rows, :]).astype(out_ref.dtype)


def sigmoid(x):
    return 0.5 * jnp.tanh(0.5 * x) + 0.5


def tail_kernel(n_before, *refs):
    refs = refs[n_before:]
    (conv_ref, conv_bias_ref, input_ref, input_bias_ref, memory_ref), gate_refs, sums = refs[:5], refs[5:8], refs[8:-1]
    out_ref = refs[-1]
    width = memory_ref.shape[1]
    owned = functools.reduce(lambda x, y: x + y, [term[...].astype(jnp.float32) for term in sums])
    spread = jnp.mean(owned * owned, axis=1, keepdims=True) + norm_epsilon
    normed = (owned * lax.rsqrt(spread)).astype(jnp.bfloat16)
    message = jnp.maximum(
        jnp.dot(normed, conv_ref[...], preferred_element_type=jnp.float32) + conv_bias_ref[...], 0.0
    ).astype(jnp.bfloat16)

    def gate(index):
        cut = slice(index * width, (index + 1) * width)
        dots = jnp.dot(message, input_ref[:, cut], preferred_element_type=jnp.float32)
        return dots + input_bias_ref[:, cut], gate_refs[index][...]

    mine, held = gate(0)
    reset = sigmoid(mine + held)
    mine, held = gate(2)
    candidate = jnp.tanh(mine + reset * held)
    mine, held = gate(1)
    update = sigmoid(mine + held)
    out_ref[...] = (1.0 - update) * candidate + update * memory_ref[...]


def on_device(
    features,
    memory,
    tile_values,
    tile_rows,
    tile_cols,
    tile_count,
    conv_weight,
    conv_bias,
    input_weight,
    input_bias,
    hidden_weight,
    hidden_bias,
):
    own_rows, width = features.shape
    n_row, n_col = lax.axis_size("row"), lax.axis_size("col")
    slots, size = tile_values.shape[2], tile_values.shape[3]
    dst_rows, src_rows = own_rows * n_row, own_rows * n_col
    col_blocks = src_rows // size
    place = jnp.stack([lax.axis_index("row"), lax.axis_index("col")]).astype(jnp.int32)

    cycle = [*range(0, n_col, 2), *range(n_col - 1, 0, -2)]
    ahead = [(cycle[at - 1], cycle[at]) for at in range(n_col)]
    behind = [(to, at) for at, to in ahead]

    def tie(*values):
        return lax.optimization_barrier(values)

    def move(block, to):
        return lax.ppermute(block, "col", to)

    blocks = [features, move(features, ahead), move(features, behind)]
    half = own_rows // 2
    dense, degree = pl.pallas_call(
        functools.partial(build_kernel, own_rows, n_row, n_col),
        out_shape=(
            jax.ShapeDtypeStruct((dst_rows, src_rows), jnp.bfloat16),
            jax.ShapeDtypeStruct((col_blocks, size), jnp.float32),
        ),
        in_specs=[smem()] * 2 + [pl.BlockSpec(memory_space=pltpu.HBM)] * 3,
        out_specs=(vmem(), vmem()),
        scratch_shapes=[
            pltpu.VMEM((col_blocks, 8, size), jnp.float32),
            pltpu.VMEM((slots, size, size), jnp.bfloat16),
            pltpu.SMEM(tile_rows.shape, jnp.int32),
            pltpu.SMEM(tile_cols.shape, jnp.int32),
            pltpu.SemaphoreType.DMA((2 + BUILD_STEPS,)),
        ],
        compiler_params=params(2 * slots * size * size + 2 * dst_rows * src_rows),
        cost_estimate=cost(0, 2 * slots * size * size + 2 * dst_rows * src_rows),
        name="build",
    )(place, tile_count.reshape(1), *[pltpu.with_memory_space_constraint(x, pltpu.HBM) for x in (tile_rows, tile_cols, tile_values)])

    gates = []

    def gate_product(block):
        nonlocal memory
        block, memory = tie(block, memory)
        cut = slice(len(gates) * width, (len(gates) + 1) * width)
        gates.append(
            jnp.dot(memory.astype(jnp.bfloat16), hidden_weight[:, cut], preferred_element_type=jnp.float32)
            + hidden_bias[cut]
        )
        return block

    added = move(degree, [(i, i ^ 1) for i in range(n_col)])
    blocks[2], degree = tie(blocks[2], degree)
    bit = 2
    while len(blocks) < n_col - 1:
        blocks.append(move(blocks[-2], ahead))
        if len(gates) < 2:
            blocks[-2] = gate_product(blocks[-2])
            gates[-1], added = tie(gates[-1], added)
        elif bit < n_col:
            blocks[-2], added = tie(blocks[-2], added)
        blocks.append(move(blocks[-2], behind))
        if bit < n_col:
            degree = degree + added
            added = move(degree, [(i, i ^ bit) for i in range(n_col)])
            bit *= 2
    upper, lower = blocks[-2][:half], blocks[-1][half:]
    across = (move(upper, ahead), move(lower, behind))
    upper, lower, memory = tie(upper, lower, memory)
    gate_product(upper)
    gates[-1], added = tie(gates[-1], added)
    degree = degree + added

    def whole(*shape):
        return pl.BlockSpec(shape, lambda i: (0, 0))

    def product(begin, count, running):
        depth = count * own_rows
        return pl.pallas_call(
            functools.partial(product_kernel, n_row, n_col, begin, count, running is None),
            grid=(1,),
            out_shape=(
                jax.ShapeDtypeStruct((dst_rows, width), jnp.float32),
                jax.ShapeDtypeStruct((own_rows, size), jnp.float32),
            ),
            in_specs=[
                smem(),
                pl.BlockSpec((dst_rows, depth), lambda i: (0, begin // count)),
                whole(col_blocks, size),
            ]
            + [whole(own_rows, width)] * count
            + ([] if running is None else [whole(dst_rows, width)]),
            out_specs=(whole(dst_rows, width), whole(own_rows, size)),
            scratch_shapes=[pltpu.VMEM((depth, width), jnp.bfloat16)],
            compiler_params=params(2 * dst_rows * depth + 4 * depth * width + 8 * dst_rows * width + 2 * MIB),
            cost_estimate=cost(2 * dst_rows * depth * width, 2 * dst_rows * depth + 6 * dst_rows * width),
            name="product",
        )(place, dense, degree, *blocks[begin : begin + count], *([] if running is None else [running]))

    def last_product(at):
        rows = dst_rows // 2
        dtypes = [jnp.float32 if part % 2 else jnp.bfloat16 for part in range(n_row // 2)]
        return pl.pallas_call(
            last_kernel,
            grid=(1,),
            out_shape=tuple(jax.ShapeDtypeStruct((own_rows, width), dtype) for dtype in dtypes),
            in_specs=[
                pl.BlockSpec((rows, own_rows), lambda i: (at, n_col - 1)),
                whole(own_rows, size),
                whole(half, width),
                whole(half, width),
                pl.BlockSpec((rows, width), lambda i: (at, 0)),
            ],
            out_specs=(whole(own_rows, width),) * len(dtypes),
            scratch_shapes=[pltpu.VMEM((own_rows, width), jnp.bfloat16)],
            compiler_params=params(2 * rows * own_rows + 6 * own_rows * width + 8 * rows * width + 2 * MIB),
            cost_estimate=cost(2 * rows * own_rows * width, 2 * rows * own_rows + 6 * rows * width),
            name="last_product",
        )(dense, scale, *across, running)

    running, begin = None, 0
    while begin < n_col - 1:
        count = n_col - 1 if n_col <= 8 else (n_col - begin) // 2
        running, scale = product(begin, count, running)
        begin += count
    sums = {n_row - 1 - at: [part] for at, part in enumerate((*last_product(0), *last_product(1)))}
    def total(terms, rows=slice(None)):
        return functools.reduce(lambda x, y: x + y, [term[rows].astype(jnp.float32) for term in terms]).astype(jnp.bfloat16)

    for part in range(n_row - 1, 0, -1):
        bit = part & -part
        over = [(i, i ^ bit) for i in range(n_row)]
        if bit == n_row // 2:
            pieces = [total(sums[part], slice(top, top + half)) for top in (0, half)]
            received = tuple(lax.ppermute(piece, "row", over) for piece in pieces)
        else:
            received = lax.ppermute(total(sums[part]), "row", over)
        sums[part ^ bit].append(received)

    weights = (conv_weight, conv_bias.reshape(1, width), input_weight, input_bias.reshape(1, 3 * width))
    result = None
    for at in range(2):
        part = pl.BlockSpec((half, width), lambda i, at=at: (at, 0))
        terms = [(term[at], whole(half, width)) if isinstance(term, tuple) else (term, part) for term in sums[0]]
        before = [] if result is None else [result]
        result = pl.pallas_call(
            functools.partial(tail_kernel, len(before)),
            grid=(1,),
            out_shape=jax.ShapeDtypeStruct((own_rows, width), jnp.float32),
            in_specs=[pl.BlockSpec(memory_space=pl.ANY)] * len(before)
            + [whole(*weight.shape) for weight in weights]
            + [part] * 4
            + [spec for _, spec in terms],
            out_specs=part,
            input_output_aliases={0: 0} if before else {},
            compiler_params=params(8 * width * width + 40 * own_rows * width),
            cost_estimate=cost(4 * own_rows * width * width, 8 * width * width + 10 * own_rows * width),
            name="tail",
        )(*before, *weights, memory, *gates, *[term for term, _ in terms])
    return result


def solution(mesh):
    placed = (
        P(("row", "col"), None),
        P(("col", "row"), None),
        P("row", "col", None, None, None),
        P("row", "col", None),
        P("row", "col", None),
        P("row", "col"),
        P(),
        P(),
        P(),
        P(),
        P(),
        P(),
    )
    return jax.shard_map(
        on_device, mesh=mesh, in_specs=placed, out_specs=P(("col", "row"), None), check_vma=False
    )
```

```python
import functools

import jax
import jax.numpy as jnp
from jax import lax
from jax.experimental import pallas as pl
from jax.experimental.pallas import tpu as pltpu
from jax.sharding import PartitionSpec as P

norm_epsilon = 1e-06
MIB = 1 << 20
LANES = 128
BUILD_STEPS = 4


def vmem():
    return pl.BlockSpec(memory_space=pltpu.VMEM)


def smem():
    return pl.BlockSpec(memory_space=pltpu.SMEM)


def params(size):
    return pltpu.CompilerParams(vmem_limit_bytes=size + size // 4 + 4 * MIB)


def cost(flops, bytes_accessed):
    return pl.CostEstimate(flops=flops, bytes_accessed=bytes_accessed, transcendentals=0)


def cycle_place(col, n):
    level = lax.shift_right_logical(col, 1)
    return jnp.where((col & 1) == 0, level, n - 1 - level)


def cycle_column(place, n):
    return jnp.where(place < n // 2, 2 * place, 2 * (n - 1 - place) + 1)


def arrival_place(owner, me, n):
    back = lax.rem(cycle_place(me, n) - cycle_place(owner, n) + n, n)
    return jnp.where(back <= n // 2, jnp.maximum(2 * back - 1, 0), 2 * (n - back))


def arrival_owner(place, me, n):
    back = (place + 1) // 2 if place % 2 else (n - place // 2) % n
    return cycle_column(lax.rem(cycle_place(me, n) - back + n, n), n)


def part_place(owner, me, n):
    return n - 1 - (owner ^ me)


def build_kernel(own_rows, n_row, n_col, place_ref, count_ref, rows_any, cols_any, tiles_any, dense_ref, degree_ref, *scratch):
    acc_ref, tiles_ref, rows_ref, cols_ref, sems = scratch
    row_me, col_me = place_ref[0], place_ref[1]
    slots, size = tiles_ref.shape[:2]
    per = own_rows // size
    some = slots // BUILD_STEPS
    small = [
        pltpu.make_async_copy(rows_any, rows_ref, sems.at[0]),
        pltpu.make_async_copy(cols_any, cols_ref, sems.at[1]),
    ]
    large = [
        pltpu.make_async_copy(
            tiles_any.at[0, 0, pl.ds(step * some, some)], tiles_ref.at[pl.ds(step * some, some)], sems.at[2 + step]
        )
        for step in range(BUILD_STEPS)
    ]
    for copy in small + large:
        copy.start()
    dense_ref[...] = jnp.zeros_like(dense_ref)
    acc_ref[...] = jnp.zeros_like(acc_ref)

    def one(slot, carry):
        a, b = rows_ref[0, 0, slot], cols_ref[0, 0, slot]
        row = (part_place(lax.div(a, per), row_me, n_row) * per + lax.rem(a, per)) * size
        col = (arrival_place(lax.div(b, per), col_me, n_col) * per + lax.rem(b, per)) * size
        tile = tiles_ref[slot]
        dense_ref[pl.ds(pl.multiple_of(row, size), size), pl.ds(pl.multiple_of(col, size), size)] = tile
        wide = tile.astype(jnp.float32).reshape(size // 8, 8, size)
        acc_ref[b] += jnp.sum(wide, axis=0)
        return carry

    for copy in small:
        copy.wait()
    for step, copy in enumerate(large):
        copy.wait()
        lax.fori_loop(step * some, jnp.minimum(count_ref[0], (step + 1) * some), one, 0)
    degree_ref[...] = jnp.sum(acc_ref[...], axis=1)


def product_kernel(n_row, n_col, begin, n_blocks, first, *refs):
    place_ref, dense_ref, degree_ref = refs[:3]
    block_refs = refs[3 : 3 + n_blocks]
    sum_refs = () if first else refs[3 + n_blocks : 4 + n_blocks]
    panel_ref = refs[-1]
    sum_out_ref, scale_ref = refs[-3:-1]
    width, size = panel_ref.shape[1], degree_ref.shape[1]
    own_rows = dense_ref.shape[0] // n_row

    def scale(row):
        owner = arrival_owner(begin + row // own_rows, place_ref[1], n_col)
        index = owner * (own_rows // size) + row % own_rows // size
        line = lax.rsqrt(1.0 + degree_ref[pl.ds(index, 1), :])
        return jnp.broadcast_to(line, (size, size)).T

    for place, block in enumerate(block_refs):
        for top in range(0, own_rows, size):
            row = place * own_rows + top
            spread = scale(row)
            for left in range(0, width, LANES):
                cut = slice(left, left + LANES)
                value = block[top : top + size, cut].astype(jnp.float32) * spread
                panel_ref[row : row + size, cut] = value.astype(jnp.bfloat16)
    for top in range(0, own_rows, size):
        scale_ref[top : top + size, :] = scale((n_col - 1 - begin) * own_rows + top)
    for part in range(n_row):
        rows = slice(part * own_rows, (part + 1) * own_rows)
        value = jnp.dot(dense_ref[rows, :], panel_ref[...], preferred_element_type=jnp.float32)
        if not first:
            value = value + sum_refs[0][rows, :]
        sum_out_ref[rows, :] = value


def last_kernel(*refs):
    dense_ref, scale_ref, upper_ref, lower_ref, sum_ref, *out_refs, panel_ref = refs
    own_rows, width = panel_ref.shape
    for block, top in ((upper_ref, 0), (lower_ref, own_rows // 2)):
        rows = slice(top, top + own_rows // 2)
        for left in range(0, width, LANES):
            cut = slice(left, left + LANES)
            panel_ref[rows, cut] = (block[:, cut].astype(jnp.float32) * scale_ref[rows, :]).astype(jnp.bfloat16)
    end = 0
    for out_ref in out_refs:
        rows = slice(end, end + out_ref.shape[0])
        end = rows.stop
        value = jnp.dot(dense_ref[rows, :], panel_ref[...], preferred_element_type=jnp.float32)
        out_ref[...] = (value + sum_ref[rows, :]).astype(out_ref.dtype)


def sigmoid(x):
    return 0.5 * jnp.tanh(0.5 * x) + 0.5


def tail_kernel(n_before, *refs):
    refs = refs[n_before:]
    (conv_ref, conv_bias_ref, input_ref, input_bias_ref, memory_ref), gate_refs, sums = refs[:5], refs[5:8], refs[8:-1]
    out_ref = refs[-1]
    width = memory_ref.shape[1]
    owned = functools.reduce(lambda x, y: x + y, [term[...].astype(jnp.float32) for term in sums])
    spread = jnp.mean(owned * owned, axis=1, keepdims=True) + norm_epsilon
    normed = (owned * lax.rsqrt(spread)).astype(jnp.bfloat16)
    message = jnp.maximum(
        jnp.dot(normed, conv_ref[...], preferred_element_type=jnp.float32) + conv_bias_ref[...], 0.0
    ).astype(jnp.bfloat16)

    def gate(index):
        cut = slice(index * width, (index + 1) * width)
        dots = jnp.dot(message, input_ref[:, cut], preferred_element_type=jnp.float32)
        return dots + input_bias_ref[:, cut], gate_refs[index][...]

    mine, held = gate(0)
    reset = sigmoid(mine + held)
    mine, held = gate(2)
    candidate = jnp.tanh(mine + reset * held)
    mine, held = gate(1)
    update = sigmoid(mine + held)
    out_ref[...] = (1.0 - update) * candidate + update * memory_ref[...]


def on_device(
    features,
    memory,
    tile_values,
    tile_rows,
    tile_cols,
    tile_count,
    conv_weight,
    conv_bias,
    input_weight,
    input_bias,
    hidden_weight,
    hidden_bias,
):
    own_rows, width = features.shape
    n_row, n_col = lax.axis_size("row"), lax.axis_size("col")
    slots, size = tile_values.shape[2], tile_values.shape[3]
    dst_rows, src_rows = own_rows * n_row, own_rows * n_col
    col_blocks = src_rows // size
    place = jnp.stack([lax.axis_index("row"), lax.axis_index("col")]).astype(jnp.int32)

    cycle = [*range(0, n_col, 2), *range(n_col - 1, 0, -2)]
    ahead = [(cycle[at - 1], cycle[at]) for at in range(n_col)]
    behind = [(to, at) for at, to in ahead]

    def tie(*values):
        return lax.optimization_barrier(values)

    def move(block, to):
        return lax.ppermute(block, "col", to)

    blocks = [features, move(features, ahead), move(features, behind)]
    half = own_rows // 2
    dense, degree = pl.pallas_call(
        functools.partial(build_kernel, own_rows, n_row, n_col),
        out_shape=(
            jax.ShapeDtypeStruct((dst_rows, src_rows), jnp.bfloat16),
            jax.ShapeDtypeStruct((col_blocks, size), jnp.float32),
        ),
        in_specs=[smem()] * 2 + [pl.BlockSpec(memory_space=pltpu.HBM)] * 3,
        out_specs=(vmem(), vmem()),
        scratch_shapes=[
            pltpu.VMEM((col_blocks, 8, size), jnp.float32),
            pltpu.VMEM((slots, size, size), jnp.bfloat16),
            pltpu.SMEM(tile_rows.shape, jnp.int32),
            pltpu.SMEM(tile_cols.shape, jnp.int32),
            pltpu.SemaphoreType.DMA((2 + BUILD_STEPS,)),
        ],
        compiler_params=params(2 * slots * size * size + 2 * dst_rows * src_rows),
        cost_estimate=cost(0, 2 * slots * size * size + 2 * dst_rows * src_rows),
        name="build",
    )(place, tile_count.reshape(1), *[pltpu.with_memory_space_constraint(x, pltpu.HBM) for x in (tile_rows, tile_cols, tile_values)])

    gates = []

    def gate_product(block):
        nonlocal memory
        block, memory = tie(block, memory)
        cut = slice(len(gates) * width, (len(gates) + 1) * width)
        gates.append(
            jnp.dot(memory.astype(jnp.bfloat16), hidden_weight[:, cut], preferred_element_type=jnp.float32)
            + hidden_bias[cut]
        )
        return block

    added = move(degree, [(i, i ^ 1) for i in range(n_col)])
    blocks[2], degree = tie(blocks[2], degree)
    bit = 2
    while len(blocks) < n_col - 1:
        blocks.append(move(blocks[-2], ahead))
        if len(gates) < 2:
            blocks[-2] = gate_product(blocks[-2])
            gates[-1], added = tie(gates[-1], added)
        elif bit < n_col:
            blocks[-2], added = tie(blocks[-2], added)
        blocks.append(move(blocks[-2], behind))
        if bit < n_col:
            degree = degree + added
            added = move(degree, [(i, i ^ bit) for i in range(n_col)])
            bit *= 2
    upper, lower = blocks[-2][:half], blocks[-1][half:]
    across = (move(upper, ahead), move(lower, behind))
    upper, lower, memory = tie(upper, lower, memory)
    gate_product(upper)
    gates[-1], added = tie(gates[-1], added)
    degree = degree + added

    def whole(*shape):
        return pl.BlockSpec(shape, lambda i: (0, 0))

    def product(begin, count, running):
        depth = count * own_rows
        return pl.pallas_call(
            functools.partial(product_kernel, n_row, n_col, begin, count, running is None),
            grid=(1,),
            out_shape=(
                jax.ShapeDtypeStruct((dst_rows, width), jnp.float32),
                jax.ShapeDtypeStruct((own_rows, size), jnp.float32),
            ),
            in_specs=[
                smem(),
                pl.BlockSpec((dst_rows, depth), lambda i: (0, begin // count)),
                whole(col_blocks, size),
            ]
            + [whole(own_rows, width)] * count
            + ([] if running is None else [whole(dst_rows, width)]),
            out_specs=(whole(dst_rows, width), whole(own_rows, size)),
            scratch_shapes=[pltpu.VMEM((depth, width), jnp.bfloat16)],
            compiler_params=params(2 * dst_rows * depth + 4 * depth * width + 8 * dst_rows * width + 2 * MIB),
            cost_estimate=cost(2 * dst_rows * depth * width, 2 * dst_rows * depth + 6 * dst_rows * width),
            name="product",
        )(place, dense, degree, *blocks[begin : begin + count], *([] if running is None else [running]))

    def last_product(at, height):
        rows = dst_rows // 2
        dtypes = [jnp.float32 if top // own_rows % 2 else jnp.bfloat16 for top in range(0, rows, height)]
        return pl.pallas_call(
            last_kernel,
            grid=(1,),
            out_shape=tuple(jax.ShapeDtypeStruct((height, width), dtype) for dtype in dtypes),
            in_specs=[
                pl.BlockSpec((rows, own_rows), lambda i: (at, n_col - 1)),
                whole(own_rows, size),
                whole(half, width),
                whole(half, width),
                pl.BlockSpec((rows, width), lambda i: (at, 0)),
            ],
            out_specs=(whole(height, width),) * len(dtypes),
            scratch_shapes=[pltpu.VMEM((own_rows, width), jnp.bfloat16)],
            compiler_params=params(2 * rows * own_rows + 6 * own_rows * width + 8 * rows * width + 2 * MIB),
            cost_estimate=cost(2 * rows * own_rows * width, 2 * rows * own_rows + 6 * rows * width),
            name="last_product",
        )(dense, scale, *across, running)

    running, begin = None, 0
    while begin < n_col - 1:
        count = n_col - 1 if n_col <= 8 else (n_col - begin) // 2
        running, scale = product(begin, count, running)
        begin += count
    def total(terms):
        return functools.reduce(lambda x, y: x + y, [term.astype(jnp.float32) for term in terms]).astype(jnp.bfloat16)

    def send(value, bit):
        return lax.ppermute(value, "row", [(i, i ^ bit) for i in range(n_row)])

    def halve(sums, end):
        for part in sorted(sums, reverse=True):
            if part > end:
                sums[part & (part - 1)].append(send(total(sums[part]), part & -part))
        return sums[end]

    middle = n_row // 2
    upper, lower = last_product(0, half), last_product(1, own_rows)
    sums = [{n_row - 1 - at: [upper[2 * at + which]] for at in range(middle)} for which in range(2)]
    given = [total(halve(each, middle)) for each in sums]
    given[0], *lower = tie(given[0], *lower)
    arrived = [send(value, middle) for value in given]
    terms = halve({middle - 1 - at: [part] for at, part in enumerate(lower)}, 0)

    weights = (conv_weight, conv_bias.reshape(1, width), input_weight, input_bias.reshape(1, 3 * width))
    result = None
    for at in range(2):
        part = pl.BlockSpec((half, width), lambda i, at=at: (at, 0))
        operands = [(term, part) for term in terms] + [(arrived[at], whole(half, width))]
        before = [] if result is None else [result]
        result = pl.pallas_call(
            functools.partial(tail_kernel, len(before)),
            grid=(1,),
            out_shape=jax.ShapeDtypeStruct((own_rows, width), jnp.float32),
            in_specs=[pl.BlockSpec(memory_space=pl.ANY)] * len(before)
            + [whole(*weight.shape) for weight in weights]
            + [part] * 4
            + [spec for _, spec in operands],
            out_specs=part,
            input_output_aliases={0: 0} if before else {},
            compiler_params=params(8 * width * width + 40 * own_rows * width),
            cost_estimate=cost(4 * own_rows * width * width, 8 * width * width + 10 * own_rows * width),
            name="tail",
        )(*before, *weights, memory, *gates, *[term for term, _ in operands])
    return result


def solution(mesh):
    placed = (
        P(("row", "col"), None),
        P(("col", "row"), None),
        P("row", "col", None, None, None),
        P("row", "col", None),
        P("row", "col", None),
        P("row", "col"),
        P(),
        P(),
        P(),
        P(),
        P(),
        P(),
    )
    return jax.shard_map(
        on_device, mesh=mesh, in_specs=placed, out_specs=P(("col", "row"), None), check_vma=False
    )
```

```python
import functools

import jax
import jax.numpy as jnp
from jax import lax
from jax.experimental import pallas as pl
from jax.experimental.pallas import tpu as pltpu
from jax.sharding import PartitionSpec as P

norm_epsilon = 1e-06
MIB = 1 << 20
LANES = 128
BUILD_STEPS = 4


def vmem():
    return pl.BlockSpec(memory_space=pltpu.VMEM)


def smem():
    return pl.BlockSpec(memory_space=pltpu.SMEM)


def params(size):
    return pltpu.CompilerParams(vmem_limit_bytes=size + size // 4 + 4 * MIB)


def cost(flops, bytes_accessed):
    return pl.CostEstimate(flops=flops, bytes_accessed=bytes_accessed, transcendentals=0)


def cycle_place(col, n):
    level = lax.shift_right_logical(col, 1)
    return jnp.where((col & 1) == 0, level, n - 1 - level)


def cycle_column(place, n):
    return jnp.where(place < n // 2, 2 * place, 2 * (n - 1 - place) + 1)


def arrival_place(owner, me, n):
    back = lax.rem(cycle_place(me, n) - cycle_place(owner, n) + n, n)
    return jnp.where(back <= n // 2, jnp.maximum(2 * back - 1, 0), 2 * (n - back))


def arrival_owner(place, me, n):
    back = (place + 1) // 2 if place % 2 else (n - place // 2) % n
    return cycle_column(lax.rem(cycle_place(me, n) - back + n, n), n)


def part_place(owner, me, n):
    return n - 1 - (owner ^ me)


def build_kernel(own_rows, n_row, n_col, place_ref, count_ref, rows_any, cols_any, tiles_any, dense_ref, degree_ref, *scratch):
    acc_ref, tiles_ref, rows_ref, cols_ref, sems = scratch
    row_me, col_me = place_ref[0], place_ref[1]
    slots, size = tiles_ref.shape[:2]
    per = own_rows // size
    some = slots // BUILD_STEPS
    small = [
        pltpu.make_async_copy(rows_any, rows_ref, sems.at[0]),
        pltpu.make_async_copy(cols_any, cols_ref, sems.at[1]),
    ]
    large = [
        pltpu.make_async_copy(
            tiles_any.at[0, 0, pl.ds(step * some, some)], tiles_ref.at[pl.ds(step * some, some)], sems.at[2 + step]
        )
        for step in range(BUILD_STEPS)
    ]
    for copy in small + large:
        copy.start()
    dense_ref[...] = jnp.zeros_like(dense_ref)
    acc_ref[...] = jnp.zeros_like(acc_ref)

    def one(slot, carry):
        a, b = rows_ref[0, 0, slot], cols_ref[0, 0, slot]
        row = (part_place(lax.div(a, per), row_me, n_row) * per + lax.rem(a, per)) * size
        col = (arrival_place(lax.div(b, per), col_me, n_col) * per + lax.rem(b, per)) * size
        tile = tiles_ref[slot]
        dense_ref[pl.ds(pl.multiple_of(row, size), size), pl.ds(pl.multiple_of(col, size), size)] = tile
        wide = tile.astype(jnp.float32).reshape(size // 8, 8, size)
        acc_ref[b] += jnp.sum(wide, axis=0)
        return carry

    for copy in small:
        copy.wait()
    for step, copy in enumerate(large):
        copy.wait()
        lax.fori_loop(step * some, jnp.minimum(count_ref[0], (step + 1) * some), one, 0)
    degree_ref[...] = jnp.sum(acc_ref[...], axis=1)


def product_kernel(n_row, n_col, begin, n_blocks, first, *refs):
    place_ref, dense_ref, degree_ref = refs[:3]
    block_refs = refs[3 : 3 + n_blocks]
    sum_refs = () if first else refs[3 + n_blocks : 4 + n_blocks]
    panel_ref = refs[-1]
    sum_out_ref, scale_ref = refs[-3:-1]
    width, size = panel_ref.shape[1], degree_ref.shape[1]
    own_rows = dense_ref.shape[0] // n_row

    def scale(row):
        owner = arrival_owner(begin + row // own_rows, place_ref[1], n_col)
        index = owner * (own_rows // size) + row % own_rows // size
        line = lax.rsqrt(1.0 + degree_ref[pl.ds(index, 1), :])
        return jnp.broadcast_to(line, (size, size)).T

    for place, block in enumerate(block_refs):
        for top in range(0, own_rows, size):
            row = place * own_rows + top
            spread = scale(row)
            for left in range(0, width, LANES):
                cut = slice(left, left + LANES)
                value = block[top : top + size, cut].astype(jnp.float32) * spread
                panel_ref[row : row + size, cut] = value.astype(jnp.bfloat16)
    for top in range(0, own_rows, size):
        scale_ref[top : top + size, :] = scale((n_col - 1 - begin) * own_rows + top)
    for part in range(n_row):
        rows = slice(part * own_rows, (part + 1) * own_rows)
        value = jnp.dot(dense_ref[rows, :], panel_ref[...], preferred_element_type=jnp.float32)
        if not first:
            value = value + sum_refs[0][rows, :]
        sum_out_ref[rows, :] = value


def last_kernel(*refs):
    dense_ref, scale_ref, upper_ref, lower_ref, sum_ref, *out_refs, panel_ref = refs
    own_rows, width = panel_ref.shape
    for block, top in ((upper_ref, 0), (lower_ref, own_rows // 2)):
        rows = slice(top, top + own_rows // 2)
        for left in range(0, width, LANES):
            cut = slice(left, left + LANES)
            panel_ref[rows, cut] = (block[:, cut].astype(jnp.float32) * scale_ref[rows, :]).astype(jnp.bfloat16)
    end = 0
    for out_ref in out_refs:
        rows = slice(end, end + out_ref.shape[0])
        end = rows.stop
        value = jnp.dot(dense_ref[rows, :], panel_ref[...], preferred_element_type=jnp.float32)
        out_ref[...] = (value + sum_ref[rows, :]).astype(out_ref.dtype)


def sigmoid(x):
    return 0.5 * jnp.tanh(0.5 * x) + 0.5


def tail_kernel(n_before, *refs):
    refs = refs[n_before:]
    (conv_ref, conv_bias_ref, input_ref, input_bias_ref, memory_ref), gate_refs, sums = refs[:5], refs[5:8], refs[8:-1]
    out_ref = refs[-1]
    width = memory_ref.shape[1]
    owned = functools.reduce(lambda x, y: x + y, [term[...].astype(jnp.float32) for term in sums])
    spread = jnp.mean(owned * owned, axis=1, keepdims=True) + norm_epsilon
    normed = (owned * lax.rsqrt(spread)).astype(jnp.bfloat16)
    message = jnp.maximum(
        jnp.dot(normed, conv_ref[...], preferred_element_type=jnp.float32) + conv_bias_ref[...], 0.0
    ).astype(jnp.bfloat16)

    def gate(index):
        cut = slice(index * width, (index + 1) * width)
        dots = jnp.dot(message, input_ref[:, cut], preferred_element_type=jnp.float32)
        return dots + input_bias_ref[:, cut], gate_refs[index][...]

    mine, held = gate(0)
    reset = sigmoid(mine + held)
    mine, held = gate(2)
    candidate = jnp.tanh(mine + reset * held)
    mine, held = gate(1)
    update = sigmoid(mine + held)
    out_ref[...] = (1.0 - update) * candidate + update * memory_ref[...]


def on_device(
    features,
    memory,
    tile_values,
    tile_rows,
    tile_cols,
    tile_count,
    conv_weight,
    conv_bias,
    input_weight,
    input_bias,
    hidden_weight,
    hidden_bias,
):
    own_rows, width = features.shape
    n_row, n_col = lax.axis_size("row"), lax.axis_size("col")
    slots, size = tile_values.shape[2], tile_values.shape[3]
    dst_rows, src_rows = own_rows * n_row, own_rows * n_col
    col_blocks = src_rows // size
    place = jnp.stack([lax.axis_index("row"), lax.axis_index("col")]).astype(jnp.int32)

    cycle = [*range(0, n_col, 2), *range(n_col - 1, 0, -2)]
    ahead = [(cycle[at - 1], cycle[at]) for at in range(n_col)]
    behind = [(to, at) for at, to in ahead]

    def tie(*values):
        return lax.optimization_barrier(values)

    def move(block, to):
        return lax.ppermute(block, "col", to)

    blocks = [features, move(features, ahead), move(features, behind)]
    half = own_rows // 2
    dense, degree = pl.pallas_call(
        functools.partial(build_kernel, own_rows, n_row, n_col),
        out_shape=(
            jax.ShapeDtypeStruct((dst_rows, src_rows), jnp.bfloat16),
            jax.ShapeDtypeStruct((col_blocks, size), jnp.float32),
        ),
        in_specs=[smem()] * 2 + [pl.BlockSpec(memory_space=pltpu.HBM)] * 3,
        out_specs=(vmem(), vmem()),
        scratch_shapes=[
            pltpu.VMEM((col_blocks, 8, size), jnp.float32),
            pltpu.VMEM((slots, size, size), jnp.bfloat16),
            pltpu.SMEM(tile_rows.shape, jnp.int32),
            pltpu.SMEM(tile_cols.shape, jnp.int32),
            pltpu.SemaphoreType.DMA((2 + BUILD_STEPS,)),
        ],
        compiler_params=params(2 * slots * size * size + 2 * dst_rows * src_rows),
        cost_estimate=cost(0, 2 * slots * size * size + 2 * dst_rows * src_rows),
        name="build",
    )(place, tile_count.reshape(1), *[pltpu.with_memory_space_constraint(x, pltpu.HBM) for x in (tile_rows, tile_cols, tile_values)])

    gates = []

    def gate_product(block):
        nonlocal memory
        block, memory = tie(block, memory)
        cut = slice(len(gates) * width, (len(gates) + 1) * width)
        gates.append(
            jnp.dot(memory.astype(jnp.bfloat16), hidden_weight[:, cut], preferred_element_type=jnp.float32)
            + hidden_bias[cut]
        )
        return block

    added = move(degree, [(i, i ^ 1) for i in range(n_col)])
    blocks[2], degree = tie(blocks[2], degree)
    bit = 2
    while len(blocks) < n_col - 1:
        blocks.append(move(blocks[-2], ahead))
        if len(gates) < 2:
            blocks[-2] = gate_product(blocks[-2])
            gates[-1], added = tie(gates[-1], added)
        elif bit < n_col:
            blocks[-2], added = tie(blocks[-2], added)
        blocks.append(move(blocks[-2], behind))
        if bit < n_col:
            degree = degree + added
            added = move(degree, [(i, i ^ bit) for i in range(n_col)])
            bit *= 2
    ahead_two, behind_two = ([(at, dict(way)[to]) for at, to in way] for way in (ahead, behind))
    upper, lower = blocks[-4][:half], blocks[-3][half:]
    across = (move(upper, ahead_two), move(lower, behind_two))
    upper, lower = blocks[-2], blocks[-1]
    upper, lower, memory = tie(upper, lower, memory)
    gate_product(upper)
    gates[-1], added = tie(gates[-1], added)
    degree = degree + added

    def whole(*shape):
        return pl.BlockSpec(shape, lambda i: (0, 0))

    def product(begin, count, running):
        depth = count * own_rows
        return pl.pallas_call(
            functools.partial(product_kernel, n_row, n_col, begin, count, running is None),
            grid=(1,),
            out_shape=(
                jax.ShapeDtypeStruct((dst_rows, width), jnp.float32),
                jax.ShapeDtypeStruct((own_rows, size), jnp.float32),
            ),
            in_specs=[
                smem(),
                pl.BlockSpec((dst_rows, depth), lambda i: (0, begin // count)),
                whole(col_blocks, size),
            ]
            + [whole(own_rows, width)] * count
            + ([] if running is None else [whole(dst_rows, width)]),
            out_specs=(whole(dst_rows, width), whole(own_rows, size)),
            scratch_shapes=[pltpu.VMEM((depth, width), jnp.bfloat16)],
            compiler_params=params(2 * dst_rows * depth + 4 * depth * width + 8 * dst_rows * width + 2 * MIB),
            cost_estimate=cost(2 * dst_rows * depth * width, 2 * dst_rows * depth + 6 * dst_rows * width),
            name="product",
        )(place, dense, degree, *blocks[begin : begin + count], *([] if running is None else [running]))

    def last_product(at, height):
        rows = dst_rows // 2
        dtypes = [jnp.float32 if top // own_rows % 2 else jnp.bfloat16 for top in range(0, rows, height)]
        return pl.pallas_call(
            last_kernel,
            grid=(1,),
            out_shape=tuple(jax.ShapeDtypeStruct((height, width), dtype) for dtype in dtypes),
            in_specs=[
                pl.BlockSpec((rows, own_rows), lambda i: (at, n_col - 1)),
                whole(own_rows, size),
                whole(half, width),
                whole(half, width),
                pl.BlockSpec((rows, width), lambda i: (at, 0)),
            ],
            out_specs=(whole(height, width),) * len(dtypes),
            scratch_shapes=[pltpu.VMEM((own_rows, width), jnp.bfloat16)],
            compiler_params=params(2 * rows * own_rows + 6 * own_rows * width + 8 * rows * width + 2 * MIB),
            cost_estimate=cost(2 * rows * own_rows * width, 2 * rows * own_rows + 6 * rows * width),
            name="last_product",
        )(dense, scale, *across, running)

    running, begin = None, 0
    while begin < n_col - 1:
        count = n_col - 1 if n_col <= 8 else (n_col - begin) // 2
        running, scale = product(begin, count, running)
        begin += count
    def total(terms):
        return functools.reduce(lambda x, y: x + y, [term.astype(jnp.float32) for term in terms]).astype(jnp.bfloat16)

    def send(value, bit):
        return lax.ppermute(value, "row", [(i, i ^ bit) for i in range(n_row)])

    def halve(sums, end):
        for part in sorted(sums, reverse=True):
            if part > end:
                sums[part & (part - 1)].append(send(total(sums[part]), part & -part))
        return sums[end]

    middle = n_row // 2
    upper, lower = last_product(0, half), last_product(1, own_rows)
    sums = [{n_row - 1 - at: [upper[2 * at + which]] for at in range(middle)} for which in range(2)]
    given = [total(halve(each, middle)) for each in sums]
    given[0], *lower = tie(given[0], *lower)
    arrived = [send(value, middle) for value in given]
    terms = halve({middle - 1 - at: [part] for at, part in enumerate(lower)}, 0)

    weights = (conv_weight, conv_bias.reshape(1, width), input_weight, input_bias.reshape(1, 3 * width))
    result = None
    for at in range(2):
        part = pl.BlockSpec((half, width), lambda i, at=at: (at, 0))
        operands = [(term, part) for term in terms] + [(arrived[at], whole(half, width))]
        before = [] if result is None else [result]
        result = pl.pallas_call(
            functools.partial(tail_kernel, len(before)),
            grid=(1,),
            out_shape=jax.ShapeDtypeStruct((own_rows, width), jnp.float32),
            in_specs=[pl.BlockSpec(memory_space=pl.ANY)] * len(before)
            + [whole(*weight.shape) for weight in weights]
            + [part] * 4
            + [spec for _, spec in operands],
            out_specs=part,
            input_output_aliases={0: 0} if before else {},
            compiler_params=params(8 * width * width + 40 * own_rows * width),
            cost_estimate=cost(4 * own_rows * width * width, 8 * width * width + 10 * own_rows * width),
            name="tail",
        )(*before, *weights, memory, *gates, *[term for term, _ in operands])
    return result


def solution(mesh):
    placed = (
        P(("row", "col"), None),
        P(("col", "row"), None),
        P("row", "col", None, None, None),
        P("row", "col", None),
        P("row", "col", None),
        P("row", "col"),
        P(),
        P(),
        P(),
        P(),
        P(),
        P(),
    )
    return jax.shard_map(
        on_device, mesh=mesh, in_specs=placed, out_specs=P(("col", "row"), None), check_vma=False
    )
```

```python
import functools

import jax
import jax.numpy as jnp
from jax import lax
from jax.experimental import pallas as pl
from jax.experimental.pallas import tpu as pltpu
from jax.sharding import PartitionSpec as P

norm_epsilon = 1e-06
MIB = 1 << 20
LANES = 128
BUILD_STEPS = 4


def vmem():
    return pl.BlockSpec(memory_space=pltpu.VMEM)


def smem():
    return pl.BlockSpec(memory_space=pltpu.SMEM)


def params(size):
    return pltpu.CompilerParams(vmem_limit_bytes=size + size // 4 + 4 * MIB)


def cost(flops, bytes_accessed):
    return pl.CostEstimate(flops=flops, bytes_accessed=bytes_accessed, transcendentals=0)


def cycle_place(col, n):
    level = lax.shift_right_logical(col, 1)
    return jnp.where((col & 1) == 0, level, n - 1 - level)


def cycle_column(place, n):
    return jnp.where(place < n // 2, 2 * place, 2 * (n - 1 - place) + 1)


def arrival_place(owner, me, n):
    back = lax.rem(cycle_place(me, n) - cycle_place(owner, n) + n, n)
    return jnp.where(back <= n // 2, jnp.maximum(2 * back - 1, 0), 2 * (n - back))


def arrival_owner(place, me, n):
    back = (place + 1) // 2 if place % 2 else (n - place // 2) % n
    return cycle_column(lax.rem(cycle_place(me, n) - back + n, n), n)


def part_place(owner, me, n):
    return n - 1 - (owner ^ me)


def build_kernel(own_rows, n_row, n_col, place_ref, count_ref, rows_any, cols_any, tiles_any, dense_ref, degree_ref, *scratch):
    acc_ref, tiles_ref, rows_ref, cols_ref, sems = scratch
    row_me, col_me = place_ref[0], place_ref[1]
    slots, size = tiles_ref.shape[:2]
    per = own_rows // size
    some = slots // BUILD_STEPS
    small = [
        pltpu.make_async_copy(rows_any, rows_ref, sems.at[0]),
        pltpu.make_async_copy(cols_any, cols_ref, sems.at[1]),
    ]
    large = [
        pltpu.make_async_copy(
            tiles_any.at[0, 0, pl.ds(step * some, some)], tiles_ref.at[pl.ds(step * some, some)], sems.at[2 + step]
        )
        for step in range(BUILD_STEPS)
    ]
    for copy in small + large:
        copy.start()
    dense_ref[...] = jnp.zeros_like(dense_ref)
    acc_ref[...] = jnp.zeros_like(acc_ref)

    def one(slot, carry):
        a, b = rows_ref[0, 0, slot], cols_ref[0, 0, slot]
        row = (part_place(lax.div(a, per), row_me, n_row) * per + lax.rem(a, per)) * size
        col = (arrival_place(lax.div(b, per), col_me, n_col) * per + lax.rem(b, per)) * size
        tile = tiles_ref[slot]
        dense_ref[pl.ds(pl.multiple_of(row, size), size), pl.ds(pl.multiple_of(col, size), size)] = tile
        wide = tile.astype(jnp.float32).reshape(size // 8, 8, size)
        acc_ref[b] += jnp.sum(wide, axis=0)
        return carry

    for copy in small:
        copy.wait()
    for step, copy in enumerate(large):
        copy.wait()
        lax.fori_loop(step * some, jnp.minimum(count_ref[0], (step + 1) * some), one, 0)
    degree_ref[...] = jnp.sum(acc_ref[...], axis=1)


def product_kernel(n_row, n_col, begin, n_blocks, first, *refs):
    place_ref, dense_ref, degree_ref = refs[:3]
    block_refs = refs[3 : 3 + n_blocks]
    sum_refs = () if first else refs[3 + n_blocks : 4 + n_blocks]
    panel_ref = refs[-1]
    sum_out_ref, scale_ref = refs[-3:-1]
    width, size = panel_ref.shape[1], degree_ref.shape[1]
    own_rows = dense_ref.shape[0] // n_row

    def scale(row):
        owner = arrival_owner(begin + row // own_rows, place_ref[1], n_col)
        index = owner * (own_rows // size) + row % own_rows // size
        line = lax.rsqrt(1.0 + degree_ref[pl.ds(index, 1), :])
        return jnp.broadcast_to(line, (size, size)).T

    for place, block in enumerate(block_refs):
        for top in range(0, own_rows, size):
            row = place * own_rows + top
            spread = scale(row)
            for left in range(0, width, LANES):
                cut = slice(left, left + LANES)
                value = block[top : top + size, cut].astype(jnp.float32) * spread
                panel_ref[row : row + size, cut] = value.astype(jnp.bfloat16)
    for top in range(0, own_rows, size):
        scale_ref[top : top + size, :] = scale((n_col - 1 - begin) * own_rows + top)
    for part in range(n_row):
        rows = slice(part * own_rows, (part + 1) * own_rows)
        value = jnp.dot(dense_ref[rows, :], panel_ref[...], preferred_element_type=jnp.float32)
        if not first:
            value = value + sum_refs[0][rows, :]
        sum_out_ref[rows, :] = value


def last_kernel(*refs):
    dense_ref, scale_ref, upper_ref, lower_ref, sum_ref, *out_refs, panel_ref = refs
    own_rows, width = panel_ref.shape
    for block, top in ((upper_ref, 0), (lower_ref, own_rows // 2)):
        rows = slice(top, top + own_rows // 2)
        for left in range(0, width, LANES):
            cut = slice(left, left + LANES)
            panel_ref[rows, cut] = (block[:, cut].astype(jnp.float32) * scale_ref[rows, :]).astype(jnp.bfloat16)
    end = 0
    for out_ref in out_refs:
        rows = slice(end, end + out_ref.shape[0])
        end = rows.stop
        value = jnp.dot(dense_ref[rows, :], panel_ref[...], preferred_element_type=jnp.float32)
        out_ref[...] = (value + sum_ref[rows, :]).astype(out_ref.dtype)


def sigmoid(x):
    return 0.5 * jnp.tanh(0.5 * x) + 0.5


def tail_kernel(n_before, *refs):
    refs = refs[n_before:]
    (conv_ref, conv_bias_ref, input_ref, input_bias_ref, memory_ref), gate_refs, sums = refs[:5], refs[5:8], refs[8:-1]
    out_ref = refs[-1]
    width = memory_ref.shape[1]
    owned = functools.reduce(lambda x, y: x + y, [term[...].astype(jnp.float32) for term in sums])
    spread = jnp.mean(owned * owned, axis=1, keepdims=True) + norm_epsilon
    normed = (owned * lax.rsqrt(spread)).astype(jnp.bfloat16)
    message = jnp.maximum(
        jnp.dot(normed, conv_ref[...], preferred_element_type=jnp.float32) + conv_bias_ref[...], 0.0
    ).astype(jnp.bfloat16)

    def gate(index):
        cut = slice(index * width, (index + 1) * width)
        dots = jnp.dot(message, input_ref[:, cut], preferred_element_type=jnp.float32)
        return dots + input_bias_ref[:, cut], gate_refs[index][...]

    mine, held = gate(0)
    reset = sigmoid(mine + held)
    mine, held = gate(2)
    candidate = jnp.tanh(mine + reset * held)
    mine, held = gate(1)
    update = sigmoid(mine + held)
    out_ref[...] = (1.0 - update) * candidate + update * memory_ref[...]


def on_device(
    features,
    memory,
    tile_values,
    tile_rows,
    tile_cols,
    tile_count,
    conv_weight,
    conv_bias,
    input_weight,
    input_bias,
    hidden_weight,
    hidden_bias,
):
    own_rows, width = features.shape
    n_row, n_col = lax.axis_size("row"), lax.axis_size("col")
    slots, size = tile_values.shape[2], tile_values.shape[3]
    dst_rows, src_rows = own_rows * n_row, own_rows * n_col
    col_blocks = src_rows // size
    place = jnp.stack([lax.axis_index("row"), lax.axis_index("col")]).astype(jnp.int32)

    cycle = [*range(0, n_col, 2), *range(n_col - 1, 0, -2)]
    ahead = [(cycle[at - 1], cycle[at]) for at in range(n_col)]
    behind = [(to, at) for at, to in ahead]

    def tie(*values):
        return lax.optimization_barrier(values)

    def move(block, to):
        return lax.ppermute(block, "col", to)

    blocks = [features, move(features, ahead), move(features, behind)]
    half = own_rows // 2
    dense, degree = pl.pallas_call(
        functools.partial(build_kernel, own_rows, n_row, n_col),
        out_shape=(
            jax.ShapeDtypeStruct((dst_rows, src_rows), jnp.bfloat16),
            jax.ShapeDtypeStruct((col_blocks, size), jnp.float32),
        ),
        in_specs=[smem()] * 2 + [pl.BlockSpec(memory_space=pltpu.HBM)] * 3,
        out_specs=(vmem(), vmem()),
        scratch_shapes=[
            pltpu.VMEM((col_blocks, 8, size), jnp.float32),
            pltpu.VMEM((slots, size, size), jnp.bfloat16),
            pltpu.SMEM(tile_rows.shape, jnp.int32),
            pltpu.SMEM(tile_cols.shape, jnp.int32),
            pltpu.SemaphoreType.DMA((2 + BUILD_STEPS,)),
        ],
        compiler_params=params(2 * slots * size * size + 2 * dst_rows * src_rows),
        cost_estimate=cost(0, 2 * slots * size * size + 2 * dst_rows * src_rows),
        name="build",
    )(place, tile_count.reshape(1), *[pltpu.with_memory_space_constraint(x, pltpu.HBM) for x in (tile_rows, tile_cols, tile_values)])

    gates = []

    def gate_product(block):
        nonlocal memory
        block, memory = tie(block, memory)
        cut = slice(len(gates) * width, (len(gates) + 1) * width)
        gates.append(
            jnp.dot(memory.astype(jnp.bfloat16), hidden_weight[:, cut], preferred_element_type=jnp.float32)
            + hidden_bias[cut]
        )
        return block

    added = move(degree, [(i, i ^ 1) for i in range(n_col)])
    blocks[2], degree = tie(blocks[2], degree)
    bit = 2
    while len(blocks) < n_col - 1:
        blocks.append(move(blocks[-2], ahead))
        if len(gates) < 2:
            blocks[-2] = gate_product(blocks[-2])
            gates[-1], added = tie(gates[-1], added)
        elif bit < n_col:
            blocks[-2], added = tie(blocks[-2], added)
        blocks.append(move(blocks[-2], behind))
        if bit < n_col:
            degree = degree + added
            added = move(degree, [(i, i ^ bit) for i in range(n_col)])
            bit *= 2
    upper, lower = blocks[-2][:half], blocks[-1][half:]
    across = (move(upper, ahead), move(lower, behind))
    upper, lower, memory = tie(upper, lower, memory)
    gate_product(upper)
    gates[-1], added = tie(gates[-1], added)
    degree = degree + added

    def whole(*shape):
        return pl.BlockSpec(shape, lambda i: (0, 0))

    def product(begin, count, running):
        depth = count * own_rows
        return pl.pallas_call(
            functools.partial(product_kernel, n_row, n_col, begin, count, running is None),
            grid=(1,),
            out_shape=(
                jax.ShapeDtypeStruct((dst_rows, width), jnp.float32),
                jax.ShapeDtypeStruct((own_rows, size), jnp.float32),
            ),
            in_specs=[
                smem(),
                pl.BlockSpec((dst_rows, depth), lambda i: (0, begin // count)),
                vmem(),
            ]
            + [vmem()] * count
            + ([] if running is None else [vmem()]),
            out_specs=(whole(dst_rows, width), whole(own_rows, size)),
            scratch_shapes=[pltpu.VMEM((depth, width), jnp.bfloat16)],
            compiler_params=params(2 * dst_rows * depth + 4 * depth * width + 8 * dst_rows * width + 2 * MIB),
            cost_estimate=cost(2 * dst_rows * depth * width, 2 * dst_rows * depth + 6 * dst_rows * width),
            name="product",
        )(place, dense, degree, *blocks[begin : begin + count], *([] if running is None else [running]))

    def last_product(at, height):
        rows = dst_rows // 2
        dtypes = [jnp.float32 if top // own_rows % 2 else jnp.bfloat16 for top in range(0, rows, height)]
        return pl.pallas_call(
            last_kernel,
            grid=(1,),
            out_shape=tuple(jax.ShapeDtypeStruct((height, width), dtype) for dtype in dtypes),
            in_specs=[
                pl.BlockSpec((rows, own_rows), lambda i: (at, n_col - 1)),
                vmem(),
                vmem(),
                vmem(),
                pl.BlockSpec((rows, width), lambda i: (at, 0)),
            ],
            out_specs=(whole(height, width),) * len(dtypes),
            scratch_shapes=[pltpu.VMEM((own_rows, width), jnp.bfloat16)],
            compiler_params=params(2 * rows * own_rows + 6 * own_rows * width + 8 * rows * width + 2 * MIB),
            cost_estimate=cost(2 * rows * own_rows * width, 2 * rows * own_rows + 6 * rows * width),
            name="last_product",
        )(dense, scale, *across, running)

    running, begin = None, 0
    while begin < n_col - 1:
        count = n_col - 1 if n_col <= 8 else (n_col - begin) // 2
        running, scale = product(begin, count, running)
        begin += count
    def total(terms):
        return functools.reduce(lambda x, y: x + y, [term.astype(jnp.float32) for term in terms]).astype(jnp.bfloat16)

    def send(value, bit):
        return lax.ppermute(value, "row", [(i, i ^ bit) for i in range(n_row)])

    def halve(sums, end):
        for part in sorted(sums, reverse=True):
            if part > end:
                sums[part & (part - 1)].append(send(total(sums[part]), part & -part))
        return sums[end]

    middle = n_row // 2
    upper, lower = last_product(0, half), last_product(1, own_rows)
    sums = [{n_row - 1 - at: [upper[2 * at + which]] for at in range(middle)} for which in range(2)]
    given = [total(halve(each, middle)) for each in sums]
    given[0], *lower = tie(given[0], *lower)
    arrived = [send(value, middle) for value in given]
    terms = halve({middle - 1 - at: [part] for at, part in enumerate(lower)}, 0)

    weights = (conv_weight, conv_bias.reshape(1, width), input_weight, input_bias.reshape(1, 3 * width))
    result = None
    for at in range(2):
        part = pl.BlockSpec((half, width), lambda i, at=at: (at, 0))
        operands = [(term, part) for term in terms] + [(arrived[at], vmem())]
        before = [] if result is None else [result]
        result = pl.pallas_call(
            functools.partial(tail_kernel, len(before)),
            grid=(1,),
            out_shape=jax.ShapeDtypeStruct((own_rows, width), jnp.float32),
            in_specs=[pl.BlockSpec(memory_space=pl.ANY)] * len(before)
            + [vmem()] * len(weights)
            + [part] * 4
            + [spec for _, spec in operands],
            out_specs=part,
            input_output_aliases={0: 0} if before else {},
            compiler_params=params(8 * width * width + 40 * own_rows * width),
            cost_estimate=cost(4 * own_rows * width * width, 8 * width * width + 10 * own_rows * width),
            name="tail",
        )(*before, *weights, memory, *gates, *[term for term, _ in operands])
    return result


def solution(mesh):
    placed = (
        P(("row", "col"), None),
        P(("col", "row"), None),
        P("row", "col", None, None, None),
        P("row", "col", None),
        P("row", "col", None),
        P("row", "col"),
        P(),
        P(),
        P(),
        P(),
        P(),
        P(),
    )
    return jax.shard_map(
        on_device, mesh=mesh, in_specs=placed, out_specs=P(("col", "row"), None), check_vma=False
    )
```

```python
import functools

import jax
import jax.numpy as jnp
from jax import lax
from jax.experimental import pallas as pl
from jax.experimental.pallas import tpu as pltpu
from jax.sharding import PartitionSpec as P

norm_epsilon = 1e-06
MIB = 1 << 20
LANES = 128
BUILD_STEPS = 4


def vmem():
    return pl.BlockSpec(memory_space=pltpu.VMEM)


def smem():
    return pl.BlockSpec(memory_space=pltpu.SMEM)


def params(size):
    return pltpu.CompilerParams(vmem_limit_bytes=size + size // 4 + 4 * MIB)


def cost(flops, bytes_accessed):
    return pl.CostEstimate(flops=flops, bytes_accessed=bytes_accessed, transcendentals=0)


def cycle_place(col, n):
    level = lax.shift_right_logical(col, 1)
    return jnp.where((col & 1) == 0, level, n - 1 - level)


def cycle_column(place, n):
    return jnp.where(place < n // 2, 2 * place, 2 * (n - 1 - place) + 1)


def arrival_place(owner, me, n):
    back = lax.rem(cycle_place(me, n) - cycle_place(owner, n) + n, n)
    return jnp.where(back <= n // 2, jnp.maximum(2 * back - 1, 0), 2 * (n - back))


def arrival_owner(place, me, n):
    back = (place + 1) // 2 if place % 2 else (n - place // 2) % n
    return cycle_column(lax.rem(cycle_place(me, n) - back + n, n), n)


def part_place(owner, me, n):
    return n - 1 - (owner ^ me)


def build_kernel(own_rows, n_row, n_col, place_ref, count_ref, rows_any, cols_any, tiles_any, dense_ref, degree_ref, *scratch):
    acc_ref, tiles_ref, rows_ref, cols_ref, sems = scratch
    row_me, col_me = place_ref[0], place_ref[1]
    slots, size = tiles_ref.shape[:2]
    per = own_rows // size
    some = slots // BUILD_STEPS
    small = [
        pltpu.make_async_copy(rows_any, rows_ref, sems.at[0]),
        pltpu.make_async_copy(cols_any, cols_ref, sems.at[1]),
    ]
    large = [
        pltpu.make_async_copy(
            tiles_any.at[0, 0, pl.ds(step * some, some)], tiles_ref.at[pl.ds(step * some, some)], sems.at[2 + step]
        )
        for step in range(BUILD_STEPS)
    ]
    for copy in small + large:
        copy.start()
    dense_ref[...] = jnp.zeros_like(dense_ref)
    acc_ref[...] = jnp.zeros_like(acc_ref)

    def one(slot, carry):
        a, b = rows_ref[0, 0, slot], cols_ref[0, 0, slot]
        row = (part_place(lax.div(a, per), row_me, n_row) * per + lax.rem(a, per)) * size
        col = (arrival_place(lax.div(b, per), col_me, n_col) * per + lax.rem(b, per)) * size
        tile = tiles_ref[slot]
        dense_ref[pl.ds(pl.multiple_of(row, size), size), pl.ds(pl.multiple_of(col, size), size)] = tile
        wide = tile.astype(jnp.float32).reshape(size // 8, 8, size)
        acc_ref[b] += jnp.sum(wide, axis=0)
        return carry

    for copy in small:
        copy.wait()
    for step, copy in enumerate(large):
        copy.wait()
        lax.fori_loop(step * some, jnp.minimum(count_ref[0], (step + 1) * some), one, 0)
    degree_ref[...] = jnp.sum(acc_ref[...], axis=1)


def product_kernel(n_row, n_col, begin, n_blocks, first, *refs):
    place_ref, dense_ref, degree_ref = refs[:3]
    block_refs = refs[3 : 3 + n_blocks]
    sum_refs = () if first else refs[3 + n_blocks : 4 + n_blocks]
    panel_ref = refs[-1]
    sum_out_ref, scale_ref = refs[-3:-1]
    width, size = panel_ref.shape[1], degree_ref.shape[1]
    own_rows = dense_ref.shape[0] // n_row

    def scale(row):
        owner = arrival_owner(begin + row // own_rows, place_ref[1], n_col)
        index = owner * (own_rows // size) + row % own_rows // size
        line = lax.rsqrt(1.0 + degree_ref[pl.ds(index, 1), :])
        return jnp.broadcast_to(line, (size, size)).T

    for place, block in enumerate(block_refs):
        for top in range(0, own_rows, size):
            row = place * own_rows + top
            spread = scale(row)
            for left in range(0, width, LANES):
                cut = slice(left, left + LANES)
                value = block[top : top + size, cut].astype(jnp.float32) * spread
                panel_ref[row : row + size, cut] = value.astype(jnp.bfloat16)
    for top in range(0, own_rows, size):
        scale_ref[top : top + size, :] = scale((n_col - 1 - begin) * own_rows + top)
    for part in range(n_row):
        rows = slice(part * own_rows, (part + 1) * own_rows)
        value = jnp.dot(dense_ref[rows, :], panel_ref[...], preferred_element_type=jnp.float32)
        if not first:
            value = value + sum_refs[0][rows, :]
        sum_out_ref[rows, :] = value


def last_kernel(*refs):
    dense_ref, scale_ref, upper_ref, lower_ref, sum_ref, *out_refs, panel_ref = refs
    own_rows, width = panel_ref.shape
    for block, top in ((upper_ref, 0), (lower_ref, own_rows // 2)):
        rows = slice(top, top + own_rows // 2)
        for left in range(0, width, LANES):
            cut = slice(left, left + LANES)
            panel_ref[rows, cut] = (block[:, cut].astype(jnp.float32) * scale_ref[rows, :]).astype(jnp.bfloat16)
    end = 0
    for out_ref in out_refs:
        rows = slice(end, end + out_ref.shape[0])
        end = rows.stop
        value = jnp.dot(dense_ref[rows, :], panel_ref[...], preferred_element_type=jnp.float32)
        out_ref[...] = (value + sum_ref[rows, :]).astype(out_ref.dtype)


def sigmoid(x):
    return 0.5 * jnp.tanh(0.5 * x) + 0.5


def tail_kernel(n_before, *refs):
    refs = refs[n_before:]
    (conv_ref, conv_bias_ref, input_ref, input_bias_ref, memory_ref), gate_refs, sums = refs[:5], refs[5:8], refs[8:-1]
    out_ref = refs[-1]
    width = memory_ref.shape[1]
    owned = functools.reduce(lambda x, y: x + y, [term[...].astype(jnp.float32) for term in sums])
    spread = jnp.mean(owned * owned, axis=1, keepdims=True) + norm_epsilon
    normed = (owned * lax.rsqrt(spread)).astype(jnp.bfloat16)
    message = jnp.maximum(
        jnp.dot(normed, conv_ref[...], preferred_element_type=jnp.float32) + conv_bias_ref[...], 0.0
    ).astype(jnp.bfloat16)

    def gate(index):
        cut = slice(index * width, (index + 1) * width)
        dots = jnp.dot(message, input_ref[:, cut], preferred_element_type=jnp.float32)
        return dots + input_bias_ref[:, cut], gate_refs[index][...]

    mine, held = gate(0)
    reset = sigmoid(mine + held)
    mine, held = gate(2)
    candidate = jnp.tanh(mine + reset * held)
    mine, held = gate(1)
    update = sigmoid(mine + held)
    out_ref[...] = (1.0 - update) * candidate + update * memory_ref[...]


def on_device(
    features,
    memory,
    tile_values,
    tile_rows,
    tile_cols,
    tile_count,
    conv_weight,
    conv_bias,
    input_weight,
    input_bias,
    hidden_weight,
    hidden_bias,
):
    own_rows, width = features.shape
    n_row, n_col = lax.axis_size("row"), lax.axis_size("col")
    slots, size = tile_values.shape[2], tile_values.shape[3]
    dst_rows, src_rows = own_rows * n_row, own_rows * n_col
    col_blocks = src_rows // size
    place = jnp.stack([lax.axis_index("row"), lax.axis_index("col")]).astype(jnp.int32)

    cycle = [*range(0, n_col, 2), *range(n_col - 1, 0, -2)]
    ahead = [(cycle[at - 1], cycle[at]) for at in range(n_col)]
    behind = [(to, at) for at, to in ahead]

    def tie(*values):
        return lax.optimization_barrier(values)

    def move(block, to):
        return lax.ppermute(block, "col", to)

    blocks = [features, move(features, ahead), move(features, behind)]
    half = own_rows // 2
    dense, degree = pl.pallas_call(
        functools.partial(build_kernel, own_rows, n_row, n_col),
        out_shape=(
            jax.ShapeDtypeStruct((dst_rows, src_rows), jnp.bfloat16),
            jax.ShapeDtypeStruct((col_blocks, size), jnp.float32),
        ),
        in_specs=[smem()] * 2 + [pl.BlockSpec(memory_space=pltpu.HBM)] * 3,
        out_specs=(vmem(), vmem()),
        scratch_shapes=[
            pltpu.VMEM((col_blocks, 8, size), jnp.float32),
            pltpu.VMEM((slots, size, size), jnp.bfloat16),
            pltpu.SMEM(tile_rows.shape, jnp.int32),
            pltpu.SMEM(tile_cols.shape, jnp.int32),
            pltpu.SemaphoreType.DMA((2 + BUILD_STEPS,)),
        ],
        compiler_params=params(2 * slots * size * size + 2 * dst_rows * src_rows),
        cost_estimate=cost(0, 2 * slots * size * size + 2 * dst_rows * src_rows),
        name="build",
    )(place, tile_count.reshape(1), *[pltpu.with_memory_space_constraint(x, pltpu.HBM) for x in (tile_rows, tile_cols, tile_values)])

    gates = []

    def gate_product(block):
        nonlocal memory
        block, memory = tie(block, memory)
        cut = slice(len(gates) * width, (len(gates) + 1) * width)
        gates.append(
            jnp.dot(memory.astype(jnp.bfloat16), hidden_weight[:, cut], preferred_element_type=jnp.float32)
            + hidden_bias[cut]
        )
        return block

    added = move(degree, [(i, i ^ 2) for i in range(n_col)])
    blocks[2], degree = tie(blocks[2], degree)
    bit = 4
    while len(blocks) < n_col - 1:
        blocks.append(move(blocks[-2], ahead))
        if len(gates) < 2:
            blocks[-2] = gate_product(blocks[-2])
            gates[-1], added = tie(gates[-1], added)
        elif bit <= n_col:
            blocks[-2], added = tie(blocks[-2], added)
        blocks.append(move(blocks[-2], behind))
        if bit <= n_col:
            degree = degree + added
            added = move(degree, [(i, i ^ (bit if bit < n_col else 1)) for i in range(n_col)])
            bit *= 2
    upper, lower = blocks[-2][:half], blocks[-1][half:]
    across = (move(upper, ahead), move(lower, behind))
    upper, lower, memory = tie(upper, lower, memory)
    gate_product(upper)
    gates[-1], added = tie(gates[-1], added)
    degree = degree + added

    def whole(*shape):
        return pl.BlockSpec(shape, lambda i: (0, 0))

    def product(begin, count, running):
        depth = count * own_rows
        return pl.pallas_call(
            functools.partial(product_kernel, n_row, n_col, begin, count, running is None),
            grid=(1,),
            out_shape=(
                jax.ShapeDtypeStruct((dst_rows, width), jnp.float32),
                jax.ShapeDtypeStruct((own_rows, size), jnp.float32),
            ),
            in_specs=[
                smem(),
                pl.BlockSpec((dst_rows, depth), lambda i: (0, begin // count)),
                whole(col_blocks, size),
            ]
            + [whole(own_rows, width)] * count
            + ([] if running is None else [whole(dst_rows, width)]),
            out_specs=(whole(dst_rows, width), whole(own_rows, size)),
            scratch_shapes=[pltpu.VMEM((depth, width), jnp.bfloat16)],
            compiler_params=params(2 * dst_rows * depth + 4 * depth * width + 8 * dst_rows * width + 2 * MIB),
            cost_estimate=cost(2 * dst_rows * depth * width, 2 * dst_rows * depth + 6 * dst_rows * width),
            name="product",
        )(place, dense, degree, *blocks[begin : begin + count], *([] if running is None else [running]))

    def last_product(at, height):
        rows = dst_rows // 2
        dtypes = [jnp.float32 if top // own_rows % 2 else jnp.bfloat16 for top in range(0, rows, height)]
        return pl.pallas_call(
            last_kernel,
            grid=(1,),
            out_shape=tuple(jax.ShapeDtypeStruct((height, width), dtype) for dtype in dtypes),
            in_specs=[
                pl.BlockSpec((rows, own_rows), lambda i: (at, n_col - 1)),
                whole(own_rows, size),
                whole(half, width),
                whole(half, width),
                pl.BlockSpec((rows, width), lambda i: (at, 0)),
            ],
            out_specs=(whole(height, width),) * len(dtypes),
            scratch_shapes=[pltpu.VMEM((own_rows, width), jnp.bfloat16)],
            compiler_params=params(2 * rows * own_rows + 6 * own_rows * width + 8 * rows * width + 2 * MIB),
            cost_estimate=cost(2 * rows * own_rows * width, 2 * rows * own_rows + 6 * rows * width),
            name="last_product",
        )(dense, scale, *across, running)

    running, begin = None, 0
    while begin < n_col - 1:
        count = n_col - 1 if n_col <= 8 else (n_col - begin) // 2
        running, scale = product(begin, count, running)
        begin += count
    def total(terms):
        return functools.reduce(lambda x, y: x + y, [term.astype(jnp.float32) for term in terms]).astype(jnp.bfloat16)

    def send(value, bit):
        return lax.ppermute(value, "row", [(i, i ^ bit) for i in range(n_row)])

    def halve(sums, end):
        for part in sorted(sums, reverse=True):
            if part > end:
                sums[part & (part - 1)].append(send(total(sums[part]), part & -part))
        return sums[end]

    middle = n_row // 2
    upper, lower = last_product(0, half), last_product(1, own_rows)
    sums = [{n_row - 1 - at: [upper[2 * at + which]] for at in range(middle)} for which in range(2)]
    given = [total(halve(each, middle)) for each in sums]
    given[0], *lower = tie(given[0], *lower)
    arrived = [send(value, middle) for value in given]
    terms = halve({middle - 1 - at: [part] for at, part in enumerate(lower)}, 0)

    weights = (conv_weight, conv_bias.reshape(1, width), input_weight, input_bias.reshape(1, 3 * width))
    result = None
    for at in range(2):
        part = pl.BlockSpec((half, width), lambda i, at=at: (at, 0))
        operands = [(term, part) for term in terms] + [(arrived[at], whole(half, width))]
        before = [] if result is None else [result]
        result = pl.pallas_call(
            functools.partial(tail_kernel, len(before)),
            grid=(1,),
            out_shape=jax.ShapeDtypeStruct((own_rows, width), jnp.float32),
            in_specs=[pl.BlockSpec(memory_space=pl.ANY)] * len(before)
            + [whole(*weight.shape) for weight in weights]
            + [part] * 4
            + [spec for _, spec in operands],
            out_specs=part,
            input_output_aliases={0: 0} if before else {},
            compiler_params=params(8 * width * width + 40 * own_rows * width),
            cost_estimate=cost(4 * own_rows * width * width, 8 * width * width + 10 * own_rows * width),
            name="tail",
        )(*before, *weights, memory, *gates, *[term for term, _ in operands])
    return result


def solution(mesh):
    placed = (
        P(("row", "col"), None),
        P(("col", "row"), None),
        P("row", "col", None, None, None),
        P("row", "col", None),
        P("row", "col", None),
        P("row", "col"),
        P(),
        P(),
        P(),
        P(),
        P(),
        P(),
    )
    return jax.shard_map(
        on_device, mesh=mesh, in_specs=placed, out_specs=P(("col", "row"), None), check_vma=False
    )
```

```python
import functools

import jax
import jax.numpy as jnp
from jax import lax
from jax.experimental import pallas as pl
from jax.experimental.pallas import tpu as pltpu
from jax.sharding import PartitionSpec as P

norm_epsilon = 1e-06
MIB = 1 << 20
LANES = 128
BUILD_STEPS = 4


def vmem():
    return pl.BlockSpec(memory_space=pltpu.VMEM)


def smem():
    return pl.BlockSpec(memory_space=pltpu.SMEM)


def params(size):
    return pltpu.CompilerParams(vmem_limit_bytes=size + size // 4 + 4 * MIB)


def cost(flops, bytes_accessed):
    return pl.CostEstimate(flops=flops, bytes_accessed=bytes_accessed, transcendentals=0)


def cycle_place(col, n):
    level = lax.shift_right_logical(col, 1)
    return jnp.where((col & 1) == 0, level, n - 1 - level)


def cycle_column(place, n):
    return jnp.where(place < n // 2, 2 * place, 2 * (n - 1 - place) + 1)


def arrival_place(owner, me, n):
    back = lax.rem(cycle_place(me, n) - cycle_place(owner, n) + n, n)
    return jnp.where(back <= n // 2, jnp.maximum(2 * back - 1, 0), 2 * (n - back))


def arrival_owner(place, me, n):
    back = (place + 1) // 2 if place % 2 else (n - place // 2) % n
    return cycle_column(lax.rem(cycle_place(me, n) - back + n, n), n)


def part_place(owner, me, n):
    return n - 1 - (owner ^ me)


def build_kernel(own_rows, n_row, n_col, place_ref, count_ref, rows_any, cols_any, tiles_any, dense_ref, degree_ref, *scratch):
    acc_ref, tiles_ref, rows_ref, cols_ref, sems = scratch
    row_me, col_me = place_ref[0], place_ref[1]
    slots, size = tiles_ref.shape[:2]
    per = own_rows // size
    some = slots // BUILD_STEPS
    small = [
        pltpu.make_async_copy(rows_any, rows_ref, sems.at[0]),
        pltpu.make_async_copy(cols_any, cols_ref, sems.at[1]),
    ]
    large = [
        pltpu.make_async_copy(
            tiles_any.at[0, 0, pl.ds(step * some, some)], tiles_ref.at[pl.ds(step * some, some)], sems.at[2 + step]
        )
        for step in range(BUILD_STEPS)
    ]
    for copy in small + large:
        copy.start()
    dense_ref[...] = jnp.zeros_like(dense_ref)
    acc_ref[...] = jnp.zeros_like(acc_ref)

    def one(slot, carry):
        a, b = rows_ref[0, 0, slot], cols_ref[0, 0, slot]
        row = (part_place(lax.div(a, per), row_me, n_row) * per + lax.rem(a, per)) * size
        col = (arrival_place(lax.div(b, per), col_me, n_col) * per + lax.rem(b, per)) * size
        tile = tiles_ref[slot]
        dense_ref[pl.ds(pl.multiple_of(row, size), size), pl.ds(pl.multiple_of(col, size), size)] = tile
        wide = tile.astype(jnp.float32).reshape(size // 8, 8, size)
        acc_ref[b] += jnp.sum(wide, axis=0)
        return carry

    for copy in small:
        copy.wait()
    for step, copy in enumerate(large):
        copy.wait()
        lax.fori_loop(step * some, jnp.minimum(count_ref[0], (step + 1) * some), one, 0)
    degree_ref[...] = jnp.sum(acc_ref[...], axis=1)


def product_kernel(n_row, n_col, begin, n_blocks, first, *refs):
    place_ref, dense_ref, degree_ref = refs[:3]
    block_refs = refs[3 : 3 + n_blocks]
    sum_refs = () if first else refs[3 + n_blocks : 4 + n_blocks]
    panel_ref = refs[-1]
    sum_out_ref, scale_ref = refs[-3:-1]
    width, size = panel_ref.shape[1], degree_ref.shape[1]
    own_rows = dense_ref.shape[0] // n_row

    def scale(row):
        owner = arrival_owner(begin + row // own_rows, place_ref[1], n_col)
        index = owner * (own_rows // size) + row % own_rows // size
        line = lax.rsqrt(1.0 + degree_ref[pl.ds(index, 1), :])
        return jnp.broadcast_to(line, (size, size)).T

    for place, block in enumerate(block_refs):
        for top in range(0, own_rows, size):
            row = place * own_rows + top
            spread = scale(row)
            for left in range(0, width, LANES):
                cut = slice(left, left + LANES)
                value = block[top : top + size, cut].astype(jnp.float32) * spread
                panel_ref[row : row + size, cut] = value.astype(jnp.bfloat16)
    for top in range(0, own_rows, size):
        scale_ref[top : top + size, :] = scale((n_col - 1 - begin) * own_rows + top)
    for part in range(n_row):
        rows = slice(part * own_rows, (part + 1) * own_rows)
        value = jnp.dot(dense_ref[rows, :], panel_ref[...], preferred_element_type=jnp.float32)
        if not first:
            value = value + sum_refs[0][rows, :]
        sum_out_ref[rows, :] = value


def last_kernel(*refs):
    dense_ref, scale_ref, block_ref, sum_ref, *out_refs, panel_ref = refs
    width = panel_ref.shape[1]
    for left in range(0, width, LANES):
        cut = slice(left, left + LANES)
        panel_ref[:, cut] = (block_ref[:, cut].astype(jnp.float32) * scale_ref[...]).astype(jnp.bfloat16)
    end = 0
    for out_ref in out_refs:
        rows = slice(end, end + out_ref.shape[0])
        end = rows.stop
        value = jnp.dot(dense_ref[rows, :], panel_ref[...], preferred_element_type=jnp.float32)
        out_ref[...] = (value + sum_ref[rows, :]).astype(out_ref.dtype)


def sigmoid(x):
    return 0.5 * jnp.tanh(0.5 * x) + 0.5


def tail_kernel(n_before, *refs):
    refs = refs[n_before:]
    (conv_ref, conv_bias_ref, input_ref, input_bias_ref, memory_ref), gate_refs, sums = refs[:5], refs[5:8], refs[8:-1]
    out_ref = refs[-1]
    width = memory_ref.shape[1]
    owned = functools.reduce(lambda x, y: x + y, [term[...].astype(jnp.float32) for term in sums])
    spread = jnp.mean(owned * owned, axis=1, keepdims=True) + norm_epsilon
    normed = (owned * lax.rsqrt(spread)).astype(jnp.bfloat16)
    message = jnp.maximum(
        jnp.dot(normed, conv_ref[...], preferred_element_type=jnp.float32) + conv_bias_ref[...], 0.0
    ).astype(jnp.bfloat16)

    def gate(index):
        cut = slice(index * width, (index + 1) * width)
        dots = jnp.dot(message, input_ref[:, cut], preferred_element_type=jnp.float32)
        return dots + input_bias_ref[:, cut], gate_refs[index][...]

    mine, held = gate(0)
    reset = sigmoid(mine + held)
    mine, held = gate(2)
    candidate = jnp.tanh(mine + reset * held)
    mine, held = gate(1)
    update = sigmoid(mine + held)
    out_ref[...] = (1.0 - update) * candidate + update * memory_ref[...]


def on_device(
    features,
    memory,
    tile_values,
    tile_rows,
    tile_cols,
    tile_count,
    conv_weight,
    conv_bias,
    input_weight,
    input_bias,
    hidden_weight,
    hidden_bias,
):
    own_rows, width = features.shape
    n_row, n_col = lax.axis_size("row"), lax.axis_size("col")
    slots, size = tile_values.shape[2], tile_values.shape[3]
    dst_rows, src_rows = own_rows * n_row, own_rows * n_col
    col_blocks = src_rows // size
    place = jnp.stack([lax.axis_index("row"), lax.axis_index("col")]).astype(jnp.int32)

    cycle = [*range(0, n_col, 2), *range(n_col - 1, 0, -2)]
    ahead = [(cycle[at - 1], cycle[at]) for at in range(n_col)]
    behind = [(to, at) for at, to in ahead]

    def tie(*values):
        return lax.optimization_barrier(values)

    def move(block, to):
        return lax.ppermute(block, "col", to)

    blocks = [features, move(features, ahead), move(features, behind)]
    half = own_rows // 2
    dense, degree = pl.pallas_call(
        functools.partial(build_kernel, own_rows, n_row, n_col),
        out_shape=(
            jax.ShapeDtypeStruct((dst_rows, src_rows), jnp.bfloat16),
            jax.ShapeDtypeStruct((col_blocks, size), jnp.float32),
        ),
        in_specs=[smem()] * 2 + [pl.BlockSpec(memory_space=pltpu.HBM)] * 3,
        out_specs=(vmem(), vmem()),
        scratch_shapes=[
            pltpu.VMEM((col_blocks, 8, size), jnp.float32),
            pltpu.VMEM((slots, size, size), jnp.bfloat16),
            pltpu.SMEM(tile_rows.shape, jnp.int32),
            pltpu.SMEM(tile_cols.shape, jnp.int32),
            pltpu.SemaphoreType.DMA((2 + BUILD_STEPS,)),
        ],
        compiler_params=params(2 * slots * size * size + 2 * dst_rows * src_rows),
        cost_estimate=cost(0, 2 * slots * size * size + 2 * dst_rows * src_rows),
        name="build",
    )(place, tile_count.reshape(1), *[pltpu.with_memory_space_constraint(x, pltpu.HBM) for x in (tile_rows, tile_cols, tile_values)])

    gates = []

    def gate_product(block):
        nonlocal memory
        block, memory = tie(block, memory)
        cut = slice(len(gates) * width, (len(gates) + 1) * width)
        gates.append(
            jnp.dot(memory.astype(jnp.bfloat16), hidden_weight[:, cut], preferred_element_type=jnp.float32)
            + hidden_bias[cut]
        )
        return block

    added = move(degree, [(i, i ^ 1) for i in range(n_col)])
    blocks[2], degree = tie(blocks[2], degree)
    bit = 2
    while len(blocks) < n_col - 1:
        blocks.append(move(blocks[-2], ahead))
        if len(gates) < 2:
            blocks[-2] = gate_product(blocks[-2])
            gates[-1], added = tie(gates[-1], added)
        elif bit < n_col:
            blocks[-2], added = tie(blocks[-2], added)
        blocks.append(move(blocks[-2], behind))
        if bit < n_col:
            degree = degree + added
            added = move(degree, [(i, i ^ bit) for i in range(n_col)])
            bit *= 2
    across = move(blocks[-1], behind)
    blocks[-1] = gate_product(blocks[-1])
    gates[-1], added = tie(gates[-1], added)
    degree = degree + added

    def whole(*shape):
        return pl.BlockSpec(shape, lambda i: (0, 0))

    def product(begin, count, running):
        depth = count * own_rows
        return pl.pallas_call(
            functools.partial(product_kernel, n_row, n_col, begin, count, running is None),
            grid=(1,),
            out_shape=(
                jax.ShapeDtypeStruct((dst_rows, width), jnp.float32),
                jax.ShapeDtypeStruct((own_rows, size), jnp.float32),
            ),
            in_specs=[
                smem(),
                pl.BlockSpec((dst_rows, depth), lambda i: (0, begin // count)),
                whole(col_blocks, size),
            ]
            + [whole(own_rows, width)] * count
            + ([] if running is None else [whole(dst_rows, width)]),
            out_specs=(whole(dst_rows, width), whole(own_rows, size)),
            scratch_shapes=[pltpu.VMEM((depth, width), jnp.bfloat16)],
            compiler_params=params(2 * dst_rows * depth + 4 * depth * width + 8 * dst_rows * width + 2 * MIB),
            cost_estimate=cost(2 * dst_rows * depth * width, 2 * dst_rows * depth + 6 * dst_rows * width),
            name="product",
        )(place, dense, degree, *blocks[begin : begin + count], *([] if running is None else [running]))

    def last_product(at, height):
        rows = dst_rows // 2
        dtypes = [jnp.float32 if top // own_rows % 2 else jnp.bfloat16 for top in range(0, rows, height)]
        return pl.pallas_call(
            last_kernel,
            grid=(1,),
            out_shape=tuple(jax.ShapeDtypeStruct((height, width), dtype) for dtype in dtypes),
            in_specs=[
                pl.BlockSpec((rows, own_rows), lambda i: (at, n_col - 1)),
                whole(own_rows, size),
                whole(own_rows, width),
                pl.BlockSpec((rows, width), lambda i: (at, 0)),
            ],
            out_specs=(whole(height, width),) * len(dtypes),
            scratch_shapes=[pltpu.VMEM((own_rows, width), jnp.bfloat16)],
            compiler_params=params(2 * rows * own_rows + 6 * own_rows * width + 8 * rows * width + 2 * MIB),
            cost_estimate=cost(2 * rows * own_rows * width, 2 * rows * own_rows + 6 * rows * width),
            name="last_product",
        )(dense, scale, across, running)

    running, begin = None, 0
    while begin < n_col - 1:
        count = n_col - 1 if n_col <= 8 else (n_col - begin) // 2
        running, scale = product(begin, count, running)
        begin += count
    def total(terms):
        return functools.reduce(lambda x, y: x + y, [term.astype(jnp.float32) for term in terms]).astype(jnp.bfloat16)

    def send(value, bit):
        return lax.ppermute(value, "row", [(i, i ^ bit) for i in range(n_row)])

    def halve(sums, end):
        for part in sorted(sums, reverse=True):
            if part > end:
                sums[part & (part - 1)].append(send(total(sums[part]), part & -part))
        return sums[end]

    middle = n_row // 2
    upper, lower = last_product(0, half), last_product(1, own_rows)
    sums = [{n_row - 1 - at: [upper[2 * at + which]] for at in range(middle)} for which in range(2)]
    given = [total(halve(each, middle)) for each in sums]
    given[0], *lower = tie(given[0], *lower)
    arrived = [send(value, middle) for value in given]
    terms = halve({middle - 1 - at: [part] for at, part in enumerate(lower)}, 0)

    weights = (conv_weight, conv_bias.reshape(1, width), input_weight, input_bias.reshape(1, 3 * width))
    result = None
    for at in range(2):
        part = pl.BlockSpec((half, width), lambda i, at=at: (at, 0))
        operands = [(term, part) for term in terms] + [(arrived[at], whole(half, width))]
        before = [] if result is None else [result]
        result = pl.pallas_call(
            functools.partial(tail_kernel, len(before)),
            grid=(1,),
            out_shape=jax.ShapeDtypeStruct((own_rows, width), jnp.float32),
            in_specs=[pl.BlockSpec(memory_space=pl.ANY)] * len(before)
            + [whole(*weight.shape) for weight in weights]
            + [part] * 4
            + [spec for _, spec in operands],
            out_specs=part,
            input_output_aliases={0: 0} if before else {},
            compiler_params=params(8 * width * width + 40 * own_rows * width),
            cost_estimate=cost(4 * own_rows * width * width, 8 * width * width + 10 * own_rows * width),
            name="tail",
        )(*before, *weights, memory, *gates, *[term for term, _ in operands])
    return result


def solution(mesh):
    placed = (
        P(("row", "col"), None),
        P(("col", "row"), None),
        P("row", "col", None, None, None),
        P("row", "col", None),
        P("row", "col", None),
        P("row", "col"),
        P(),
        P(),
        P(),
        P(),
        P(),
        P(),
    )
    return jax.shard_map(
        on_device, mesh=mesh, in_specs=placed, out_specs=P(("col", "row"), None), check_vma=False
    )
```

```python
import functools

import jax
import jax.numpy as jnp
from jax import lax
from jax.experimental import pallas as pl
from jax.experimental.pallas import tpu as pltpu
from jax.sharding import PartitionSpec as P

norm_epsilon = 1e-06
MIB = 1 << 20
LANES = 128
BUILD_STEPS = 4


def vmem():
    return pl.BlockSpec(memory_space=pltpu.VMEM)


def smem():
    return pl.BlockSpec(memory_space=pltpu.SMEM)


def params(size):
    return pltpu.CompilerParams(vmem_limit_bytes=size + size // 4 + 4 * MIB)


def cost(flops, bytes_accessed):
    return pl.CostEstimate(flops=flops, bytes_accessed=bytes_accessed, transcendentals=0)


def cycle_place(col, n):
    level = lax.shift_right_logical(col, 1)
    return jnp.where((col & 1) == 0, level, n - 1 - level)


def cycle_column(place, n):
    return jnp.where(place < n // 2, 2 * place, 2 * (n - 1 - place) + 1)


def arrival_place(owner, me, n):
    back = lax.rem(cycle_place(me, n) - cycle_place(owner, n) + n, n)
    return jnp.where(back <= n // 2, jnp.maximum(2 * back - 1, 0), 2 * (n - back))


def arrival_owner(place, me, n):
    back = (place + 1) // 2 if place % 2 else (n - place // 2) % n
    return cycle_column(lax.rem(cycle_place(me, n) - back + n, n), n)


def part_place(owner, me, n):
    return n - 1 - (owner ^ me)


def build_kernel(own_rows, n_row, n_col, place_ref, count_ref, rows_any, cols_any, tiles_any, dense_ref, degree_ref, *scratch):
    acc_ref, tiles_ref, rows_ref, cols_ref, sems = scratch
    row_me, col_me = place_ref[0], place_ref[1]
    slots, size = tiles_ref.shape[:2]
    per = own_rows // size
    some = slots // BUILD_STEPS
    small = [
        pltpu.make_async_copy(rows_any, rows_ref, sems.at[0]),
        pltpu.make_async_copy(cols_any, cols_ref, sems.at[1]),
    ]
    large = [
        pltpu.make_async_copy(
            tiles_any.at[0, 0, pl.ds(step * some, some)], tiles_ref.at[pl.ds(step * some, some)], sems.at[2 + step]
        )
        for step in range(BUILD_STEPS)
    ]
    for copy in small + large:
        copy.start()
    dense_ref[...] = jnp.zeros_like(dense_ref)
    acc_ref[...] = jnp.zeros_like(acc_ref)

    def one(slot, carry):
        a, b = rows_ref[0, 0, slot], cols_ref[0, 0, slot]
        row = (part_place(lax.div(a, per), row_me, n_row) * per + lax.rem(a, per)) * size
        col = (arrival_place(lax.div(b, per), col_me, n_col) * per + lax.rem(b, per)) * size
        tile = tiles_ref[slot]
        dense_ref[pl.ds(pl.multiple_of(row, size), size), pl.ds(pl.multiple_of(col, size), size)] = tile
        wide = tile.astype(jnp.float32).reshape(size // 8, 8, size)
        acc_ref[b] += jnp.sum(wide, axis=0)
        return carry

    for copy in small:
        copy.wait()
    for step, copy in enumerate(large):
        copy.wait()
        lax.fori_loop(step * some, jnp.minimum(count_ref[0], (step + 1) * some), one, 0)
    degree_ref[...] = jnp.sum(acc_ref[...], axis=1)


def product_kernel(n_row, n_col, begin, n_blocks, first, *refs):
    place_ref, dense_ref, degree_ref = refs[:3]
    block_refs = refs[3 : 3 + n_blocks]
    sum_refs = () if first else refs[3 + n_blocks : 4 + n_blocks]
    panel_ref = refs[-1]
    sum_out_ref, scale_ref = refs[-3:-1]
    width, size = panel_ref.shape[1], degree_ref.shape[1]
    own_rows = dense_ref.shape[0] // n_row

    def scale(row):
        owner = arrival_owner(begin + row // own_rows, place_ref[1], n_col)
        index = owner * (own_rows // size) + row % own_rows // size
        line = lax.rsqrt(1.0 + degree_ref[pl.ds(index, 1), :])
        return jnp.broadcast_to(line, (size, size)).T

    for place, block in enumerate(block_refs):
        for top in range(0, own_rows, size):
            row = place * own_rows + top
            spread = scale(row)
            for left in range(0, width, LANES):
                cut = slice(left, left + LANES)
                value = block[top : top + size, cut].astype(jnp.float32) * spread
                panel_ref[row : row + size, cut] = value.astype(jnp.bfloat16)
    for top in range(0, own_rows, size):
        scale_ref[top : top + size, :] = scale((n_col - 1 - begin) * own_rows + top)
    for part in range(n_row):
        rows = slice(part * own_rows, (part + 1) * own_rows)
        value = jnp.dot(dense_ref[rows, :], panel_ref[...], preferred_element_type=jnp.float32)
        if not first:
            value = value + sum_refs[0][rows, :]
        sum_out_ref[rows, :] = value


def last_kernel(*refs):
    dense_ref, scale_ref, block_ref, sum_ref, *out_refs, panel_ref = refs
    width = panel_ref.shape[1]
    for left in range(0, width, LANES):
        cut = slice(left, left + LANES)
        panel_ref[:, cut] = (block_ref[:, cut].astype(jnp.float32) * scale_ref[...]).astype(jnp.bfloat16)
    end = 0
    for out_ref in out_refs:
        rows = slice(end, end + out_ref.shape[0])
        end = rows.stop
        value = jnp.dot(dense_ref[rows, :], panel_ref[...], preferred_element_type=jnp.float32)
        out_ref[...] = (value + sum_ref[rows, :]).astype(out_ref.dtype)


def sigmoid(x):
    return 0.5 * jnp.tanh(0.5 * x) + 0.5


def tail_kernel(n_before, *refs):
    refs = refs[n_before:]
    (conv_ref, conv_bias_ref, input_ref, input_bias_ref, memory_ref), gate_refs, sums = refs[:5], refs[5:8], refs[8:-1]
    out_ref = refs[-1]
    width = memory_ref.shape[1]
    owned = functools.reduce(lambda x, y: x + y, [term[...].astype(jnp.float32) for term in sums])
    spread = jnp.mean(owned * owned, axis=1, keepdims=True) + norm_epsilon
    normed = (owned * lax.rsqrt(spread)).astype(jnp.bfloat16)
    message = jnp.maximum(
        jnp.dot(normed, conv_ref[...], preferred_element_type=jnp.float32) + conv_bias_ref[...], 0.0
    ).astype(jnp.bfloat16)

    def gate(index):
        cut = slice(index * width, (index + 1) * width)
        dots = jnp.dot(message, input_ref[:, cut], preferred_element_type=jnp.float32)
        return dots + input_bias_ref[:, cut], gate_refs[index][...]

    mine, held = gate(0)
    reset = sigmoid(mine + held)
    mine, held = gate(2)
    candidate = jnp.tanh(mine + reset * held)
    mine, held = gate(1)
    update = sigmoid(mine + held)
    out_ref[...] = (1.0 - update) * candidate + update * memory_ref[...]


def on_device(
    features,
    memory,
    tile_values,
    tile_rows,
    tile_cols,
    tile_count,
    conv_weight,
    conv_bias,
    input_weight,
    input_bias,
    hidden_weight,
    hidden_bias,
):
    own_rows, width = features.shape
    n_row, n_col = lax.axis_size("row"), lax.axis_size("col")
    slots, size = tile_values.shape[2], tile_values.shape[3]
    dst_rows, src_rows = own_rows * n_row, own_rows * n_col
    col_blocks = src_rows // size
    place = jnp.stack([lax.axis_index("row"), lax.axis_index("col")]).astype(jnp.int32)

    cycle = [*range(0, n_col, 2), *range(n_col - 1, 0, -2)]
    ahead = [(cycle[at - 1], cycle[at]) for at in range(n_col)]
    behind = [(to, at) for at, to in ahead]

    def tie(*values):
        return lax.optimization_barrier(values)

    def move(block, to):
        return lax.ppermute(block, "col", to)

    blocks = [features, move(features, ahead), move(features, behind)]
    half = own_rows // 2
    dense, degree = pl.pallas_call(
        functools.partial(build_kernel, own_rows, n_row, n_col),
        out_shape=(
            jax.ShapeDtypeStruct((dst_rows, src_rows), jnp.bfloat16),
            jax.ShapeDtypeStruct((col_blocks, size), jnp.float32),
        ),
        in_specs=[smem()] * 2 + [pl.BlockSpec(memory_space=pltpu.HBM)] * 3,
        out_specs=(vmem(), vmem()),
        scratch_shapes=[
            pltpu.VMEM((col_blocks, 8, size), jnp.float32),
            pltpu.VMEM((slots, size, size), jnp.bfloat16),
            pltpu.SMEM(tile_rows.shape, jnp.int32),
            pltpu.SMEM(tile_cols.shape, jnp.int32),
            pltpu.SemaphoreType.DMA((2 + BUILD_STEPS,)),
        ],
        compiler_params=params(2 * slots * size * size + 2 * dst_rows * src_rows),
        cost_estimate=cost(0, 2 * slots * size * size + 2 * dst_rows * src_rows),
        name="build",
    )(place, tile_count.reshape(1), *[pltpu.with_memory_space_constraint(x, pltpu.HBM) for x in (tile_rows, tile_cols, tile_values)])

    gates = []

    def gate_product(block):
        nonlocal memory
        block, memory = tie(block, memory)
        cut = slice(len(gates) * width, (len(gates) + 1) * width)
        gates.append(
            jnp.dot(memory.astype(jnp.bfloat16), hidden_weight[:, cut], preferred_element_type=jnp.float32)
            + hidden_bias[cut]
        )
        return block

    added = move(degree, [(i, i ^ 2) for i in range(n_col)])
    blocks[2], degree = tie(blocks[2], degree)
    bit = 4
    while len(blocks) < n_col - 1:
        blocks.append(move(blocks[-2], ahead))
        if len(gates) < 2:
            blocks[-2] = gate_product(blocks[-2])
            gates[-1], added = tie(gates[-1], added)
        elif bit <= n_col:
            blocks[-2], added = tie(blocks[-2], added)
        blocks.append(move(blocks[-2], behind))
        if bit <= n_col:
            degree = degree + added
            added = move(degree, [(i, i ^ (bit if bit < n_col else 1)) for i in range(n_col)])
            bit *= 2
    across = move(blocks[-1], behind)
    blocks[-1] = gate_product(blocks[-1])
    gates[-1], added = tie(gates[-1], added)
    degree = degree + added

    def whole(*shape):
        return pl.BlockSpec(shape, lambda i: (0, 0))

    def product(begin, count, running):
        depth = count * own_rows
        return pl.pallas_call(
            functools.partial(product_kernel, n_row, n_col, begin, count, running is None),
            grid=(1,),
            out_shape=(
                jax.ShapeDtypeStruct((dst_rows, width), jnp.float32),
                jax.ShapeDtypeStruct((own_rows, size), jnp.float32),
            ),
            in_specs=[
                smem(),
                pl.BlockSpec((dst_rows, depth), lambda i: (0, begin // count)),
                whole(col_blocks, size),
            ]
            + [whole(own_rows, width)] * count
            + ([] if running is None else [whole(dst_rows, width)]),
            out_specs=(whole(dst_rows, width), whole(own_rows, size)),
            scratch_shapes=[pltpu.VMEM((depth, width), jnp.bfloat16)],
            compiler_params=params(2 * dst_rows * depth + 4 * depth * width + 8 * dst_rows * width + 2 * MIB),
            cost_estimate=cost(2 * dst_rows * depth * width, 2 * dst_rows * depth + 6 * dst_rows * width),
            name="product",
        )(place, dense, degree, *blocks[begin : begin + count], *([] if running is None else [running]))

    def last_product(at, height):
        rows = dst_rows // 2
        dtypes = [jnp.float32 if top // own_rows % 2 else jnp.bfloat16 for top in range(0, rows, height)]
        return pl.pallas_call(
            last_kernel,
            grid=(1,),
            out_shape=tuple(jax.ShapeDtypeStruct((height, width), dtype) for dtype in dtypes),
            in_specs=[
                pl.BlockSpec((rows, own_rows), lambda i: (at, n_col - 1)),
                whole(own_rows, size),
                whole(own_rows, width),
                pl.BlockSpec((rows, width), lambda i: (at, 0)),
            ],
            out_specs=(whole(height, width),) * len(dtypes),
            scratch_shapes=[pltpu.VMEM((own_rows, width), jnp.bfloat16)],
            compiler_params=params(2 * rows * own_rows + 6 * own_rows * width + 8 * rows * width + 2 * MIB),
            cost_estimate=cost(2 * rows * own_rows * width, 2 * rows * own_rows + 6 * rows * width),
            name="last_product",
        )(dense, scale, across, running)

    running, begin = None, 0
    while begin < n_col - 1:
        count = n_col - 1 if n_col <= 8 else (n_col - begin) // 2
        running, scale = product(begin, count, running)
        begin += count
    def total(terms):
        return functools.reduce(lambda x, y: x + y, [term.astype(jnp.float32) for term in terms]).astype(jnp.bfloat16)

    def send(value, bit):
        return lax.ppermute(value, "row", [(i, i ^ bit) for i in range(n_row)])

    def halve(sums, end):
        for part in sorted(sums, reverse=True):
            if part > end:
                sums[part & (part - 1)].append(send(total(sums[part]), part & -part))
        return sums[end]

    middle = n_row // 2
    upper, lower = last_product(0, half), last_product(1, own_rows)
    sums = [{n_row - 1 - at: [upper[2 * at + which]] for at in range(middle)} for which in range(2)]
    given = [total(halve(each, middle)) for each in sums]
    given[0], *lower = tie(given[0], *lower)
    arrived = [send(value, middle) for value in given]
    terms = halve({middle - 1 - at: [part] for at, part in enumerate(lower)}, 0)

    weights = (conv_weight, conv_bias.reshape(1, width), input_weight, input_bias.reshape(1, 3 * width))
    result = None
    for at in range(2):
        part = pl.BlockSpec((half, width), lambda i, at=at: (at, 0))
        operands = [(term, part) for term in terms] + [(arrived[at], whole(half, width))]
        before = [] if result is None else [result]
        result = pl.pallas_call(
            functools.partial(tail_kernel, len(before)),
            grid=(1,),
            out_shape=jax.ShapeDtypeStruct((own_rows, width), jnp.float32),
            in_specs=[pl.BlockSpec(memory_space=pl.ANY)] * len(before)
            + [whole(*weight.shape) for weight in weights]
            + [part] * 4
            + [spec for _, spec in operands],
            out_specs=part,
            input_output_aliases={0: 0} if before else {},
            compiler_params=params(8 * width * width + 40 * own_rows * width),
            cost_estimate=cost(4 * own_rows * width * width, 8 * width * width + 10 * own_rows * width),
            name="tail",
        )(*before, *weights, memory, *gates, *[term for term, _ in operands])
    return result


def solution(mesh):
    placed = (
        P(("row", "col"), None),
        P(("col", "row"), None),
        P("row", "col", None, None, None),
        P("row", "col", None),
        P("row", "col", None),
        P("row", "col"),
        P(),
        P(),
        P(),
        P(),
        P(),
        P(),
    )
    return jax.shard_map(
        on_device, mesh=mesh, in_specs=placed, out_specs=P(("col", "row"), None), check_vma=False
    )
```
